32 devices in a mesh: dp: 8 (over z, x), tensor: 4 (over y, core).
Axes of the slice: x: 2, y: 2, z: 4, core: 2. Of those that a mesh axis runs over, the one named last changes fastest.
Arguments:
- images: bfloat16 [40, 197, 768], P('dp'), may hold values from -6 to 6
- w_qkv: bfloat16 [3, 768, 768], P(None, None, 'tensor'), may hold values from -0.21875 to 0.21875
- w_proj: bfloat16 [768, 768], P('tensor'), may hold values from -0.625 to 0.625
- w_router: bfloat16 [768, 4], replicated, may hold values from -0.15625 to 0.15625
- w_in: bfloat16 [4, 768, 3072], P(None, None, 'tensor'), may hold values from -0.21875 to 0.21875
- w_out: bfloat16 [4, 3072, 768], P(None, 'tensor'), may hold values from -0.3125 to 0.3125
- gain_one: float32 [768], replicated, may hold values from 0.5 to 1.5
- gain_two: float32 [768], replicated, may hold values from 0.5 to 1.5
- routes: int32 [40, 197, 2], P('dp'), may hold values from 0 to 3, as said below
- order: int32 [8, 985], P('dp'), may hold values from 0 to 984, each once within a row
- counts: int32 [8], P('dp'), may hold values from 3 to 5, as said below
- cotangent: bfloat16 [40, 197, 768], P('dp'), may hold values from -6 to 6
Outputs:
- output: bfloat16 [40, 197, 768], P('dp')
- grad_images: float32 [40, 197, 768], P('dp')
- grad_qkv: float32 [3, 768, 768], P(None, None, 'tensor')
- grad_proj: float32 [768, 768], P('tensor')
- grad_router: float32 [768, 4], replicated
- grad_in: float32 [4, 768, 3072], P(None, None, 'tensor')
- grad_out: float32 [4, 3072, 768], P(None, 'tensor')
- grad_gain_one: float32 [768], replicated
- grad_gain_two: float32 [768], replicated
- kept: int32 [40, 197, 2], P('dp')
The draws below stay inside these ranges and needn't reach their ends.
Inputs may be any that keep to these rules, and one draw needn't show every extreme that they name: `routes`: each token names 2 different experts. `order`: each row holds every token position of its group once. `counts`: some group holds all 5 images.
All inputs are finite; a program needn't handle non-finite values.
Results may differ from the reference program's by a relative error of at most 0.024.
Values may be sent and summed in bfloat16 or wider, within the bound.
A program may use at most 192 MiB of HBM per device.

```python
import jax
import jax.numpy as jnp
from jax import lax

D = 768
H = 12
HD = 64
F = 3072
SPECIALIST_TOTAL = 4
TOPK = 2
SEQ = 197
IMG = 5
TOK = 985
CAP = 616
IMAGES = 40
N_DP = 8
N_TENSOR = 4


def draw_counts(key, part):
    key = jax.random.fold_in(key, 7)
    first, second = jax.random.split(key)
    drawn = jax.random.randint(first, (N_DP,), (IMG + 1) // 2, IMG + 1).astype(jnp.int32)
    fullest = jax.random.randint(second, (), 0, N_DP)
    return drawn.at[fullest].set(IMG)


def draw_routes(key, part):
    key = jax.random.fold_in(key, 11)
    first, second = jax.random.split(key)
    patch_sort_order = jax.random.permutation(first, SPECIALIST_TOTAL).astype(jnp.int32)
    precedence_offset = jnp.where(patch_sort_order == 0, 400, jnp.where(patch_sort_order == 1, 150, 0)).astype(jnp.int32)
    dispatcher_noise_level = jax.random.randint(second, (IMAGES, SEQ, SPECIALIST_TOTAL), 0, 1000).astype(jnp.int32)
    category_targets = jnp.arange(SPECIALIST_TOTAL, dtype=jnp.int32)
    precedence_measures = (dispatcher_noise_level + precedence_offset[None, None, :]) * SPECIALIST_TOTAL + category_targets[None, None, :]
    _, picked = lax.top_k(precedence_measures, TOPK)
    return picked.astype(jnp.int32)


def steps_of(own_key, shape, shards, smallest, high):
    level, own = 1.0, jax.random.fold_in(own_key, 6)
    for dim, blocks in shards:
        draws = jnp.exp(jax.random.uniform(jax.random.fold_in(own, dim), (blocks,), jnp.float32, smallest / len(shards), high / len(shards)))
        level = level * jnp.repeat(draws, shape[dim] // blocks).reshape([-1 if axis == dim else 1 for axis in range(len(shape))])
    return level


def scatter_about(key, dims, scale, most, cuts=(), kind=jnp.bfloat16):
    values = scale * jax.random.normal(key, dims, jnp.float32)
    if cuts:
        values = values * steps_of(key, dims, cuts, -0.22, 0.18)
    return jnp.clip(values, -most, most).astype(kind)


def setup_inputs(seed: int = 0) -> dict:
    streams_of = jax.random.split(jax.random.key(seed), 13)
    return {
        "images": scatter_about(streams_of[0], (IMAGES, SEQ, D), 1.0, 6.0, ((0, 8),)),
        "w_qkv": scatter_about(streams_of[1], (3, D, D), D ** -0.5, 0.21875, ((2, 4),)),
        "w_proj": scatter_about(streams_of[2], (D, D), (D // 8) ** -0.5, 0.625, ((0, 4),)),
        "w_router": scatter_about(streams_of[3], (D, SPECIALIST_TOTAL), (2 * D) ** -0.5, 0.15625),
        "w_in": scatter_about(streams_of[4], (SPECIALIST_TOTAL, D, F), D ** -0.5, 0.21875, ((2, 4),)),
        "w_out": scatter_about(streams_of[5], (SPECIALIST_TOTAL, F, D), (F // 8) ** -0.5, 0.3125, ((1, 4),)),
        "gain_one": jnp.clip(1.0 + 0.1 * jax.random.normal(streams_of[6], (D,), jnp.float32), 0.5, 1.5),
        "gain_two": jnp.clip(1.0 + 0.1 * jax.random.normal(streams_of[7], (D,), jnp.float32), 0.5, 1.5),
        "routes": draw_routes(jax.random.fold_in(streams_of[12], 71), 0),
        "order": jax.vmap(lambda own: jax.random.permutation(own, TOK))(jax.random.split(streams_of[9], N_DP)).reshape((N_DP, TOK)).astype(jnp.int32),
        "counts": draw_counts(jax.random.fold_in(streams_of[12], 71), 0),
        "cotangent": scatter_about(streams_of[11], (IMAGES, SEQ, D), 1.0, 6.0, ((0, 8),)),
    }


@jax.custom_vjp
def low(v):
    return lax.optimization_barrier(v.astype(jnp.bfloat16)).astype(jnp.float32)

@jax.custom_vjp
def low_back(v):
    return v

def low_keep(v):
    return (low(v), None)

def low_pass(kept, grad):
    return (grad,)

def back_keep(v):
    return (v, None)

def back_low(kept, grad):
    return (low(grad),)
low.defvjp(low_keep, low_pass)
low_back.defvjp(back_keep, back_low)
EPSILON = 1e-06
SCALE = 0.125
HIGHEST = lax.Precision.HIGHEST

def layer_norm(rows, gain):
    center = lax.optimization_barrier(jnp.mean(rows, axis=-1, keepdims=True))
    centred = rows - center
    spread = lax.optimization_barrier(jnp.mean(centred * centred, axis=-1, keepdims=True))
    return centred * lax.rsqrt(spread + EPSILON) * gain

def route_slots(routes_g, order_g, count_g):
    tokens = routes_g.shape[0]
    positions = jnp.arange(tokens, dtype=jnp.int32)
    in_image = (positions // SEQ < count_g).astype(jnp.int32)
    capacity_now = (5 * TOPK * count_g * SEQ + 4 * SPECIALIST_TOTAL - 1) // (4 * SPECIALIST_TOTAL)
    ranked = routes_g[order_g]
    alive_rows = in_image[order_g]
    pair_expert = ranked.T.reshape(-1)
    pair_alive = jnp.tile(alive_rows, TOPK)
    matches = (pair_expert[:, None] == jnp.arange(SPECIALIST_TOTAL, dtype=jnp.int32)[None, :]).astype(jnp.int32) * pair_alive[:, None]
    before = jnp.cumsum(matches, axis=0) - matches
    pair_slot = lax.optimization_barrier(jnp.sum(before * matches, axis=1))
    pair_kept = pair_alive * (pair_slot < capacity_now).astype(jnp.int32)
    inverse = jnp.zeros((tokens,), jnp.int32).at[order_g].set(positions)
    slot_of = pair_slot.reshape(TOPK, tokens)[:, inverse].T
    kept_pairs = pair_kept.reshape(TOPK, tokens)[:, inverse].T
    return (slot_of, kept_pairs)

def block_forward(rows, params, routes_g, slot_of, kept_pairs):
    w_qkv, w_proj, w_router, w_in, w_out, gain_one, gain_two = params
    parts = N_TENSOR
    local = D // parts
    heads = H // parts
    tokens = rows.shape[0]
    normed = low(layer_norm(rows, gain_one))
    spread = low_back(jnp.broadcast_to(normed[None], (parts, tokens, D)))
    projected = jnp.einsum('jtd,sdjc->sjtc', spread, w_qkv.reshape(3, D, parts, local), precision=HIGHEST)
    projected = low(low_back(projected)).reshape(3, parts, IMG, SEQ, heads, HD)
    queries, keys, values = (projected[0], projected[1], projected[2])
    precedence_measures = low_back(jnp.einsum('jinhc,jimhc->jihnm', queries, keys, precision=HIGHEST) * SCALE)
    probs = low(jax.nn.softmax(precedence_measures, axis=-1))
    mixed = low(low_back(jnp.einsum('jihnm,jimhc->jinhc', probs, values, precision=HIGHEST)))
    mixed = mixed.reshape(parts, tokens, local)
    partial_attn = jnp.einsum('jtc,jcd->jtd', mixed, w_proj.reshape(parts, local, D), precision=HIGHEST)
    hidden_one = rows + lax.optimization_barrier(jnp.sum(low(low_back(partial_attn)), axis=0))
    normed_two = low(layer_norm(hidden_one, gain_two))
    logits = jnp.dot(normed_two, w_router, precision=HIGHEST)
    gates_all = jax.nn.softmax(logits, axis=-1)
    chosen = jnp.take_along_axis(gates_all, routes_g, axis=1)
    flat_slot = routes_g * CAP + slot_of
    target = jnp.where(kept_pairs > 0, flat_slot, SPECIALIST_TOTAL * CAP).reshape(-1)
    token_ids = jnp.broadcast_to(jnp.arange(tokens, dtype=jnp.int32)[:, None], (tokens, TOPK)).reshape(-1)
    source = jnp.zeros((SPECIALIST_TOTAL * CAP + 1,), jnp.int32).at[target].set(token_ids)[:SPECIALIST_TOTAL * CAP]
    filled = jnp.zeros((SPECIALIST_TOTAL * CAP + 1,), jnp.float32).at[target].set(1.0)[:SPECIALIST_TOTAL * CAP]
    spread_two = low_back(jnp.broadcast_to(normed_two[None], (parts, tokens, D)))
    slots_in = low_back(spread_two[:, source, :] * filled[None, :, None]).reshape(parts, SPECIALIST_TOTAL, CAP, D)
    inner = jnp.einsum('jecd,edjf->jecf', slots_in, w_in.reshape(SPECIALIST_TOTAL, D, parts, F // parts), precision=HIGHEST)
    active = low(jax.nn.gelu(low_back(inner)))
    expert_rows = jnp.einsum('jecf,ejfd->jecd', active, w_out.reshape(SPECIALIST_TOTAL, parts, F // parts, D), precision=HIGHEST)
    expert_rows = low(low_back(expert_rows)).reshape(parts, SPECIALIST_TOTAL * CAP, D)
    gate_spread = low_back(jnp.broadcast_to(chosen[None], (parts, tokens, TOPK)))
    picked = expert_rows[:, jnp.minimum(flat_slot, SPECIALIST_TOTAL * CAP - 1), :]
    weighted = picked * (gate_spread * kept_pairs.astype(jnp.float32)[None])[..., None]
    partial_moe = lax.optimization_barrier(jnp.sum(weighted, axis=2))
    return hidden_one + lax.optimization_barrier(jnp.sum(low(low_back(partial_moe)), axis=0))

def reference(images, w_qkv, w_proj, w_router, w_in, w_out, gain_one, gain_two, routes, order, counts, cotangent):
    groups = counts.shape[0]
    tokens = IMG * SEQ
    weights = tuple((w.astype(jnp.float32) for w in (w_qkv, w_proj, w_router, w_in, w_out, gain_one, gain_two)))

    def group_step(totals, inputs):
        rows, back, routes_g, order_g, count_g = inputs
        slot_of, kept_pairs = route_slots(routes_g, order_g, count_g)

        def forward(rows_f, params):
            return block_forward(rows_f, params, routes_g, slot_of, kept_pairs)
        result, pullback = jax.vjp(forward, rows.astype(jnp.float32), weights)
        grad_rows, grad_params = pullback(back.astype(jnp.float32))
        totals = jax.tree.map(jnp.add, totals, grad_params)
        return (totals, (result.astype(jnp.bfloat16), grad_rows, kept_pairs))
    zeros = tuple((jnp.zeros(w.shape, jnp.float32) for w in weights))
    inputs = (images.reshape(groups, tokens, D), cotangent.reshape(groups, tokens, D), routes.reshape(groups, tokens, TOPK), order, counts)
    totals, (result, grad_rows, kept_all) = lax.scan(group_step, zeros, inputs)
    shape = images.shape
    return (result.reshape(shape), grad_rows.reshape(shape), totals[0], totals[1], totals[2], totals[3], totals[4], totals[5], totals[6], kept_all.reshape(shape[0], shape[1], TOPK))
```

```python
import functools

import jax
import jax.numpy as jnp
from jax import lax
from jax.experimental import pallas as pl
from jax.experimental.pallas import tpu as pltpu
from jax.sharding import PartitionSpec as P

HD = 64
SPECIALIST_TOTAL = 4
TOPK = 2
SEQ = 197
CAP = 616
PAIRED = SPECIALIST_TOTAL // 2
DENSE_HALF = 400


EPSILON = 1e-06
SCALE = 0.125
HIGHEST = lax.Precision.HIGHEST
BF = jnp.bfloat16
F32 = jnp.float32
MESH = pl.DeviceIdType.MESH


def layer_norm(rows, gain):
    center = jnp.mean(rows, axis=-1, keepdims=True)
    centred = rows - center
    spread = jnp.mean(centred * centred, axis=-1, keepdims=True)
    return centred * lax.rsqrt(spread + EPSILON) * gain


def route_slots(routes_g, order_g, count_g):
    tokens = routes_g.shape[0]
    positions = jnp.arange(tokens, dtype=jnp.int32)
    in_image = (positions // SEQ < count_g).astype(jnp.int32)
    capacity_now = (5 * TOPK * count_g * SEQ + 4 * SPECIALIST_TOTAL - 1) // (4 * SPECIALIST_TOTAL)
    spots = order_g[:, None] == positions[None, :]
    place = jnp.sum(jnp.where(spots, positions[:, None], 0), axis=0)
    earlier = (place[None, :] < place[:, None]).astype(BF)
    experts = jnp.arange(SPECIALIST_TOTAL, dtype=jnp.int32)
    marks = (routes_g[:, :, None] == experts).astype(jnp.int32) * in_image[:, None, None]
    marks = marks.reshape(tokens, TOPK * SPECIALIST_TOTAL)
    before = jnp.dot(earlier, marks.astype(BF), preferred_element_type=F32)
    before = before.reshape(tokens, TOPK, SPECIALIST_TOTAL).astype(jnp.int32)
    marks = marks.reshape(tokens, TOPK, SPECIALIST_TOTAL)
    first_total = jnp.sum(marks[:, 0, :], axis=0)
    before = before + jnp.stack([jnp.zeros_like(first_total), first_total])[None]
    slot_of = jnp.sum(before * marks, axis=-1)
    kept_pairs = in_image[:, None] * (slot_of < capacity_now).astype(jnp.int32)
    return (slot_of, kept_pairs)


def pair_sum(partial):
    n_t = lax.axis_size("tensor")
    core = lax.axis_index("tensor") % 2
    half = partial.shape[-1] // 2
    other = [(i, i ^ 1) for i in range(n_t)]
    mine = lax.dynamic_slice_in_dim(partial, core * half, half, partial.ndim - 1)
    gone = lax.dynamic_slice_in_dim(partial, (1 - core) * half, half, partial.ndim - 1)
    got = lax.ppermute(gone, "tensor", other)
    total = (mine.astype(F32) + got.astype(F32)).astype(BF)
    step = 2
    while step < n_t:
        got = lax.ppermute(total, "tensor", [(i, i ^ step) for i in range(n_t)])
        total = (total.astype(F32) + got.astype(F32)).astype(BF)
        step *= 2
    back = lax.ppermute(total, "tensor", other)
    return jnp.where(
        core == 0,
        jnp.concatenate([total, back], axis=-1),
        jnp.concatenate([back, total], axis=-1),
    )


def add_rows(out, left, right, start, rows, tile):
    def step(i, carry):
        at = pl.ds(pl.multiple_of(start + i * tile, 16), tile)
        out[at, :] = (left[at, :].astype(F32) + right[at, :].astype(F32)).astype(BF)
        return carry

    lax.fori_loop(0, rows // tile, step, 0)


def tree_kernel(
    parts, main_ref, dense_ref, out_ref,
    got_x, got_low, got_mid, part_sum, total,
    send_x, recv_x, send_low, recv_low, send_mid, recv_mid, send_down, recv_down, send_pair, recv_pair, keep,
):
    place = lax.axis_index("dp")
    x = lax.rem(place, 2)
    z = place // 2
    inner = jnp.logical_or(z == 1, z == 2)
    outer = jnp.logical_not(inner)
    pair = place + 1 - 2 * x
    line = (z + 1 - 2 * lax.rem(z, 2)) * 2 + x
    middle = (3 - z) * 2 + x
    main_rows = main_ref.shape[0]
    dense_rows = dense_ref.shape[1]
    rows = main_rows // parts
    spans = [(i * rows, rows, 48) for i in range(parts)] + [(main_rows, dense_rows, 80)]

    barrier = pltpu.get_barrier_semaphore()
    for peer in (pair, line):
        pl.semaphore_signal(barrier, inc=1, device_id={"dp": peer}, device_id_type=MESH)

    @pl.when(inner)
    def _():
        pl.semaphore_signal(barrier, inc=1, device_id={"dp": middle}, device_id_type=MESH)
        pl.semaphore_wait(barrier, 3)

    @pl.when(outer)
    def _():
        pl.semaphore_wait(barrier, 2)

    def send(src, dst, sems, recvs, i, peer):
        return pltpu.make_async_remote_copy(
            src_ref=src, dst_ref=dst, send_sem=sems.at[i], recv_sem=recvs.at[i],
            device_id={"dp": peer}, device_id_type=MESH,
        )

    def at(ref, i):
        start, count, _ = spans[i]
        return ref.at[pl.ds(start, count), :]

    def x_copy():
        return send(dense_ref.at[1 - x], got_x, send_x, recv_x, 0, pair)

    def low_copy(i):
        source = at(main_ref, i) if i < parts else at(part_sum, i)
        return send(source, at(got_low, i), send_low, recv_low, i, line)

    def mid_copy(i):
        return send(at(part_sum, i), at(got_mid, i), send_mid, recv_mid, i, middle)

    def down_copy(i):
        return send(at(total, i), at(total, i), send_down, recv_down, i, line)

    def pair_copy(i):
        start, count, _ = spans[i]
        return send(
            at(total, i), out_ref.at[x, pl.ds(start, count), :], send_pair, recv_pair, i, pair
        )

    def keep_copy(i):
        start, count, _ = spans[i]
        return pltpu.make_async_copy(
            at(total, i), out_ref.at[x, pl.ds(start, count), :], keep.at[i]
        )

    x_copy().start()

    @pl.when(outer)
    def _():
        for i in range(parts):
            low_copy(i).start()

    x_copy().wait()

    def join(i, carry):
        here = pl.ds(pl.multiple_of(i * 80, 16), 80)
        there = pl.ds(pl.multiple_of(main_rows + i * 80, 16), 80)
        part_sum[there, :] = (
            dense_ref[x, here, :].astype(F32) + got_x[here, :].astype(F32)
        ).astype(BF)
        return carry

    lax.fori_loop(0, dense_rows // 80, join, 0)
    order = [0, 1, 2, parts] + list(range(3, parts))

    @pl.when(outer)
    def _():
        low_copy(parts).start()
        for i in order:
            down_copy(i).wait_recv()
            pair_copy(i).start()
            keep_copy(i).start()

    @pl.when(inner)
    def _():
        def finish(i):
            mid_copy(i).wait_recv()
            start, count, tile = spans[i]
            add_rows(total, part_sum, got_mid, start, count, tile)
            down_copy(i).start()
            pair_copy(i).start()
            keep_copy(i).start()

        for n, i in enumerate(order):
            low_copy(i).wait_recv()
            start, count, tile = spans[i]
            if i == parts:
                add_rows(part_sum, part_sum, got_low, start, count, tile)
            else:
                add_rows(part_sum, main_ref, got_low, start, count, tile)
            mid_copy(i).start()
            if n:
                finish(order[n - 1])
        finish(order[-1])

    @pl.when(outer)
    def _():
        for i in order:
            low_copy(i).wait_send()

    @pl.when(inner)
    def _():
        for i in order:
            mid_copy(i).wait_send()
            down_copy(i).wait_send()

    for i in order:
        keep_copy(i).wait()
        pair_copy(i).wait()


def tree_sum(main, dense, parts):
    rows = main.shape[0] + dense.shape[1]
    width = main.shape[1]
    vmem = pl.BlockSpec(memory_space=pltpu.VMEM)
    sems = [pltpu.SemaphoreType.DMA((parts + 1,))] * 9
    return pl.pallas_call(
        functools.partial(tree_kernel, parts),
        out_shape=jax.ShapeDtypeStruct((2, rows, width), BF),
        in_specs=[vmem, vmem],
        out_specs=pl.BlockSpec(memory_space=pl.ANY),
        scratch_shapes=[pltpu.VMEM((dense.shape[1], width), BF)]
        + [pltpu.VMEM((rows, width), BF)] * 4
        + [pltpu.SemaphoreType.DMA((1,))] * 2
        + sems,
        compiler_params=pltpu.CompilerParams(
            collective_id=0, has_side_effects=True, vmem_limit_bytes=58 * 2**20
        ),
        cost_estimate=pl.CostEstimate(flops=10**8, bytes_accessed=10**8, transcendentals=0),
    )(main, dense)


def swap_sum(main, dense):
    n_dp = lax.axis_size("dp")
    x = lax.axis_index("dp") % 2

    def swap(value, step):
        return lax.ppermute(value, "dp", [(i, i ^ step) for i in range(n_dp)])

    gone = lax.dynamic_index_in_dim(dense, 1 - x, 0, keepdims=False)
    mine = lax.dynamic_index_in_dim(dense, x, 0, keepdims=False)
    joined = (mine.astype(F32) + swap(gone, 1).astype(F32)).astype(BF)
    total = jnp.concatenate([main, joined], axis=0)
    step = 2
    while step < n_dp:
        total = (total.astype(F32) + swap(total, step).astype(F32)).astype(BF)
        step *= 2
    other = swap(total, 1)
    return jnp.where(x == 0, jnp.stack([total, other]), jnp.stack([other, total]))


def select_rows(target, first, count):
    columns = first + jnp.arange(count, dtype=jnp.int32)
    return (target[:, 0] == columns[:, None]) | (target[:, 1] == columns[:, None])


def slot_gates(target, gates, first, count):
    columns = first + jnp.arange(count, dtype=jnp.int32)
    return jnp.sum(
        jnp.where(target[:, 0] == columns[:, None], gates[:, 0], 0.0)
        + jnp.where(target[:, 1] == columns[:, None], gates[:, 1], 0.0),
        axis=1,
    )


def dots(spec, left, right):
    return jnp.einsum(spec, left, right, preferred_element_type=F32)


def per_device(
    images,
    w_qkv,
    w_proj,
    w_router,
    w_in,
    w_out,
    gain_one,
    gain_two,
    routes,
    order,
    counts,
    cotangent,
):
    img_count, seq_len, width = images.shape
    tokens = img_count * seq_len
    local = w_proj.shape[0]
    heads = local // HD
    slots = SPECIALIST_TOTAL * CAP
    half_slots = PAIRED * CAP
    n_dp = lax.axis_size("dp")
    x = lax.axis_index("dp") % 2
    swap = [(i, i ^ 1) for i in range(n_dp)]
    rows = images.reshape(tokens, width).astype(F32)
    routes_g = routes.reshape(tokens, TOPK)
    slot_of, kept_pairs = route_slots(routes_g, order[0], counts[0])
    target = jnp.where(kept_pairs > 0, routes_g * CAP + slot_of, -1)
    target_pair = lax.ppermute(target, "dp", swap)
    back_low = cotangent.reshape(tokens, width)
    back_pair = lax.ppermute(back_low, "dp", swap)
    normed = layer_norm(rows, gain_one).astype(BF)
    projected = dots("td,sdc->stc", normed, w_qkv).astype(BF)
    shaped = projected.reshape(3, img_count, seq_len, heads, HD)
    queries, keys, values = (shaped[0], shaped[1], shaped[2])
    scores = dots("inhc,imhc->ihnm", queries, keys) * SCALE
    peak = jnp.max(scores, axis=-1, keepdims=True)
    log_total = peak + jnp.log(jnp.sum(jnp.exp(scores - peak), axis=-1, keepdims=True))
    probs = jnp.exp(scores - log_total).astype(BF)
    mixed = dots("ihnm,imhc->inhc", probs, values)
    mixed = mixed.astype(BF).reshape(tokens, local)
    partial_attn = jnp.dot(mixed, w_proj, preferred_element_type=F32)
    hidden_one = rows + pair_sum(partial_attn.astype(BF)).astype(F32)
    normed_two = layer_norm(hidden_one, gain_two).astype(BF)
    normed_pair = lax.ppermute(normed_two, "dp", swap)
    logits = jnp.dot(normed_two, w_router, preferred_element_type=F32)
    gates_all = jax.nn.softmax(logits, axis=-1)
    choose = (routes_g[:, :, None] == jnp.arange(SPECIALIST_TOTAL, dtype=jnp.int32)).astype(F32)
    chosen = jnp.sum(choose * gates_all[:, None, :], axis=-1)
    chosen_pair = lax.ppermute(chosen, "dp", swap)

    select = select_rows(target, 0, slots).astype(BF)
    gates = slot_gates(target, chosen, 0, slots)[:, None]
    shape = (SPECIALIST_TOTAL, CAP, width)
    slots_in = dots("st,td->sd", select, normed_two).astype(BF).reshape(shape)
    back_rows = dots("st,td->sd", select, back_low)
    grad_rows_out = (gates * back_rows).astype(BF).reshape(shape)
    inner = dots("ecd,edf->ecf", slots_in, w_in)
    active, gelu_back = jax.vjp(jax.nn.gelu, inner)
    active = active.astype(BF)
    grad_active = dots("ecd,efd->ecf", grad_rows_out, w_out)
    grad_inner = gelu_back(grad_active)[0].astype(BF)
    expert_rows = dots("ecf,efd->ecd", active, w_out).astype(BF).reshape(slots, width)
    grad_slots = dots("ecf,edf->ecd", grad_inner, w_in).astype(BF).reshape(slots, width)
    gate_rows = jnp.sum(expert_rows.astype(F32) * back_rows, axis=-1).astype(BF)
    weighted = (gates * expert_rows.astype(F32)).astype(BF)
    partial_moe = dots("st,sd->td", select, weighted).astype(BF)
    part_normed = dots("st,sd->td", select, grad_slots).astype(BF)
    owner = jnp.arange(slots, dtype=jnp.int32) // CAP
    spread = jnp.where(owner[:, None] == jnp.arange(128, dtype=jnp.int32), gate_rows[:, None], 0)
    part_gates = dots("st,se->te", select, spread.astype(BF)).astype(BF)
    output = hidden_one + pair_sum(partial_moe).astype(F32)
    summed = pair_sum(jnp.concatenate([part_normed, part_gates, part_gates], axis=-1))
    summed = summed.astype(F32)
    sum_normed = summed[:, :width]
    grad_gates = summed[:, width : width + SPECIALIST_TOTAL]

    select_pair = select_rows(target_pair, x * half_slots, half_slots).astype(BF)
    gates_pair = slot_gates(target_pair, chosen_pair, x * half_slots, half_slots)[:, None]
    half_shape = (PAIRED, CAP, width)
    own_in = lax.dynamic_slice_in_dim(w_in, x * PAIRED, PAIRED, 0)
    own_out = lax.dynamic_slice_in_dim(w_out, x * PAIRED, PAIRED, 0)
    pair_in = dots("st,td->sd", select_pair, normed_pair).astype(BF).reshape(half_shape)
    pair_back = dots("st,td->sd", select_pair, back_pair)
    pair_back = (gates_pair * pair_back).astype(BF).reshape(half_shape)
    pair_inner = dots("ecd,edf->ecf", pair_in, own_in)
    pair_active, pair_gelu_back = jax.vjp(jax.nn.gelu, pair_inner)
    pair_active = pair_active.astype(BF)
    pair_grad = pair_gelu_back(dots("ecd,efd->ecf", pair_back, own_out))[0].astype(BF)

    def both(own, other):
        own = lax.dynamic_slice_in_dim(own, x * PAIRED, PAIRED, 0)
        return jnp.concatenate([own, other], axis=1)

    grad_in = dots("ecd,ecf->edf", both(slots_in, pair_in), both(grad_inner, pair_grad))
    grad_out = dots("ecf,ecd->efd", both(active, pair_active), both(grad_rows_out, pair_back))
    main = jnp.stack([grad_in, grad_out], axis=1).astype(BF).reshape(-1, width)

    back = back_low.astype(F32)
    grad_logits = gates_all * (grad_gates - jnp.sum(gates_all * grad_gates, axis=-1, keepdims=True))
    grad_router = jnp.dot(normed_two.astype(F32).T, grad_logits, precision=HIGHEST)
    deriv_standardized_second = sum_normed + jnp.dot(
        grad_logits, w_router.astype(F32).T, precision=HIGHEST
    )
    _, norm_back_two = jax.vjp(layer_norm, hidden_one, gain_two)
    grad_hidden_part, grad_gain_two = norm_back_two(deriv_standardized_second)
    grad_hidden = back + grad_hidden_part
    grad_attn = grad_hidden.astype(BF)
    grad_proj = dots("tc,td->cd", mixed, grad_attn)
    grad_mixed = dots("td,cd->tc", grad_attn, w_proj)
    grad_mixed = grad_mixed.astype(BF).reshape(img_count, seq_len, heads, HD)
    again = dots("inhc,imhc->ihnm", queries, keys) * SCALE
    probs_again = jnp.exp(again - log_total)
    grad_values = dots("ihnm,inhc->imhc", probs_again.astype(BF), grad_mixed)
    grad_probs = dots("inhc,imhc->ihnm", grad_mixed, values)
    centre_term = jnp.sum(probs_again * grad_probs, axis=-1, keepdims=True)
    grad_scores = (probs_again * (grad_probs - centre_term)).astype(BF)
    query_gradient = dots("ihnm,imhc->inhc", grad_scores, keys) * SCALE
    grad_keys = dots("ihnm,inhc->imhc", grad_scores, queries) * SCALE
    grad_projected = (
        jnp.stack([query_gradient, grad_keys, grad_values]).astype(BF).reshape(3, tokens, local)
    )
    grad_qkv = dots("td,stc->sdc", normed, grad_projected)
    part_normed_one = dots("stc,sdc->td", grad_projected, w_qkv)
    sum_normed_one = pair_sum(part_normed_one.astype(BF)).astype(F32)
    _, norm_back_one = jax.vjp(layer_norm, rows, gain_one)
    partial_row_gradient, grad_gain_one = norm_back_one(sum_normed_one)
    grad_input = grad_hidden + partial_row_gradient

    pieces = [grad_qkv.reshape(-1), grad_proj.reshape(-1), grad_router.T.reshape(-1)]
    pieces += [grad_gain_one, grad_gain_two]
    flat = jnp.concatenate(pieces).astype(BF)
    flat = jnp.pad(flat, (0, 2 * DENSE_HALF * width - flat.shape[0]))
    dense = flat.reshape(2, DENSE_HALF, width)
    if n_dp == 8:
        whole = tree_sum(main, dense, 16)
    else:
        whole = swap_sum(main, dense)
    main_rows = main.shape[0]
    experts = whole[:, :main_rows].astype(F32)
    experts = experts.reshape(SPECIALIST_TOTAL, 2, width, width)
    flat = whole[:, main_rows:].astype(F32).reshape(-1)
    ends = [0]
    for piece in pieces:
        ends.append(ends[-1] + piece.shape[0])
    sums = [flat[a:b] for a, b in zip(ends[:-1], ends[1:])]
    return (
        output.astype(BF).reshape(images.shape),
        grad_input.reshape(images.shape),
        sums[0].reshape(grad_qkv.shape),
        sums[1].reshape(grad_proj.shape),
        sums[2].reshape(SPECIALIST_TOTAL, width).T,
        experts[:, 0],
        experts[:, 1],
        sums[3],
        sums[4],
        kept_pairs.reshape(img_count, seq_len, TOPK),
    )


def solution(mesh):
    return jax.shard_map(
        per_device,
        mesh=mesh,
        in_specs=(
            P("dp", None, None),
            P(None, None, "tensor"),
            P("tensor", None),
            P(),
            P(None, None, "tensor"),
            P(None, "tensor", None),
            P(),
            P(),
            P("dp", None, None),
            P("dp", None),
            P("dp"),
            P("dp", None, None),
        ),
        out_specs=(
            P("dp", None, None),
            P("dp", None, None),
            P(None, None, "tensor"),
            P("tensor", None),
            P(),
            P(None, None, "tensor"),
            P(None, "tensor", None),
            P(),
            P(),
            P("dp", None, None),
        ),
        check_vma=False,
    )
```

```python
import functools

import jax
import jax.numpy as jnp
from jax import lax
from jax.experimental import pallas as pl
from jax.experimental.pallas import tpu as pltpu
from jax.sharding import PartitionSpec as P

HD = 64
SPECIALIST_TOTAL = 4
TOPK = 2
SEQ = 197
SEQ_PAD = 208
CAP = 616
CAP_PAD = 640
TILE = 320
PAIRED = SPECIALIST_TOTAL // 2
LANES = 128
DENSE_HALF = 400


EPSILON = 1e-06
SCALE = 0.125
BF = jnp.bfloat16
F32 = jnp.float32
MESH = pl.DeviceIdType.MESH
VMEM_LIMIT = 60 * 2**20


def dot(left, right, left_dim=1, right_dim=0):
    return lax.dot_general(
        left, right, (((left_dim,), (right_dim,)), ((), ())), preferred_element_type=F32
    )


def lane_ids(shape):
    return lax.broadcasted_iota(jnp.int32, shape, len(shape) - 1)


def standardize(rows):
    center = jnp.mean(rows, axis=-1, keepdims=True)
    centred = rows - center
    spread = jnp.mean(centred * centred, axis=-1, keepdims=True)
    root = lax.rsqrt(spread + EPSILON)
    return centred * root, root


def norm_back(grad, plain, root, gain):
    grad = grad * gain
    first = jnp.mean(grad, axis=-1, keepdims=True)
    second = jnp.mean(grad * plain, axis=-1, keepdims=True)
    return root * (grad - first - plain * second)


def route_slots(routes_g, order_g, count_g):
    tokens = routes_g.shape[0]
    positions = jnp.arange(tokens, dtype=jnp.int32)
    in_image = (positions // SEQ < count_g).astype(jnp.int32)
    capacity_now = (5 * TOPK * count_g * SEQ + 4 * SPECIALIST_TOTAL - 1) // (4 * SPECIALIST_TOTAL)
    spots = order_g[:, None] == positions[None, :]
    place = jnp.sum(jnp.where(spots, positions[:, None], 0), axis=0)
    earlier = (place[None, :] < place[:, None]).astype(BF)
    experts = jnp.arange(SPECIALIST_TOTAL, dtype=jnp.int32)
    marks = (routes_g[:, :, None] == experts).astype(jnp.int32) * in_image[:, None, None]
    marks = marks.reshape(tokens, TOPK * SPECIALIST_TOTAL)
    before = jnp.dot(earlier, marks.astype(BF), preferred_element_type=F32)
    before = before.reshape(tokens, TOPK, SPECIALIST_TOTAL).astype(jnp.int32)
    marks = marks.reshape(tokens, TOPK, SPECIALIST_TOTAL)
    first_total = jnp.sum(marks[:, 0, :], axis=0)
    before = before + jnp.stack([jnp.zeros_like(first_total), first_total])[None]
    slot_of = jnp.sum(before * marks, axis=-1)
    kept_pairs = in_image[:, None] * (slot_of < capacity_now).astype(jnp.int32)
    held = jnp.max(jnp.where((marks * kept_pairs[:, :, None]) > 0, before, -1), axis=1)
    return (held, kept_pairs)


def pair_sum(partial):
    n_t = lax.axis_size("tensor")
    core = lax.axis_index("tensor") % 2
    half = partial.shape[-1] // 2
    other = [(i, i ^ 1) for i in range(n_t)]
    mine = lax.dynamic_slice_in_dim(partial, core * half, half, partial.ndim - 1)
    gone = lax.dynamic_slice_in_dim(partial, (1 - core) * half, half, partial.ndim - 1)
    got = lax.ppermute(gone, "tensor", other)
    total = (mine.astype(F32) + got.astype(F32)).astype(BF)
    step = 2
    while step < n_t:
        got = lax.ppermute(total, "tensor", [(i, i ^ step) for i in range(n_t)])
        total = (total.astype(F32) + got.astype(F32)).astype(BF)
        step *= 2
    back = lax.ppermute(total, "tensor", other)
    return jnp.where(
        core == 0,
        jnp.concatenate([total, back], axis=-1),
        jnp.concatenate([back, total], axis=-1),
    )


def head_mask(shape, head):
    return lane_ids(shape) // HD == head


def attend(query, key, head):
    alone = jnp.where(head_mask(query.shape, head), query, jnp.zeros_like(query))
    scores = dot(alone, key, 1, 1) * SCALE
    scores = jnp.where(lane_ids(scores.shape) < SEQ, scores, -jnp.inf)
    powers = jnp.exp(scores - jnp.max(scores, axis=-1, keepdims=True))
    return powers / jnp.sum(powers, axis=-1, keepdims=True)


def attention_kernel(images, w_qkv, w_proj, gain, partial, qkv, mixed):
    def image(i, carry):
        plain, _ = standardize(images[i].astype(F32))
        normed = (plain * gain[...]).astype(BF)
        for s in range(3):
            qkv[s, i] = dot(normed, w_qkv[s]).astype(BF)
        query, key, value = (qkv[s, i] for s in range(3))
        result = jnp.zeros(query.shape, F32)
        for head in range(query.shape[1] // HD):
            weights = attend(query, key, head).astype(BF)
            result = jnp.where(head_mask(query.shape, head), dot(weights, value), result)
        result = result.astype(BF)
        mixed[i] = result
        partial[i] = dot(result, w_proj[...]).astype(BF)
        return carry

    lax.fori_loop(0, images.shape[0], image, 0)


def softmax_of(logits, axis):
    ids = lax.broadcasted_iota(jnp.int32, logits.shape, axis)
    logits = jnp.where(ids < SPECIALIST_TOTAL, logits, -jnp.inf)
    powers = jnp.exp(logits - jnp.max(logits, axis=axis, keepdims=True))
    return powers / jnp.sum(powers, axis=axis, keepdims=True)


def second_norm_kernel(images, attended, gain, normed):
    def image(i, carry):
        plain, _ = standardize(images[i].astype(F32) + attended[i].astype(F32))
        normed[i] = (plain * gain[...]).astype(BF)
        return carry

    lax.fori_loop(0, images.shape[0], image, 0)


def gelu_both(rows):
    inner = 0.7978845608028654 * (rows + 0.044715 * rows * rows * rows)
    curve = jnp.tanh(inner)
    half = 0.5 * (1.0 + curve)
    slope = half + 0.5 * rows * (1.0 - curve * curve) * (
        0.7978845608028654 * (1.0 + 3.0 * 0.044715 * rows * rows)
    )
    return rows * half, slope


def expert_rows(expert, tokens, back, held, gates, w_in, w_out, slots, grads, active, inner, sent):
    width = tokens.shape[1]
    row = held[pl.ds(expert, 1), :]
    gate = gates[pl.ds(expert, 1), :]

    def tile(i, carry):
        at = pl.ds(pl.multiple_of(i * TILE, 16), TILE)
        ids = lax.broadcasted_iota(jnp.int32, (TILE, row.shape[1]), 0) + i * TILE
        hit = ids == row
        pick = jnp.where(hit, 1.0, 0.0).astype(BF)
        scale = jnp.sum(jnp.where(hit, gate, 0.0), axis=1, keepdims=True)
        buffer = dot(pick, tokens[...]).astype(BF)
        slots[at, :] = buffer
        raw = dot(pick, back[...])
        grad = (scale * raw).astype(BF)
        grads[at, :] = grad
        value, slope = gelu_both(dot(buffer, w_in[expert]))
        value = value.astype(BF)
        active[at, :] = value
        delta = (dot(grad, w_out[expert], 1, 1) * slope).astype(BF)
        inner[at, :] = delta
        if sent is not None:
            out = dot(value, w_out[expert]).astype(BF).astype(F32)
            share = jnp.sum(out * raw, axis=1, keepdims=True)
            sent[at, :width] = (scale * out).astype(BF)
            sent[at, width : 2 * width] = dot(delta, w_in[expert], 1, 1).astype(BF)
            lane = lane_ids((TILE, LANES)) == expert
            sent[at, 2 * width :] = jnp.where(lane, share, 0.0).astype(BF)
        return carry

    lax.fori_loop(0, CAP_PAD // TILE, tile, 0)


def return_rows(expert, held_col, sent, total, fresh):
    def image(i, carry):
        at = pl.ds(pl.multiple_of(i * SEQ_PAD, 16), SEQ_PAD)
        column = held_col[at, :]
        column = jnp.sum(
            jnp.where(lane_ids(column.shape) == expert, column, 0), axis=1, keepdims=True
        )
        pick = jnp.where(lane_ids((SEQ_PAD, CAP_PAD)) == column, 1.0, 0.0).astype(BF)
        back = dot(pick, sent[...])
        total[at, :] = back if fresh else total[at, :] + back
        return carry

    lax.fori_loop(0, total.shape[0] // SEQ_PAD, image, 0)


def weight_rows(left, right, total, fresh, final):
    width = left.shape[1]

    def step(i, carry):
        at = pl.ds(pl.multiple_of(i * 256, 256), 256)
        grad = dot(left[:, at], right[...], 0, 0)
        if fresh:
            total[at, :] = grad
        else:
            final[at, :] = (total[at, :] + grad).astype(BF)
        return carry

    lax.fori_loop(0, width // 256, step, 0)


def expert_kernel(
    tokens, tokens_pair, back, back_pair, held, held_pair, held_col, w_router, w_in, w_out,
    moe, sums, main,
    gates, gates_pair, slots, grads, active, inner, sent, total, grad_in, grad_out,
):
    x = lax.rem(lax.axis_index("dp"), 2)
    gates[...] = softmax_of(dot(w_router[...], tokens[...], 1, 1), 0)
    gates_pair[...] = softmax_of(dot(w_router[...], tokens_pair[...], 1, 1), 0)
    width = tokens.shape[1]
    for k in range(PAIRED):
        expert = x * PAIRED + k
        expert_rows(
            expert, tokens, back, held, gates, w_in, w_out, slots, grads, active, inner, sent
        )
        return_rows(expert, held_col, sent, total, k == 0)
        weight_rows(slots, inner, grad_in, True, None)
        weight_rows(active, grads, grad_out, True, None)
        expert_rows(
            expert, tokens_pair, back_pair, held_pair, gates_pair, w_in, w_out,
            slots, grads, active, inner, None,
        )
        weight_rows(slots, inner, grad_in, False, main.at[k, 0])
        weight_rows(active, grads, grad_out, False, main.at[k, 1])
    for k in range(PAIRED):
        expert = (1 - x) * PAIRED + k
        expert_rows(
            expert, tokens, back, held, gates, w_in, w_out, slots, grads, active, inner, sent
        )
        return_rows(expert, held_col, sent, total, False)

    def cast(i, carry):
        at = pl.ds(pl.multiple_of(i * SEQ_PAD, 16), SEQ_PAD)
        moe[at, :] = total[at, :width].astype(BF)
        sums[at, :] = total[at, width:].astype(BF)
        return carry

    lax.fori_loop(0, total.shape[0] // SEQ_PAD, cast, 0)


def backward_kernel(
    images, attended, cotangent, moe, sums, qkv, mixed, w_qkv, w_proj, w_router, gain_one, gain_two,
    output, partial, grad_hidden, grad_dense, grad_small,
):
    width = images.shape[2]
    local = w_proj.shape[0]
    grad_dense[...] = jnp.zeros_like(grad_dense)
    grad_small[...] = jnp.zeros_like(grad_small)
    router = w_router[...]

    def image(i, carry):
        rows = images[i].astype(F32)
        hidden = rows + attended[i].astype(F32)
        output[i] = (hidden + moe[i].astype(F32)).astype(BF)[:SEQ]
        plain, root = standardize(hidden)
        normed = (plain * gain_two[...]).astype(BF)
        gates = softmax_of(dot(normed, router, 1, 1), 1)
        grad_gates = sums[i, :, width:].astype(F32)[:, :8]
        grad_logits = gates * (grad_gates - jnp.sum(gates * grad_gates, axis=-1, keepdims=True))
        high = grad_logits.astype(BF)
        low = (grad_logits - high.astype(F32)).astype(BF)
        delta = sums[i, :, :width].astype(F32) + (dot(high, router) + dot(low, router))
        grad_small[0:8, :] += dot(high, normed, 0, 0) + dot(low, normed, 0, 0)
        grad_small[8:9, :] += jnp.sum(delta * plain, axis=0, keepdims=True)
        grad = cotangent[i].astype(F32) + norm_back(delta, plain, root, gain_two[...])
        grad_hidden[i] = grad
        grad = grad.astype(BF)
        weighted = mixed[i]
        grad_dense[3] += dot(weighted, grad, 0, 0)
        grad_mixed = dot(grad, w_proj[...], 1, 1).astype(BF)
        query, key, value = (qkv[s, i] for s in range(3))
        parts = [jnp.zeros(query.shape, F32) for _ in range(3)]
        for head in range(local // HD):
            mask = head_mask(query.shape, head)
            weights = attend(query, key, head)
            alone = jnp.where(mask, grad_mixed, jnp.zeros_like(grad_mixed))
            grad_weights = dot(alone, value, 1, 1)
            center = jnp.sum(weights * grad_weights, axis=-1, keepdims=True)
            scores = (weights * (grad_weights - center)).astype(BF)
            parts[0] = jnp.where(mask, dot(scores, key) * SCALE, parts[0])
            parts[1] = jnp.where(mask, dot(scores, query, 0, 0) * SCALE, parts[1])
            parts[2] = jnp.where(mask, dot(weights.astype(BF), grad_mixed, 0, 0), parts[2])
        first, _ = standardize(rows)
        first = (first * gain_one[...]).astype(BF)
        back = jnp.zeros((SEQ_PAD, width), F32)
        for s in range(3):
            part = parts[s].astype(BF)
            grad_dense[s] += dot(part, first, 0, 0)
            back = back + dot(part, w_qkv[s], 1, 1)
        partial[i] = back.astype(BF)
        return carry

    lax.fori_loop(0, images.shape[0], image, 0)


def last_kernel(images, sums, grad_hidden, gain, grad_images, grad_gain):
    grad_gain[...] = jnp.zeros_like(grad_gain)

    def image(i, carry):
        plain, root = standardize(images[i].astype(F32))
        delta = sums[i].astype(F32)
        grad_gain[0:1, :] += jnp.sum(delta * plain, axis=0, keepdims=True)
        grad_images[i] = (grad_hidden[i] + norm_back(delta, plain, root, gain[...]))[:SEQ]
        return carry

    lax.fori_loop(0, images.shape[0], image, 0)


def call(kernel, outs, scratch, *args, flops=0):
    vmem = pl.BlockSpec(memory_space=pltpu.VMEM)
    return pl.pallas_call(
        kernel,
        out_shape=tuple(jax.ShapeDtypeStruct(shape, kind) for shape, kind in outs),
        in_specs=[vmem] * len(args),
        out_specs=tuple(vmem for _ in outs),
        scratch_shapes=[pltpu.VMEM(shape, kind) for shape, kind in scratch],
        compiler_params=pltpu.CompilerParams(vmem_limit_bytes=VMEM_LIMIT),
        cost_estimate=pl.CostEstimate(flops=flops, bytes_accessed=10**7, transcendentals=0),
    )(*args)


def add_rows(out, left, right, start, rows, tile):
    def step(i, carry):
        at = pl.ds(pl.multiple_of(start + i * tile, 16), tile)
        out[at, :] = (left[at, :].astype(F32) + right[at, :].astype(F32)).astype(BF)
        return carry

    lax.fori_loop(0, rows // tile, step, 0)


def tree_kernel(
    parts, main_ref, dense_ref, out_ref,
    got_x, got_low, got_mid, part_sum, total,
    send_x, recv_x, send_low, recv_low, send_mid, recv_mid, send_down, recv_down, send_pair, recv_pair, keep,
):
    place = lax.axis_index("dp")
    x = lax.rem(place, 2)
    z = place // 2
    inner = jnp.logical_or(z == 1, z == 2)
    outer = jnp.logical_not(inner)
    pair = place + 1 - 2 * x
    line = (z + 1 - 2 * lax.rem(z, 2)) * 2 + x
    middle = (3 - z) * 2 + x
    main_rows = main_ref.shape[0]
    dense_rows = dense_ref.shape[1]
    rows = main_rows // parts
    spans = [(i * rows, rows, 48) for i in range(parts)] + [(main_rows, dense_rows, 80)]

    barrier = pltpu.get_barrier_semaphore()
    for peer in (pair, line):
        pl.semaphore_signal(barrier, inc=1, device_id={"dp": peer}, device_id_type=MESH)

    @pl.when(inner)
    def _():
        pl.semaphore_signal(barrier, inc=1, device_id={"dp": middle}, device_id_type=MESH)
        pl.semaphore_wait(barrier, 3)

    @pl.when(outer)
    def _():
        pl.semaphore_wait(barrier, 2)

    def send(src, dst, sems, recvs, i, peer):
        return pltpu.make_async_remote_copy(
            src_ref=src, dst_ref=dst, send_sem=sems.at[i], recv_sem=recvs.at[i],
            device_id={"dp": peer}, device_id_type=MESH,
        )

    def at(ref, i):
        start, count, _ = spans[i]
        return ref.at[pl.ds(start, count), :]

    def x_copy():
        return send(dense_ref.at[1 - x], got_x, send_x, recv_x, 0, pair)

    def low_copy(i):
        source = at(main_ref, i) if i < parts else at(part_sum, i)
        return send(source, at(got_low, i), send_low, recv_low, i, line)

    def mid_copy(i):
        return send(at(part_sum, i), at(got_mid, i), send_mid, recv_mid, i, middle)

    def down_copy(i):
        return send(at(total, i), at(total, i), send_down, recv_down, i, line)

    def pair_copy(i):
        start, count, _ = spans[i]
        return send(
            at(total, i), out_ref.at[x, pl.ds(start, count), :], send_pair, recv_pair, i, pair
        )

    def keep_copy(i):
        start, count, _ = spans[i]
        return pltpu.make_async_copy(
            at(total, i), out_ref.at[x, pl.ds(start, count), :], keep.at[i]
        )

    x_copy().start()

    @pl.when(outer)
    def _():
        for i in range(parts):
            low_copy(i).start()

    x_copy().wait()

    def join(i, carry):
        here = pl.ds(pl.multiple_of(i * 80, 16), 80)
        there = pl.ds(pl.multiple_of(main_rows + i * 80, 16), 80)
        part_sum[there, :] = (
            dense_ref[x, here, :].astype(F32) + got_x[here, :].astype(F32)
        ).astype(BF)
        return carry

    lax.fori_loop(0, dense_rows // 80, join, 0)
    order = list(range(parts + 1))

    @pl.when(outer)
    def _():
        low_copy(parts).start()
        for i in order:
            down_copy(i).wait_recv()
            pair_copy(i).start()
            keep_copy(i).start()

    @pl.when(inner)
    def _():
        def finish(i):
            mid_copy(i).wait_recv()
            start, count, tile = spans[i]
            add_rows(total, part_sum, got_mid, start, count, tile)
            down_copy(i).start()
            pair_copy(i).start()
            keep_copy(i).start()

        for n, i in enumerate(order):
            low_copy(i).wait_recv()
            start, count, tile = spans[i]
            if i == parts:
                add_rows(part_sum, part_sum, got_low, start, count, tile)
            else:
                add_rows(part_sum, main_ref, got_low, start, count, tile)
            mid_copy(i).start()
            if n:
                finish(order[n - 1])
        finish(order[-1])

    @pl.when(outer)
    def _():
        for i in order:
            low_copy(i).wait_send()

    @pl.when(inner)
    def _():
        for i in order:
            mid_copy(i).wait_send()
            down_copy(i).wait_send()

    for i in order:
        keep_copy(i).wait()
        pair_copy(i).wait()


def tree_sum(main, dense, parts):
    rows = main.shape[0] + dense.shape[1]
    width = main.shape[1]
    vmem = pl.BlockSpec(memory_space=pltpu.VMEM)
    sems = [pltpu.SemaphoreType.DMA((parts + 1,))] * 9
    return pl.pallas_call(
        functools.partial(tree_kernel, parts),
        out_shape=jax.ShapeDtypeStruct((2, rows, width), BF),
        in_specs=[vmem, vmem],
        out_specs=pl.BlockSpec(memory_space=pl.ANY),
        scratch_shapes=[pltpu.VMEM((dense.shape[1], width), BF)]
        + [pltpu.VMEM((rows, width), BF)] * 4
        + [pltpu.SemaphoreType.DMA((1,))] * 2
        + sems,
        compiler_params=pltpu.CompilerParams(
            collective_id=0, has_side_effects=True, vmem_limit_bytes=58 * 2**20
        ),
        cost_estimate=pl.CostEstimate(flops=10**8, bytes_accessed=10**8, transcendentals=0),
    )(main, dense)


def swap_sum(main, dense):
    n_dp = lax.axis_size("dp")
    x = lax.axis_index("dp") % 2

    def swap(value, step):
        return lax.ppermute(value, "dp", [(i, i ^ step) for i in range(n_dp)])

    gone = lax.dynamic_index_in_dim(dense, 1 - x, 0, keepdims=False)
    mine = lax.dynamic_index_in_dim(dense, x, 0, keepdims=False)
    joined = (mine.astype(F32) + swap(gone, 1).astype(F32)).astype(BF)
    total = jnp.concatenate([main, joined], axis=0)
    step = 2
    while step < n_dp:
        total = (total.astype(F32) + swap(total, step).astype(F32)).astype(BF)
        step *= 2
    other = swap(total, 1)
    return jnp.where(x == 0, jnp.stack([total, other]), jnp.stack([other, total]))


def per_device(
    images,
    w_qkv,
    w_proj,
    w_router,
    w_in,
    w_out,
    gain_one,
    gain_two,
    routes,
    order,
    counts,
    cotangent,
):
    img_count, seq_len, width = images.shape
    tokens = img_count * seq_len
    local = w_proj.shape[0]
    n_dp = lax.axis_size("dp")
    swap = [(i, i ^ 1) for i in range(n_dp)]
    routes_g = routes.reshape(tokens, TOPK)
    held, kept_pairs = route_slots(routes_g, order[0], counts[0])
    held = jnp.pad(
        held.reshape(img_count, seq_len, SPECIALIST_TOTAL),
        ((0, 0), (0, SEQ_PAD - seq_len), (0, LANES - SPECIALIST_TOTAL)),
        constant_values=-1,
    )
    padded = img_count * SEQ_PAD
    held_col = held.reshape(padded, LANES)
    held_row = held_col[:, :8].T
    held_pair = lax.ppermute(held_row, "dp", swap)
    pads = ((0, 0), (0, SEQ_PAD - seq_len), (0, 0))
    rows = jnp.pad(images, pads)
    back = jnp.pad(cotangent, pads)
    back_pair = lax.ppermute(back, "dp", swap)
    router = jnp.pad(w_router.T, ((0, 8 - SPECIALIST_TOTAL), (0, 0)))
    gain_one = gain_one[None]
    gain_two = gain_two[None]
    cube = (img_count, SEQ_PAD, width)
    flat = (padded, width)

    partial, qkv, mixed = call(
        attention_kernel,
        [(cube, BF), ((3, img_count, SEQ_PAD, local), BF), ((img_count, SEQ_PAD, local), BF)],
        [],
        rows, w_qkv, w_proj, gain_one,
        flops=3 * 10**9,
    )
    attended = pair_sum(partial)
    (normed,) = call(second_norm_kernel, [(cube, BF)], [], rows, attended, gain_two)
    normed_pair = lax.ppermute(normed, "dp", swap)
    work = (CAP_PAD, width)
    wide = 2 * width + LANES
    moe, sums, main = call(
        expert_kernel,
        [(flat, BF), ((padded, width + LANES), BF), ((PAIRED, 2, width, width), BF)],
        [((8, padded), F32)] * 2
        + [(work, BF)] * 4
        + [((CAP_PAD, wide), BF), ((padded, wide), F32)]
        + [((width, width), F32)] * 2,
        normed.reshape(flat), normed_pair.reshape(flat), back.reshape(flat), back_pair.reshape(flat),
        held_row, held_pair, held_col, router, w_in, w_out,
        flops=5 * 10**10,
    )
    moe = pair_sum(moe).reshape(cube)
    sums = pair_sum(jnp.pad(sums, ((0, 0), (0, LANES))))[:, : width + LANES]
    output, partial, grad_hidden, grad_dense, grad_small = call(
        backward_kernel,
        [
            (images.shape, BF),
            (cube, BF),
            (cube, F32),
            ((4, local, width), F32),
            ((16, width), F32),
        ],
        [],
        rows, attended, back, moe, sums.reshape(img_count, SEQ_PAD, width + LANES),
        qkv, mixed, w_qkv, w_proj, router, gain_one, gain_two,
        flops=6 * 10**9,
    )
    grad_images, grad_gain = call(
        last_kernel,
        [(images.shape, F32), ((8, width), F32)],
        [],
        rows, pair_sum(partial), grad_hidden, gain_one,
    )

    dense_rows = grad_dense.reshape(4 * local, width)
    dense = jnp.concatenate([dense_rows, grad_small[:9], grad_gain[:1]]).astype(BF)
    dense = jnp.pad(dense, ((0, 2 * DENSE_HALF - dense.shape[0]), (0, 0)))
    dense = dense.reshape(2, DENSE_HALF, width)
    main = main.reshape(-1, width)
    if n_dp == 8:
        whole = tree_sum(main, dense, 16)
    else:
        whole = swap_sum(main, dense)
    main_rows = main.shape[0]
    experts = whole[:, :main_rows].reshape(SPECIALIST_TOTAL, 2, width, width)
    dense = whole[:, main_rows:].reshape(2 * DENSE_HALF, width).astype(F32)
    grads = dense[: 3 * local].reshape(3, local, width)
    small = dense[4 * local :]
    return (
        output,
        grad_images,
        grads.transpose(0, 2, 1),
        dense[3 * local : 4 * local],
        small[:SPECIALIST_TOTAL].T,
        experts[:, 0].astype(F32),
        experts[:, 1].astype(F32),
        small[9],
        small[8],
        kept_pairs.reshape(img_count, seq_len, TOPK),
    )


def solution(mesh):
    return jax.shard_map(
        per_device,
        mesh=mesh,
        in_specs=(
            P("dp", None, None),
            P(None, None, "tensor"),
            P("tensor", None),
            P(),
            P(None, None, "tensor"),
            P(None, "tensor", None),
            P(),
            P(),
            P("dp", None, None),
            P("dp", None),
            P("dp"),
            P("dp", None, None),
        ),
        out_specs=(
            P("dp", None, None),
            P("dp", None, None),
            P(None, None, "tensor"),
            P("tensor", None),
            P(),
            P(None, None, "tensor"),
            P(None, "tensor", None),
            P(),
            P(),
            P("dp", None, None),
        ),
        check_vma=False,
    )
```

```python
import functools

import jax
import jax.numpy as jnp
from jax import lax
from jax.experimental import pallas as pl
from jax.experimental.pallas import tpu as pltpu
from jax.sharding import PartitionSpec as P

HD = 64
SPECIALIST_TOTAL = 4
TOPK = 2
SEQ = 197
SEQ_PAD = 208
CAP = 616
CAP_PAD = 640
TILE = 320
PAIRED = SPECIALIST_TOTAL // 2
LANES = 128
PIECE = 128
RING = 4
DENSE_CUTS = ((0, 96), (96, 96), (192, 96), (288, 96), (384, 16))
DENSE_HALF = 400


EPSILON = 1e-06
SCALE = 0.125
BF = jnp.bfloat16
F32 = jnp.float32
MESH = pl.DeviceIdType.MESH
VMEM_LIMIT = 62 * 2**20


def dot(left, right, left_dim=1, right_dim=0):
    return lax.dot_general(
        left, right, (((left_dim,), (right_dim,)), ((), ())), preferred_element_type=F32
    )


def lane_ids(shape):
    return lax.broadcasted_iota(jnp.int32, shape, len(shape) - 1)


def standardize(rows):
    center = jnp.mean(rows, axis=-1, keepdims=True)
    centred = rows - center
    spread = jnp.mean(centred * centred, axis=-1, keepdims=True)
    root = lax.rsqrt(spread + EPSILON)
    return centred * root, root


def norm_back(grad, plain, root, gain):
    grad = grad * gain
    first = jnp.mean(grad, axis=-1, keepdims=True)
    second = jnp.mean(grad * plain, axis=-1, keepdims=True)
    return root * (grad - first - plain * second)


def route_slots(routes_g, order_g, count_g):
    tokens = routes_g.shape[0]
    positions = jnp.arange(tokens, dtype=jnp.int32)
    in_image = (positions // SEQ < count_g).astype(jnp.int32)
    capacity_now = (5 * TOPK * count_g * SEQ + 4 * SPECIALIST_TOTAL - 1) // (4 * SPECIALIST_TOTAL)
    spots = order_g[:, None] == positions[None, :]
    place = jnp.sum(jnp.where(spots, positions[:, None], 0), axis=0)
    earlier = (place[None, :] < place[:, None]).astype(BF)
    experts = jnp.arange(SPECIALIST_TOTAL, dtype=jnp.int32)
    marks = (routes_g[:, :, None] == experts).astype(jnp.int32) * in_image[:, None, None]
    marks = marks.reshape(tokens, TOPK * SPECIALIST_TOTAL)
    before = jnp.dot(earlier, marks.astype(BF), preferred_element_type=F32)
    before = before.reshape(tokens, TOPK, SPECIALIST_TOTAL).astype(jnp.int32)
    marks = marks.reshape(tokens, TOPK, SPECIALIST_TOTAL)
    first_total = jnp.sum(marks[:, 0, :], axis=0)
    before = before + jnp.stack([jnp.zeros_like(first_total), first_total])[None]
    slot_of = jnp.sum(before * marks, axis=-1)
    kept_pairs = in_image[:, None] * (slot_of < capacity_now).astype(jnp.int32)
    held = jnp.max(jnp.where((marks * kept_pairs[:, :, None]) > 0, before, -1), axis=1)
    return (held, kept_pairs)


def pair_sum(partial):
    n_t = lax.axis_size("tensor")
    core = lax.axis_index("tensor") % 2
    half = partial.shape[-1] // 2
    other = [(i, i ^ 1) for i in range(n_t)]
    mine = lax.dynamic_slice_in_dim(partial, core * half, half, partial.ndim - 1)
    gone = lax.dynamic_slice_in_dim(partial, (1 - core) * half, half, partial.ndim - 1)
    got = lax.ppermute(gone, "tensor", other)
    total = (mine.astype(F32) + got.astype(F32)).astype(BF)
    step = 2
    while step < n_t:
        got = lax.ppermute(total, "tensor", [(i, i ^ step) for i in range(n_t)])
        total = (total.astype(F32) + got.astype(F32)).astype(BF)
        step *= 2
    back = lax.ppermute(total, "tensor", other)
    return jnp.where(
        core == 0,
        jnp.concatenate([total, back], axis=-1),
        jnp.concatenate([back, total], axis=-1),
    )


def head_mask(shape, head):
    return lane_ids(shape) // HD == head


def image_rows(i):
    return pl.ds(pl.multiple_of(i * SEQ_PAD, 16), SEQ_PAD)


def attend(query, key, head):
    alone = jnp.where(head_mask(query.shape, head), query, jnp.zeros_like(query))
    scores = dot(alone, key, 1, 1) * SCALE
    scores = jnp.where(lane_ids(scores.shape) < SEQ, scores, -jnp.inf)
    powers = jnp.exp(scores - jnp.max(scores, axis=-1, keepdims=True))
    return powers / jnp.sum(powers, axis=-1, keepdims=True)


def attention_image(i, images, w_qkv, w_proj, gain, partial, qkv, mixed):
    at = image_rows(i)
    plain, _ = standardize(images[at, :].astype(F32))
    normed = (plain * gain[...]).astype(BF)
    for s in range(3):
        qkv[s, at, :] = dot(normed, w_qkv[s]).astype(BF)
    query, key, value = (qkv[s, at, :] for s in range(3))
    result = jnp.zeros(query.shape, F32)
    for head in range(query.shape[1] // HD):
        weights = attend(query, key, head).astype(BF)
        result = jnp.where(head_mask(query.shape, head), dot(weights, value), result)
    result = result.astype(BF)
    mixed[at, :] = result
    partial[at, :] = dot(result, w_proj[...]).astype(BF)


def softmax_of(logits, axis):
    ids = lax.broadcasted_iota(jnp.int32, logits.shape, axis)
    logits = jnp.where(ids < SPECIALIST_TOTAL, logits, -jnp.inf)
    powers = jnp.exp(logits - jnp.max(logits, axis=axis, keepdims=True))
    return powers / jnp.sum(powers, axis=axis, keepdims=True)


def second_norm_image(i, images, attended, gain, normed):
    at = image_rows(i)
    plain, _ = standardize(images[at, :].astype(F32) + attended[at, :].astype(F32))
    normed[at, :] = (plain * gain[...]).astype(BF)


def gelu_both(rows):
    inner = 0.7978845608028654 * (rows + 0.044715 * rows * rows * rows)
    curve = jnp.tanh(inner)
    half = 0.5 * (1.0 + curve)
    slope = half + 0.5 * rows * (1.0 - curve * curve) * (
        0.7978845608028654 * (1.0 + 3.0 * 0.044715 * rows * rows)
    )
    return rows * half, slope


def expert_rows(expert, tokens, back, held, gates, w_in, w_out, factors, offset, sent, tick):
    width = tokens.shape[1]
    row = held[pl.ds(expert, 1), :]
    gate = gates[pl.ds(expert, 1), :]

    def tile(i, carry):
        ids = lax.broadcasted_iota(jnp.int32, (TILE, row.shape[1]), 0) + i * TILE
        hit = ids == row
        pick = jnp.where(hit, 1.0, 0.0).astype(BF)
        scale = jnp.sum(jnp.where(hit, gate, 0.0), axis=1, keepdims=True)
        buffer = dot(pick, tokens[...]).astype(BF)
        raw = dot(pick, back[...])
        grad = (scale * raw).astype(BF)
        value, slope = gelu_both(dot(buffer, w_in[...]))
        value = value.astype(BF)
        delta = (dot(grad, w_out[...], 1, 1) * slope).astype(BF)
        if factors is not None:
            at = pl.ds(pl.multiple_of(offset + i * TILE, 16), TILE)
            for ref, rows in zip(factors, (buffer, delta, value, grad)):
                ref[at, :] = rows
        if sent is not None:
            at = pl.ds(pl.multiple_of(i * TILE, 16), TILE)
            out = dot(value, w_out[...]).astype(BF).astype(F32)
            share = jnp.sum(out * raw, axis=1, keepdims=True)
            sent[at, :width] = (scale * out).astype(BF)
            sent[at, width : 2 * width] = dot(delta, w_in[...], 1, 1).astype(BF)
            lane = lane_ids((TILE, LANES)) == expert
            sent[at, 2 * width :] = jnp.where(lane, share, 0.0).astype(BF)
        if tick is not None:
            tick(i)
        return carry

    lax.fori_loop(0, CAP_PAD // TILE, tile, 0)


def return_rows(expert, held_col, sent, total, fresh, final, after):
    def image(i, carry):
        at = image_rows(i)
        column = held_col[at, :]
        column = jnp.sum(
            jnp.where(lane_ids(column.shape) == expert, column, 0), axis=1, keepdims=True
        )
        pick = jnp.where(lane_ids((SEQ_PAD, CAP_PAD)) == column, 1.0, 0.0).astype(BF)
        back = dot(pick, sent[...])
        if final is None:
            total[at, :] = back if fresh else total[at, :] + back
        else:
            back = back + total[at, :]
            start = 0
            for ref in final:
                ref[at, :] = back[:, start : start + ref.shape[1]].astype(BF)
                start += ref.shape[1]
        if after is not None:
            after(i)
        return carry

    lax.fori_loop(0, total.shape[0] // SEQ_PAD, image, 0)


def weight_rows(left, right, final, start, after):
    def step(i, carry):
        rows = pl.ds(pl.multiple_of(i * 256, 256), 256)
        to = pl.ds(pl.multiple_of(start + i * 256, 256), 256)
        final[to, :] = dot(left[:, rows], right[...], 0, 0).astype(BF)
        if after is not None:
            after(i)
        return carry

    lax.fori_loop(0, left.shape[1] // 256, step, 0)


def backward_image(
    i, images, attended, cotangent, sums, gate_sums, qkv, mixed, w_qkv, w_proj, w_router,
    gain_one, gain_two, partial, grad_hidden, grad_dense, grad_small,
):
    width = images.shape[1]
    at = image_rows(i)
    router = w_router[...]
    rows = images[at, :].astype(F32)
    plain, root = standardize(rows + attended[at, :].astype(F32))
    normed = (plain * gain_two[...]).astype(BF)
    gates = softmax_of(dot(normed, router, 1, 1), 1)
    grad_gates = gate_sums[at, :].astype(F32)[:, :8]
    grad_logits = gates * (grad_gates - jnp.sum(gates * grad_gates, axis=-1, keepdims=True))
    high = grad_logits.astype(BF)
    low = (grad_logits - high.astype(F32)).astype(BF)
    delta = sums[at, :].astype(F32) + (dot(high, router) + dot(low, router))
    grad_small[0:8, :] += dot(high, normed, 0, 0) + dot(low, normed, 0, 0)
    grad_small[8:9, :] += jnp.sum(delta * plain, axis=0, keepdims=True)
    grad = cotangent[at, :].astype(F32) + norm_back(delta, plain, root, gain_two[...])
    grad_hidden[at, :width] = grad
    grad = grad.astype(BF)
    grad_dense[3] += dot(mixed[at, :], grad, 0, 0)
    grad_mixed = dot(grad, w_proj[...], 1, 1).astype(BF)
    query, key, value = (qkv[s, at, :] for s in range(3))
    parts = [jnp.zeros(query.shape, F32) for _ in range(3)]
    for head in range(query.shape[1] // HD):
        mask = head_mask(query.shape, head)
        weights = attend(query, key, head)
        alone = jnp.where(mask, grad_mixed, jnp.zeros_like(grad_mixed))
        grad_weights = dot(alone, value, 1, 1)
        center = jnp.sum(weights * grad_weights, axis=-1, keepdims=True)
        scores = (weights * (grad_weights - center)).astype(BF)
        parts[0] = jnp.where(mask, dot(scores, key) * SCALE, parts[0])
        parts[1] = jnp.where(mask, dot(scores, query, 0, 0) * SCALE, parts[1])
        parts[2] = jnp.where(mask, dot(weights.astype(BF), grad_mixed, 0, 0), parts[2])
    first, _ = standardize(rows)
    first = (first * gain_one[...]).astype(BF)
    back = jnp.zeros((SEQ_PAD, width), F32)
    for s in range(3):
        part = parts[s].astype(BF)
        grad_dense[s] += dot(part, first, 0, 0)
        back = back + dot(part, w_qkv[s], 1, 1)
    partial[at, :] = back.astype(BF)


def output_image(i, images, attended, moe, output):
    at = image_rows(i)
    hidden = images[at, :].astype(F32) + attended[at, :].astype(F32)
    output[at, :] = (hidden + moe[at, :].astype(F32)).astype(BF)


def last_image(i, images, sums, grad_hidden, gain, grad_images, start, grad_gain):
    width = images.shape[1]
    at = image_rows(i)
    plain, root = standardize(images[at, :].astype(F32))
    delta = sums[at, :].astype(F32)
    grad_gain[0:1, :] += jnp.sum(delta * plain, axis=0, keepdims=True)
    grad = grad_hidden[at, :width] + norm_back(delta, plain, root, gain[...])
    grad_images[at, start : start + width] = grad


def loop(count, body):
    def step(i, carry):
        body(i)
        return carry

    lax.fori_loop(0, count, step, 0)


def attention_kernel(images, w_qkv, w_proj, gain, partial, qkv, mixed):
    loop(
        images.shape[0] // SEQ_PAD,
        lambda i: attention_image(i, images, w_qkv, w_proj, gain, partial, qkv, mixed),
    )


def second_norm_kernel(images, attended, gain, normed):
    loop(
        images.shape[0] // SEQ_PAD, lambda i: second_norm_image(i, images, attended, gain, normed)
    )


def expert_kernel(
    tokens, tokens_pair, back, back_pair, held, held_pair, held_col, w_router, w_in, w_out,
    moe, sums, gate_sums, main,
    gates, gates_pair, slots, inner, active, grads, sent, total,
):
    x = lax.rem(lax.axis_index("dp"), 2)
    gates[...] = softmax_of(dot(w_router[...], tokens[...], 1, 1), 0)
    gates_pair[...] = softmax_of(dot(w_router[...], tokens_pair[...], 1, 1), 0)
    width = tokens.shape[1]
    factors = (slots, inner, active, grads)
    for k in range(SPECIALIST_TOTAL):
        expert = lax.rem(x + k // PAIRED, 2) * PAIRED + k % PAIRED
        weights = (w_in.at[expert], w_out.at[expert])
        mine = factors if k < PAIRED else None
        expert_rows(expert, tokens, back, held, gates, *weights, mine, 0, sent, None)
        final = (moe, sums, gate_sums) if k == SPECIALIST_TOTAL - 1 else None
        return_rows(expert, held_col, sent, total, k == 0, final, None)
        if k < PAIRED:
            expert_rows(
                expert, tokens_pair, back_pair, held_pair, gates_pair, *weights, mine, CAP_PAD, None, None
            )
            weight_rows(slots, inner, main, 2 * k * width, None)
            weight_rows(active, grads, main, (2 * k + 1) * width, None)


def backward_kernel(
    images, attended, cotangent, moe, sums, gate_sums, qkv, mixed, w_qkv, w_proj, w_router,
    gain_one, gain_two,
    output, partial, grad_hidden, grad_dense, grad_small,
):
    grad_dense[...] = jnp.zeros_like(grad_dense)
    grad_small[...] = jnp.zeros_like(grad_small)

    def image(i):
        backward_image(
            i, images, attended, cotangent, sums, gate_sums, qkv, mixed, w_qkv, w_proj, w_router,
            gain_one, gain_two, partial, grad_hidden, grad_dense, grad_small,
        )
        output_image(i, images, attended, moe, output)

    loop(images.shape[0] // SEQ_PAD, image)


def last_kernel(images, sums, grad_hidden, gain, grad_images, grad_gain):
    grad_gain[...] = jnp.zeros_like(grad_gain)
    loop(
        images.shape[0] // SEQ_PAD,
        lambda i: last_image(i, images, sums, grad_hidden, gain, grad_images, 0, grad_gain),
    )


def call(kernel, outs, scratch, *args, flops=0):
    vmem = pl.BlockSpec(memory_space=pltpu.VMEM)
    return pl.pallas_call(
        kernel,
        out_shape=tuple(jax.ShapeDtypeStruct(shape, kind) for shape, kind in outs),
        in_specs=[vmem] * len(args),
        out_specs=tuple(vmem for _ in outs),
        scratch_shapes=[pltpu.VMEM(shape, kind) for shape, kind in scratch],
        compiler_params=pltpu.CompilerParams(vmem_limit_bytes=VMEM_LIMIT),
        cost_estimate=pl.CostEstimate(flops=flops, bytes_accessed=10**7, transcendentals=0),
    )(*args)


def swap_sum(main, dense):
    n_dp = lax.axis_size("dp")
    x = lax.axis_index("dp") % 2

    def swap(value, step):
        return lax.ppermute(value, "dp", [(i, i ^ step) for i in range(n_dp)])

    gone = lax.dynamic_index_in_dim(dense, 1 - x, 0, keepdims=False)
    mine = lax.dynamic_index_in_dim(dense, x, 0, keepdims=False)
    joined = (mine.astype(F32) + swap(gone, 1).astype(F32)).astype(BF)
    total = jnp.concatenate([main, joined], axis=0)
    step = 2
    while step < n_dp:
        total = (total.astype(F32) + swap(total, step).astype(F32)).astype(BF)
        step *= 2
    other = swap(total, 1)
    return jnp.where(x == 0, jnp.stack([total, other]), jnp.stack([other, total]))


def plain_step(rows, back, held_row, held_col, w_qkv, w_proj, router, w_in, w_out, gain_one, gain_two):
    padded, width = rows.shape
    local = w_proj.shape[0]
    n_dp = lax.axis_size("dp")
    swap = [(i, i ^ 1) for i in range(n_dp)]
    flat = (padded, width)
    held_pair = lax.ppermute(held_row, "dp", swap)
    back_pair = lax.ppermute(back, "dp", swap)
    partial, qkv, mixed = call(
        attention_kernel,
        [(flat, BF), ((3, padded, local), BF), ((padded, local), BF)],
        [],
        rows, w_qkv, w_proj, gain_one,
    )
    attended = pair_sum(partial)
    (normed,) = call(second_norm_kernel, [(flat, BF)], [], rows, attended, gain_two)
    normed_pair = lax.ppermute(normed, "dp", swap)
    wide = 2 * width + LANES
    moe, sums, gate_sums, main = call(
        expert_kernel,
        [(flat, BF), (flat, BF), ((padded, LANES), BF), ((4 * width, width), BF)],
        [((8, padded), F32)] * 2
        + [((2 * CAP_PAD, width), BF)] * 4
        + [((CAP_PAD, wide), BF), ((padded, wide), F32)],
        normed, normed_pair, back, back_pair,
        held_row, held_pair, held_col, router, w_in, w_out,
    )
    moe = pair_sum(moe)
    sums = pair_sum(sums)
    gate_sums = pair_sum(jnp.concatenate([gate_sums, gate_sums], axis=-1))[:, :LANES]
    output, partial, grad_hidden, grad_dense, grad_small = call(
        backward_kernel,
        [(flat, BF), (flat, BF), (flat, F32), ((4, local, width), F32), ((16, width), F32)],
        [],
        rows, attended, back, moe, sums, gate_sums,
        qkv, mixed, w_qkv, w_proj, router, gain_one, gain_two,
    )
    grad_images, grad_gain = call(
        last_kernel,
        [(flat, F32), ((8, width), F32)],
        [],
        rows, pair_sum(partial), grad_hidden, gain_one,
    )
    dense = grad_dense.reshape(2, 2 * local, width)
    small = jnp.stack([grad_small, jnp.pad(grad_gain, ((0, 8), (0, 0)))])
    dense = jnp.concatenate([dense, small], axis=1).astype(BF)
    whole = swap_sum(main, dense)
    rows_main = main.shape[0]
    experts = whole[:, :rows_main].reshape(SPECIALIST_TOTAL, 2, width, width)
    return output, grad_images, experts[:, 0], experts[:, 1], whole[:, rows_main:]


(
    ATT_RS, ATT_Y, ATT_AG, Z_X, Z_CORE, D_RS, G_RS, D_Y, G_Y, D_AG,
    O_RS, O_Y, O_AG, B_RS, B_Y, B_AG, COT, DENSE,
) = range(18)


def step_kernel(
    images, cotangent, held, held_pair, held_col, w_qkv, w_proj, router, gain_one, gain_two, w_in, w_out,
    output, grad_images, out_in, out_out, out_dense,
    back_pair, tokens, tokens_pair, attended, partial, qkv, mixed,
    core_a, far_a, core_d, far_d, core_o, far_o, core_g, far_g, gate_part, gate_sum,
    gates, gates_pair, slots, inner, active, grads, sent, total, slot_in, slot_out,
    grad_dense, grad_small, grad_last, main, landed, middle_ring, dense, dense_x, dense_landed, dense_middle,
    sends, recvs, weight_sems, send_low, recv_low, send_mid, recv_mid, send_down, recv_down,
    send_pair, recv_pair, keep, out_sems,
):
    place = lax.axis_index("dp")
    spot = lax.axis_index("tensor")
    x = lax.rem(place, 2)
    z = place // 2
    c = lax.rem(spot, 2)
    y = spot // 2
    inside = jnp.logical_or(z == 1, z == 2)
    outside = jnp.logical_not(inside)
    core = {"tensor": spot + 1 - 2 * c}
    far = {"tensor": spot + 2 - 4 * y}
    pair = {"dp": place + 1 - 2 * x}
    line = {"dp": (z + 1 - 2 * lax.rem(z, 2)) * 2 + x}
    middle = {"dp": (3 - z) * 2 + x}
    width = images.shape[1]
    half = width // 2
    count = images.shape[0] // SEQ_PAD
    pieces = main.shape[0] // PIECE
    per_expert = 2 * width // PIECE
    mine = pl.ds(pl.multiple_of(c * half, LANES), half)
    other = pl.ds(pl.multiple_of((1 - c) * half, LANES), half)
    local = w_proj.shape[0]

    barrier = pltpu.get_barrier_semaphore()
    for peer in (core, far, pair, line):
        pl.semaphore_signal(barrier, inc=1, device_id=peer, device_id_type=MESH)

    @pl.when(inside)
    def _():
        pl.semaphore_signal(barrier, inc=1, device_id=middle, device_id_type=MESH)

    def load(k):
        expert = lax.rem(x + k // PAIRED, 2) * PAIRED + k % PAIRED
        return [
            pltpu.make_async_copy(w_in.at[expert], slot_in.at[k % 2], weight_sems.at[0, k % 2]),
            pltpu.make_async_copy(w_out.at[expert], slot_out.at[k % 2], weight_sems.at[1, k % 2]),
        ]

    for k in range(2):
        for copy in load(k):
            copy.start()
    grad_dense[...] = jnp.zeros_like(grad_dense)
    grad_small[...] = jnp.zeros_like(grad_small)
    grad_last[...] = jnp.zeros_like(grad_last)

    @pl.when(inside)
    def _():
        pl.semaphore_wait(barrier, 5)

    @pl.when(outside)
    def _():
        pl.semaphore_wait(barrier, 4)

    def remote(src, dst, send, recv, peer):
        return pltpu.make_async_remote_copy(
            src_ref=src, dst_ref=dst, send_sem=send, recv_sem=recv,
            device_id=peer, device_id_type=MESH,
        )

    def channel(k, i, src, dst, peer):
        return remote(src, dst, sends.at[k, i], recvs.at[k, i], peer)

    def rs_copy(k, i, part, got):
        return channel(k, i, part.at[image_rows(i), other], got.at[image_rows(i), :], core)

    def far_copy(k, i, part, got):
        return channel(k, i, part.at[image_rows(i), mine], got.at[image_rows(i), :], far)

    def give_copy(k, i, result):
        view = result.at[image_rows(i), mine]
        return channel(k, i, view, view, core)

    def join_core(ks, i, part, near, got):
        at = image_rows(i)
        rs_copy(ks[0], i, part, near).wait_recv()
        rows = part[at, mine].astype(F32) + near[at, :].astype(F32)
        part[at, mine] = rows.astype(BF)
        far_copy(ks[1], i, part, got).start()

    def join_far(ks, i, part, got, result):
        at = image_rows(i)
        far_copy(ks[1], i, part, got).wait_recv()
        rows = part[at, mine].astype(F32) + got[at, :].astype(F32)
        result[at, mine] = rows.astype(BF)
        give_copy(ks[2], i, result).start()

    def sent_all(ks, part, near, got, result):
        def wait(i):
            rs_copy(ks[0], i, part, near).wait_send()
            far_copy(ks[1], i, part, got).wait_send()
            give_copy(ks[2], i, result).wait_send()

        loop(count, wait)

    def staged(step, lag, body):
        i = step - lag

        @pl.when(jnp.logical_and(i >= 0, i < count))
        def _():
            body(i)

    cot_copy = channel(COT, 0, cotangent.at[:, mine], back_pair.at[:, mine], pair)
    cot_give = channel(COT, 1, back_pair.at[:, mine], back_pair.at[:, mine], core)
    cot_copy.start()

    att = (ATT_RS, ATT_Y, ATT_AG)

    def token_copy(i):
        at = image_rows(i)
        return channel(Z_X, i, tokens.at[at, mine], tokens_pair.at[at, mine], pair)

    def token_give(i):
        view = tokens_pair.at[image_rows(i), mine]
        return channel(Z_CORE, i, view, view, core)

    def attention_step(step):
        def first(i):
            attention_image(i, images, w_qkv, w_proj, gain_one, partial, qkv, mixed)
            rs_copy(ATT_RS, i, partial, core_a).start()

        def norm(i):
            give_copy(ATT_AG, i, attended).wait_recv()
            second_norm_image(i, images, attended, gain_two, tokens)
            token_copy(i).start()

        def give(i):
            token_copy(i).wait_recv()
            token_give(i).start()

        staged(step, 0, first)
        staged(step, 1, lambda i: join_core(att, i, partial, core_a, far_a))
        staged(step, 2, lambda i: join_far(att, i, partial, far_a, attended))
        staged(step, 3, norm)
        staged(step, 5, give)

    loop(count + 3, attention_step)
    gates[...] = softmax_of(dot(router[...], tokens[...], 1, 1), 0)

    def piece(n):
        if isinstance(n, int) and n >= pieces:
            start, size = DENSE_CUTS[n - pieces]
            at = pl.ds(start, size)
            views = [ref.at[at, :] for ref in (dense.at[x], dense_landed, dense_middle)]
            return views + [out_dense.at[x, at, :]]
        at = pl.ds(pl.multiple_of(n * PIECE, PIECE), PIECE)
        return [main.at[at, :], landed.at[at, :], middle_ring.at[lax.rem(n, RING)], None]

    def out_views(n):
        if isinstance(n, int) and n >= pieces:
            return [(None, piece(n)[3])]
        per_kind = width // PIECE
        expert = x * PAIRED + n // per_expert
        kind = lax.rem(n // per_kind, 2)
        at = pl.ds(pl.multiple_of(lax.rem(n, per_kind) * PIECE, PIECE), PIECE)
        return [(kind == 0, out_in.at[expert, at, :]), (kind == 1, out_out.at[expert, at, :])]

    def low_copy(n):
        own, got, _, _ = piece(n)
        return remote(own, got, send_low.at[n], recv_low.at[n], line)

    def mid_copy(n):
        own, _, got, _ = piece(n)
        return remote(own, got, send_mid.at[n], recv_mid.at[n], middle)

    def down_copy(n):
        _, done, _, _ = piece(n)
        return remote(done, done, send_down.at[n], recv_down.at[n], line)

    def each_out(n, act):
        done = piece(n)[1]
        for when, view in out_views(n):
            copies = (
                remote(done, view, send_pair.at[n], recv_pair.at[n], pair),
                pltpu.make_async_copy(done, view, keep.at[n]),
            )
            if when is None:
                act(*copies)
            else:
                pl.when(when)(functools.partial(act, *copies))

    def publish(n):
        def act(swap, own):
            swap.start()
            own.start()

        each_out(n, act)

    def add_piece(to, left, right):
        rows = to.shape[0]
        size = 64 if rows % 64 == 0 else 48 if rows % 48 == 0 else 16

        def add(i):
            at = pl.ds(pl.multiple_of(i * size, 16), size)
            to[at, :] = (left[at, :].astype(F32) + right[at, :].astype(F32)).astype(BF)

        loop(rows // size, add)

    last = pieces + len(DENSE_CUTS)

    def tick(n):
        def when(n, body):
            if isinstance(n, int):
                if 0 <= n < last:
                    body(n)
            else:
                pl.when(n >= 0)(functools.partial(body, n))

        def gather(n):
            own, got, _, _ = piece(n)
            low_copy(n).wait_recv()
            add_piece(own, own, got)
            mid_copy(n).start()

        def finish(n):
            own, done, got, _ = piece(n)
            mid_copy(n).wait_recv()
            add_piece(done, own, got)
            down_copy(n).start()
            publish(n)

        def forward(n):
            down_copy(n).wait_recv()
            publish(n)

        @pl.when(inside)
        def _():
            when(n, gather)
            when(n - 1, finish)

        @pl.when(outside)
        def _():
            when(n - 2, forward)

    def lift(n):
        @pl.when(outside)
        def _():
            low_copy(n).start()

    factors = (slots, inner, active, grads)
    turn = 0
    final = (grads.at[: count * SEQ_PAD], slots.at[: count * SEQ_PAD], gate_part)
    moe_part, sum_part, _ = final
    dee = (D_RS, D_Y, D_AG)
    oh = (O_RS, O_Y, O_AG)
    moe, sums = tokens_pair, back_pair

    def gate_near(i):
        at = image_rows(i)
        return channel(G_RS, i, gate_part.at[at, :], core_g.at[at, :], core)

    def gate_far(i):
        at = image_rows(i)
        return channel(G_Y, i, gate_sum.at[at, :], far_g.at[at, :], far)

    def send_parts(i):
        rs_copy(D_RS, i, sum_part, core_d).start()
        gate_near(i).start()
        rs_copy(O_RS, i, moe_part, core_o).start()

    for k in range(SPECIALIST_TOTAL):
        expert = lax.rem(x + k // PAIRED, 2) * PAIRED + k % PAIRED
        weights = (slot_in.at[k % 2], slot_out.at[k % 2])
        for copy in load(k):
            copy.wait()
        kept = factors if k < PAIRED else None
        base = turn
        expert_rows(
            expert, tokens, cotangent, held, gates, *weights, kept, 0, sent,
            (lambda i, base=base: tick(base + i)) if k else None,
        )
        if k:
            turn += 2
        ends = k == SPECIALIST_TOTAL - 1
        return_rows(
            expert, held_col, sent, total, k == 0, final if ends else None,
            send_parts if ends else None,
        )
        if k:
            tick(turn)
            turn += 1
        if k == 0:
            cot_copy.wait_recv()
            cot_give.start()
            for i in range(count - 2, count):
                token_copy(i).wait_recv()
                token_give(i).start()
            loop(count, lambda i: token_give(i).wait_recv())
            cot_give.wait_recv()
            gates_pair[...] = softmax_of(dot(router[...], tokens_pair[...], 1, 1), 0)
            cot_copy.wait_send()
            cot_give.wait_send()
        if k < PAIRED:
            base = turn
            expert_rows(
                expert, tokens_pair, back_pair, held_pair, gates_pair, *weights, kept, CAP_PAD, None,
                (lambda i, base=base: tick(base + i)) if k else None,
            )
            if k:
                turn += 2
            for copy in load(k + 2):
                copy.start()
            per_step = 256 // PIECE
            for kind, (left, right) in enumerate(((slots, inner), (active, grads))):
                first = k * per_expert + kind * (width // PIECE)

                def after(i, first=first):
                    for j in range(per_step):
                        lift(first + i * per_step + j)

                weight_rows(left, right, main, (2 * k + kind) * width, after)
        if k == PAIRED - 1:

            def tokens_sent(i):
                token_copy(i).wait_send()
                token_give(i).wait_send()

            loop(count, tokens_sent)
            sent_all(att, partial, core_a, far_a, attended)

    bee = (B_RS, B_Y, B_AG)

    def backward_step(step):
        def gates_core(i):
            join_core(dee, i, sum_part, core_d, far_d)
            at = image_rows(i)
            gate_near(i).wait_recv()
            rows = gate_part[at, :].astype(F32) + core_g[at, :].astype(F32)
            gate_sum[at, :] = rows.astype(BF)
            gate_far(i).start()

        def gates_all(i):
            join_far(dee, i, sum_part, far_d, sums)
            at = image_rows(i)
            gate_far(i).wait()
            rows = gate_sum[at, :].astype(F32) + far_g[at, :].astype(F32)
            gate_sum[at, :] = rows.astype(BF)

        def back(i):
            give_copy(D_AG, i, sums).wait()
            backward_image(
                i, images, attended, cotangent, sums, gate_sum, qkv, mixed, w_qkv, w_proj, router,
                gain_one, gain_two, partial, total, grad_dense, grad_small,
            )
            rs_copy(B_RS, i, partial, core_a).start()

        def finish(i):
            give_copy(B_AG, i, sums).wait_recv()
            last_image(i, images, sums, total, gain_one, total, width, grad_last)
            grads_out(i).start()

        def emit(i):
            give_copy(O_AG, i, moe).wait()
            output_image(i, images, attended, moe, moe)
            rows_out(i).start()

        staged(step, 0, gates_core)
        staged(step, 1, gates_all)
        staged(step, 2, back)
        staged(step, 3, lambda i: join_core(bee, i, partial, core_a, far_a))
        staged(step, 4, lambda i: join_core(oh, i, moe_part, core_o, far_o))
        staged(step, 4, lambda i: join_far(bee, i, partial, far_a, sums))
        staged(step, 5, finish)
        staged(step, 5, lambda i: join_far(oh, i, moe_part, far_o, moe))
        staged(step, 6, emit)

    def grads_out(i):
        at = image_rows(i)
        return pltpu.make_async_copy(
            total.at[at, pl.ds(width, width)], grad_images.at[at, :], out_sems.at[0, i]
        )

    def rows_out(i):
        at = image_rows(i)
        return pltpu.make_async_copy(moe.at[at, :], output.at[at, :], out_sems.at[1, i])

    base = turn
    steps = count + 6

    def backward_turn(step):
        backward_step(step)
        tick(base + step)

    loop(steps, backward_turn)
    turn += steps

    def pack(i):
        at = pl.ds(pl.multiple_of(i * local, 16), local)
        dense[i // 2, pl.ds(pl.multiple_of(lax.rem(i, 2) * local, 16), local), :] = grad_dense[
            i
        ].astype(BF)

    loop(4, pack)
    dense[0, 2 * local : 2 * local + 16, :] = grad_small[...].astype(BF)
    dense[1, 2 * local : 2 * local + 16, :] = grad_last[...].astype(BF)

    def dense_copy(i):
        start, size = DENSE_CUTS[i]
        at = pl.ds(start, size)
        return channel(DENSE, i, dense.at[1 - x, at, :], dense_x.at[at, :], pair)

    cuts = range(len(DENSE_CUTS))
    for i in cuts:
        dense_copy(i).start()
    dense_from = min(turn + 4, pieces)
    while turn < dense_from:
        tick(turn)
        turn += 1
    for i in cuts:
        start, size = DENSE_CUTS[i]
        at = pl.ds(start, size)
        dense_copy(i).wait()
        dense[x, at, :] = (dense[x, at, :].astype(F32) + dense_x[at, :].astype(F32)).astype(BF)
        lift(pieces + i)
    while turn < last + 2:
        tick(turn)
        turn += 1

    def rest(i):
        rs_copy(D_RS, i, sum_part, core_d).wait_send()
        far_copy(D_Y, i, sum_part, far_d).wait_send()
        gate_near(i).wait_send()
        rs_copy(O_RS, i, moe_part, core_o).wait_send()
        far_copy(O_Y, i, moe_part, far_o).wait_send()
        grads_out(i).wait()
        rows_out(i).wait()

    loop(count, rest)
    sent_all(bee, partial, core_a, far_a, sums)

    def settle(n):
        @pl.when(outside)
        def _():
            low_copy(n).wait_send()

        @pl.when(inside)
        def _():
            mid_copy(n).wait_send()
            down_copy(n).wait_send()

        def act(swap, own):
            swap.wait()
            own.wait()

        each_out(n, act)

    loop(pieces, settle)
    for n in range(pieces, last):
        settle(n)


def eight_step(rows, back, held_row, held_col, w_qkv, w_proj, router, w_in, w_out, gain_one, gain_two):
    padded, width = rows.shape
    local = w_proj.shape[0]
    count = padded // SEQ_PAD
    n_dp = lax.axis_size("dp")
    held_pair = lax.ppermute(held_row, "dp", [(i, i ^ 1) for i in range(n_dp)])
    half = width // 2
    wide = 2 * width + LANES
    pieces = 4 * width // PIECE
    last = pieces + len(DENSE_CUTS)
    vmem = pl.BlockSpec(memory_space=pltpu.VMEM)
    hbm = pl.BlockSpec(memory_space=pl.ANY)
    flat = ((padded, width), BF)
    part = ((padded, half), BF)
    thin = ((padded, LANES), BF)
    square = (width, width)
    dense = ((DENSE_HALF, width), BF)
    scratch = [flat] * 5 + [((3, padded, local), BF), ((padded, local), BF)]
    scratch += [part] * 6 + [thin] * 4
    scratch += [((8, padded), F32)] * 2 + [((2 * CAP_PAD, width), BF)] * 4
    scratch += [((CAP_PAD, wide), BF), ((padded, wide), F32), ((2, *square), BF), ((2, *square), BF)]
    scratch += [((4, local, width), F32)] + [((16, width), F32)] * 2
    scratch += [((4 * width, width), BF)] * 2 + [((RING, PIECE, width), BF)]
    scratch += [((2, DENSE_HALF, width), BF)] + [dense] * 3
    dma = pltpu.SemaphoreType.DMA
    sems = [dma((18, count))] * 2 + [dma((2, 2))] + [dma((last,))] * 9 + [dma((2, count))]
    outs = [(flat[0], BF), (flat[0], F32)] + [((SPECIALIST_TOTAL, *square), BF)] * 2
    outs += [((2, DENSE_HALF, width), BF)]
    return pl.pallas_call(
        step_kernel,
        out_shape=tuple(jax.ShapeDtypeStruct(shape, kind) for shape, kind in outs),
        in_specs=[vmem] * 10 + [hbm] * 2,
        out_specs=tuple(hbm for _ in outs),
        scratch_shapes=[pltpu.VMEM(shape, kind) for shape, kind in scratch] + sems,
        compiler_params=pltpu.CompilerParams(
            collective_id=0, has_side_effects=True, vmem_limit_bytes=VMEM_LIMIT
        ),
        cost_estimate=pl.CostEstimate(flops=6 * 10**10, bytes_accessed=10**8, transcendentals=0),
    )(
        rows, back, held_row, held_pair, held_col, w_qkv, w_proj, router, gain_one, gain_two, w_in, w_out
    )


def per_device(
    images,
    w_qkv,
    w_proj,
    w_router,
    w_in,
    w_out,
    gain_one,
    gain_two,
    routes,
    order,
    counts,
    cotangent,
):
    img_count, seq_len, width = images.shape
    tokens = img_count * seq_len
    local = w_proj.shape[0]
    routes_g = routes.reshape(tokens, TOPK)
    held, kept_pairs = route_slots(routes_g, order[0], counts[0])
    held = jnp.pad(
        held.reshape(img_count, seq_len, SPECIALIST_TOTAL),
        ((0, 0), (0, SEQ_PAD - seq_len), (0, LANES - SPECIALIST_TOTAL)),
        constant_values=-1,
    )
    padded = img_count * SEQ_PAD
    held_col = held.reshape(padded, LANES)
    held_row = held_col[:, :8].T
    pads = ((0, 0), (0, SEQ_PAD - seq_len), (0, 0))
    rows = jnp.pad(images, pads).reshape(padded, width)
    back = jnp.pad(cotangent, pads).reshape(padded, width)
    router = jnp.pad(w_router.T, ((0, 8 - SPECIALIST_TOTAL), (0, 0)))
    step = eight_step if lax.axis_size("dp") == 8 else plain_step
    output, grad_images, grad_in, grad_out, dense = step(
        rows, back, held_row, held_col, w_qkv, w_proj, router, w_in, w_out,
        gain_one[None], gain_two[None],
    )
    cube = (img_count, SEQ_PAD, width)
    dense = dense.astype(F32)
    grads = dense[:, : 2 * local].reshape(4, local, width)
    return (
        output.reshape(cube)[:, :seq_len],
        grad_images.reshape(cube)[:, :seq_len],
        grads[:3].transpose(0, 2, 1),
        grads[3],
        dense[0, 2 * local : 2 * local + SPECIALIST_TOTAL].T,
        grad_in.astype(F32),
        grad_out.astype(F32),
        dense[1, 2 * local],
        dense[0, 2 * local + 8],
        kept_pairs.reshape(img_count, seq_len, TOPK),
    )


def solution(mesh):
    return jax.shard_map(
        per_device,
        mesh=mesh,
        in_specs=(
            P("dp", None, None),
            P(None, None, "tensor"),
            P("tensor", None),
            P(),
            P(None, None, "tensor"),
            P(None, "tensor", None),
            P(),
            P(),
            P("dp", None, None),
            P("dp", None),
            P("dp"),
            P("dp", None, None),
        ),
        out_specs=(
            P("dp", None, None),
            P("dp", None, None),
            P(None, None, "tensor"),
            P("tensor", None),
            P(),
            P(None, None, "tensor"),
            P(None, "tensor", None),
            P(),
            P(),
            P("dp", None, None),
        ),
        check_vma=False,
    )
```

```python
import functools

import jax
import jax.numpy as jnp
from jax import lax
from jax.experimental import pallas as pl
from jax.experimental.pallas import tpu as pltpu
from jax.sharding import PartitionSpec as P

HD = 64
SPECIALIST_TOTAL = 4
TOPK = 2
SEQ = 197
SEQ_PAD = 208
CAP = 616
CAP_PAD = 640
TILE = 320
PAIRED = SPECIALIST_TOTAL // 2
LANES = 128
PIECE = 128
RING = 6
LAG = 2
DENSE_CUTS = ((0, 96), (96, 96), (192, 96), (288, 96), (384, 16))
DENSE_HALF = 400


EPSILON = 1e-06
SCALE = 0.125
BF = jnp.bfloat16
F32 = jnp.float32
MESH = pl.DeviceIdType.MESH
VMEM_LIMIT = 62 * 2**20


def dot(left, right, left_dim=1, right_dim=0):
    return lax.dot_general(
        left, right, (((left_dim,), (right_dim,)), ((), ())), preferred_element_type=F32
    )


def lane_ids(shape):
    return lax.broadcasted_iota(jnp.int32, shape, len(shape) - 1)


def standardize(rows):
    center = jnp.mean(rows, axis=-1, keepdims=True)
    centred = rows - center
    spread = jnp.mean(centred * centred, axis=-1, keepdims=True)
    root = lax.rsqrt(spread + EPSILON)
    return centred * root, root


def norm_back(grad, plain, root, gain):
    grad = grad * gain
    first = jnp.mean(grad, axis=-1, keepdims=True)
    second = jnp.mean(grad * plain, axis=-1, keepdims=True)
    return root * (grad - first - plain * second)


def route_slots(routes_g, order_g, count_g):
    tokens = routes_g.shape[0]
    positions = jnp.arange(tokens, dtype=jnp.int32)
    in_image = (positions // SEQ < count_g).astype(jnp.int32)
    capacity_now = (5 * TOPK * count_g * SEQ + 4 * SPECIALIST_TOTAL - 1) // (4 * SPECIALIST_TOTAL)
    spots = order_g[:, None] == positions[None, :]
    place = jnp.sum(jnp.where(spots, positions[:, None], 0), axis=0)
    earlier = (place[None, :] < place[:, None]).astype(BF)
    experts = jnp.arange(SPECIALIST_TOTAL, dtype=jnp.int32)
    marks = (routes_g[:, :, None] == experts).astype(jnp.int32) * in_image[:, None, None]
    marks = marks.reshape(tokens, TOPK * SPECIALIST_TOTAL)
    before = jnp.dot(earlier, marks.astype(BF), preferred_element_type=F32)
    before = before.reshape(tokens, TOPK, SPECIALIST_TOTAL).astype(jnp.int32)
    marks = marks.reshape(tokens, TOPK, SPECIALIST_TOTAL)
    first_total = jnp.sum(marks[:, 0, :], axis=0)
    before = before + jnp.stack([jnp.zeros_like(first_total), first_total])[None]
    slot_of = jnp.sum(before * marks, axis=-1)
    kept_pairs = in_image[:, None] * (slot_of < capacity_now).astype(jnp.int32)
    held = jnp.max(jnp.where((marks * kept_pairs[:, :, None]) > 0, before, -1), axis=1)
    return (held, kept_pairs)


def pair_sum(partial):
    n_t = lax.axis_size("tensor")
    core = lax.axis_index("tensor") % 2
    half = partial.shape[-1] // 2
    other = [(i, i ^ 1) for i in range(n_t)]
    mine = lax.dynamic_slice_in_dim(partial, core * half, half, partial.ndim - 1)
    gone = lax.dynamic_slice_in_dim(partial, (1 - core) * half, half, partial.ndim - 1)
    got = lax.ppermute(gone, "tensor", other)
    total = (mine.astype(F32) + got.astype(F32)).astype(BF)
    step = 2
    while step < n_t:
        got = lax.ppermute(total, "tensor", [(i, i ^ step) for i in range(n_t)])
        total = (total.astype(F32) + got.astype(F32)).astype(BF)
        step *= 2
    back = lax.ppermute(total, "tensor", other)
    return jnp.where(
        core == 0,
        jnp.concatenate([total, back], axis=-1),
        jnp.concatenate([back, total], axis=-1),
    )


def head_mask(shape, head):
    return lane_ids(shape) // HD == head


def image_rows(i):
    return pl.ds(pl.multiple_of(i * SEQ_PAD, 16), SEQ_PAD)


def attend(query, key, head):
    alone = jnp.where(head_mask(query.shape, head), query, jnp.zeros_like(query))
    scores = dot(alone, key, 1, 1) * SCALE
    scores = jnp.where(lane_ids(scores.shape) < SEQ, scores, -jnp.inf)
    powers = jnp.exp(scores - jnp.max(scores, axis=-1, keepdims=True))
    return powers / jnp.sum(powers, axis=-1, keepdims=True)


def attention_image(i, images, w_qkv, w_proj, gain, partial, qkv, mixed):
    at = image_rows(i)
    plain, _ = standardize(images[at, :].astype(F32))
    normed = (plain * gain[...]).astype(BF)
    for s in range(3):
        qkv[s, at, :] = dot(normed, w_qkv[s], 1, 1).astype(BF)
    query, key, value = (qkv[s, at, :] for s in range(3))
    result = jnp.zeros(query.shape, F32)
    for head in range(query.shape[1] // HD):
        weights = attend(query, key, head).astype(BF)
        result = jnp.where(head_mask(query.shape, head), dot(weights, value), result)
    result = result.astype(BF)
    mixed[at, :] = result
    partial[at, :] = dot(result, w_proj[...]).astype(BF)


def softmax_of(logits, axis):
    ids = lax.broadcasted_iota(jnp.int32, logits.shape, axis)
    logits = jnp.where(ids < SPECIALIST_TOTAL, logits, -jnp.inf)
    powers = jnp.exp(logits - jnp.max(logits, axis=axis, keepdims=True))
    return powers / jnp.sum(powers, axis=axis, keepdims=True)


def second_norm_image(i, images, attended, gain, normed):
    at = image_rows(i)
    plain, _ = standardize(images[at, :].astype(F32) + attended[at, :].astype(F32))
    normed[at, :] = (plain * gain[...]).astype(BF)


def gelu_both(rows):
    inner = 0.7978845608028654 * (rows + 0.044715 * rows * rows * rows)
    curve = jnp.tanh(inner)
    half = 0.5 * (1.0 + curve)
    slope = half + 0.5 * rows * (1.0 - curve * curve) * (
        0.7978845608028654 * (1.0 + 3.0 * 0.044715 * rows * rows)
    )
    return rows * half, slope


def expert_rows(expert, tokens, back, held, gates, w_in, w_out, factors, offset, sent, tick):
    width = tokens.shape[1]
    row = held[pl.ds(expert, 1), :]
    gate = gates[pl.ds(expert, 1), :]

    def tile(i, carry):
        ids = lax.broadcasted_iota(jnp.int32, (TILE, row.shape[1]), 0) + i * TILE
        hit = ids == row
        pick = jnp.where(hit, 1.0, 0.0).astype(BF)
        scale = jnp.sum(jnp.where(hit, gate, 0.0), axis=1, keepdims=True)
        buffer = dot(pick, tokens[...]).astype(BF)
        raw = dot(pick, back[...])
        grad = (scale * raw).astype(BF)
        value, slope = gelu_both(dot(buffer, w_in[...]))
        value = value.astype(BF)
        delta = (dot(grad, w_out[...], 1, 1) * slope).astype(BF)
        if factors is not None:
            at = pl.ds(pl.multiple_of(offset + i * TILE, 16), TILE)
            for ref, rows in zip(factors, (buffer, delta, value, grad)):
                ref[at, :] = rows
        if sent is not None:
            at = pl.ds(pl.multiple_of(i * TILE, 16), TILE)
            out = dot(value, w_out[...]).astype(BF).astype(F32)
            share = jnp.sum(out * raw, axis=1, keepdims=True)
            sent[at, :width] = (scale * out).astype(BF)
            sent[at, width : 2 * width] = dot(delta, w_in[...], 1, 1).astype(BF)
            lane = lane_ids((TILE, LANES)) == expert
            sent[at, 2 * width :] = jnp.where(lane, share, 0.0).astype(BF)
        if tick is not None:
            tick(i)
        return carry

    lax.fori_loop(0, CAP_PAD // TILE, tile, 0)


def return_rows(expert, held_col, sent, total, fresh, final, after, first=0, stop=None):
    def image(i, carry):
        at = image_rows(i)
        column = held_col[at, :]
        column = jnp.sum(
            jnp.where(lane_ids(column.shape) == expert, column, 0), axis=1, keepdims=True
        )
        pick = jnp.where(lane_ids((SEQ_PAD, CAP_PAD)) == column, 1.0, 0.0).astype(BF)
        back = dot(pick, sent[...])
        if final is None:
            total[at, :] = back if fresh else total[at, :] + back
        else:
            back = back + total[at, :]
            start = 0
            for ref in final:
                ref[at, :] = back[:, start : start + ref.shape[1]].astype(BF)
                start += ref.shape[1]
        if after is not None:
            after(i)
        return carry

    lax.fori_loop(first, stop or total.shape[0] // SEQ_PAD, image, 0)


def weight_rows(left, right, final, start, after):
    def step(i, carry):
        rows = pl.ds(pl.multiple_of(i * 256, 256), 256)
        to = pl.ds(pl.multiple_of(start + i * 256, 256), 256)
        final[to, :] = dot(left[:, rows], right[...], 0, 0).astype(BF)
        if after is not None:
            after(i)
        return carry

    lax.fori_loop(0, left.shape[1] // 256, step, 0)


def backward_image(
    i, images, attended, cotangent, sums, gate_sums, qkv, mixed, w_qkv, w_proj, w_router,
    gain_one, gain_two, partial, grad_hidden, grad_dense, grad_small,
):
    width = images.shape[1]
    at = image_rows(i)
    router = w_router[...]
    rows = images[at, :].astype(F32)
    plain, root = standardize(rows + attended[at, :].astype(F32))
    normed = (plain * gain_two[...]).astype(BF)
    gates = softmax_of(dot(normed, router, 1, 1), 1)
    grad_gates = gate_sums[at, :].astype(F32)[:, :8]
    grad_logits = gates * (grad_gates - jnp.sum(gates * grad_gates, axis=-1, keepdims=True))
    high = grad_logits.astype(BF)
    low = (grad_logits - high.astype(F32)).astype(BF)
    delta = sums[at, :].astype(F32) + (dot(high, router) + dot(low, router))
    grad_small[0:8, :] += dot(high, normed, 0, 0) + dot(low, normed, 0, 0)
    grad_small[8:9, :] += jnp.sum(delta * plain, axis=0, keepdims=True)
    grad = cotangent[at, :].astype(F32) + norm_back(delta, plain, root, gain_two[...])
    grad_hidden[at, :width] = grad
    grad = grad.astype(BF)
    grad_dense[3] += dot(mixed[at, :], grad, 0, 0)
    grad_mixed = dot(grad, w_proj[...], 1, 1).astype(BF)
    query, key, value = (qkv[s, at, :] for s in range(3))
    parts = [jnp.zeros(query.shape, F32) for _ in range(3)]
    for head in range(query.shape[1] // HD):
        mask = head_mask(query.shape, head)
        weights = attend(query, key, head)
        alone = jnp.where(mask, grad_mixed, jnp.zeros_like(grad_mixed))
        grad_weights = dot(alone, value, 1, 1)
        center = jnp.sum(weights * grad_weights, axis=-1, keepdims=True)
        scores = (weights * (grad_weights - center)).astype(BF)
        parts[0] = jnp.where(mask, dot(scores, key) * SCALE, parts[0])
        parts[1] = jnp.where(mask, dot(scores, query, 0, 0) * SCALE, parts[1])
        parts[2] = jnp.where(mask, dot(weights.astype(BF), grad_mixed, 0, 0), parts[2])
    first, _ = standardize(rows)
    first = (first * gain_one[...]).astype(BF)
    back = jnp.zeros((SEQ_PAD, width), F32)
    for s in range(3):
        part = parts[s].astype(BF)
        grad_dense[s] += dot(part, first, 0, 0)
        back = back + dot(part, w_qkv[s])
    partial[at, :] = back.astype(BF)


def output_image(i, images, attended, moe, output):
    at = image_rows(i)
    hidden = images[at, :].astype(F32) + attended[at, :].astype(F32)
    output[at, :] = (hidden + moe[at, :].astype(F32)).astype(BF)


def last_image(i, images, sums, grad_hidden, gain, grad_images, start, grad_gain):
    width = images.shape[1]
    at = image_rows(i)
    plain, root = standardize(images[at, :].astype(F32))
    delta = sums[at, :].astype(F32)
    grad_gain[0:1, :] += jnp.sum(delta * plain, axis=0, keepdims=True)
    grad = grad_hidden[at, :width] + norm_back(delta, plain, root, gain[...])
    grad_images[at, start : start + width] = grad


def loop(count, body):
    def step(i, carry):
        body(i)
        return carry

    lax.fori_loop(0, count, step, 0)


def attention_kernel(images, w_qkv, w_proj, gain, partial, qkv, mixed):
    loop(
        images.shape[0] // SEQ_PAD,
        lambda i: attention_image(i, images, w_qkv, w_proj, gain, partial, qkv, mixed),
    )


def second_norm_kernel(images, attended, gain, normed):
    loop(
        images.shape[0] // SEQ_PAD, lambda i: second_norm_image(i, images, attended, gain, normed)
    )


def expert_kernel(
    tokens, tokens_pair, back, back_pair, held, held_pair, held_col, w_router, w_in, w_out,
    moe, sums, gate_sums, main,
    gates, gates_pair, slots, inner, active, grads, sent, total,
):
    x = lax.rem(lax.axis_index("dp"), 2)
    gates[...] = softmax_of(dot(w_router[...], tokens[...], 1, 1), 0)
    gates_pair[...] = softmax_of(dot(w_router[...], tokens_pair[...], 1, 1), 0)
    width = tokens.shape[1]
    factors = (slots, inner, active, grads)
    for k in range(SPECIALIST_TOTAL):
        expert = lax.rem(x + k // PAIRED, 2) * PAIRED + k % PAIRED
        weights = (w_in.at[expert], w_out.at[expert])
        mine = factors if k < PAIRED else None
        expert_rows(expert, tokens, back, held, gates, *weights, mine, 0, sent, None)
        final = (moe, sums, gate_sums) if k == SPECIALIST_TOTAL - 1 else None
        return_rows(expert, held_col, sent, total, k == 0, final, None)
        if k < PAIRED:
            expert_rows(
                expert, tokens_pair, back_pair, held_pair, gates_pair, *weights, mine, CAP_PAD, None, None
            )
            weight_rows(slots, inner, main, 2 * k * width, None)
            weight_rows(active, grads, main, (2 * k + 1) * width, None)


def backward_kernel(
    images, attended, cotangent, moe, sums, gate_sums, qkv, mixed, w_qkv, w_proj, w_router,
    gain_one, gain_two,
    output, partial, grad_hidden, grad_dense, grad_small,
):
    grad_dense[...] = jnp.zeros_like(grad_dense)
    grad_small[...] = jnp.zeros_like(grad_small)

    def image(i):
        backward_image(
            i, images, attended, cotangent, sums, gate_sums, qkv, mixed, w_qkv, w_proj, w_router,
            gain_one, gain_two, partial, grad_hidden, grad_dense, grad_small,
        )
        output_image(i, images, attended, moe, output)

    loop(images.shape[0] // SEQ_PAD, image)


def last_kernel(images, sums, grad_hidden, gain, grad_images, grad_gain):
    grad_gain[...] = jnp.zeros_like(grad_gain)
    loop(
        images.shape[0] // SEQ_PAD,
        lambda i: last_image(i, images, sums, grad_hidden, gain, grad_images, 0, grad_gain),
    )


def call(kernel, outs, scratch, *args, flops=0):
    vmem = pl.BlockSpec(memory_space=pltpu.VMEM)
    return pl.pallas_call(
        kernel,
        out_shape=tuple(jax.ShapeDtypeStruct(shape, kind) for shape, kind in outs),
        in_specs=[vmem] * len(args),
        out_specs=tuple(vmem for _ in outs),
        scratch_shapes=[pltpu.VMEM(shape, kind) for shape, kind in scratch],
        compiler_params=pltpu.CompilerParams(vmem_limit_bytes=VMEM_LIMIT),
        cost_estimate=pl.CostEstimate(flops=flops, bytes_accessed=10**7, transcendentals=0),
    )(*args)


def swap_sum(main, dense):
    n_dp = lax.axis_size("dp")
    x = lax.axis_index("dp") % 2

    def swap(value, step):
        return lax.ppermute(value, "dp", [(i, i ^ step) for i in range(n_dp)])

    gone = lax.dynamic_index_in_dim(dense, 1 - x, 0, keepdims=False)
    mine = lax.dynamic_index_in_dim(dense, x, 0, keepdims=False)
    joined = (mine.astype(F32) + swap(gone, 1).astype(F32)).astype(BF)
    total = jnp.concatenate([main, joined], axis=0)
    step = 2
    while step < n_dp:
        total = (total.astype(F32) + swap(total, step).astype(F32)).astype(BF)
        step *= 2
    other = swap(total, 1)
    return jnp.where(x == 0, jnp.stack([total, other]), jnp.stack([other, total]))


def plain_step(rows, back, held_row, held_col, w_qkv, w_proj, router, w_in, w_out, gain_one, gain_two):
    padded, width = rows.shape
    local = w_proj.shape[0]
    router = jnp.pad(router, ((0, 8 - SPECIALIST_TOTAL), (0, 0)))
    n_dp = lax.axis_size("dp")
    swap = [(i, i ^ 1) for i in range(n_dp)]
    flat = (padded, width)
    held_pair = lax.ppermute(held_row, "dp", swap)
    back_pair = lax.ppermute(back, "dp", swap)
    partial, qkv, mixed = call(
        attention_kernel,
        [(flat, BF), ((3, padded, local), BF), ((padded, local), BF)],
        [],
        rows, w_qkv, w_proj, gain_one,
    )
    attended = pair_sum(partial)
    (normed,) = call(second_norm_kernel, [(flat, BF)], [], rows, attended, gain_two)
    normed_pair = lax.ppermute(normed, "dp", swap)
    wide = 2 * width + LANES
    moe, sums, gate_sums, main = call(
        expert_kernel,
        [(flat, BF), (flat, BF), ((padded, LANES), BF), ((4 * width, width), BF)],
        [((8, padded), F32)] * 2
        + [((2 * CAP_PAD, width), BF)] * 4
        + [((CAP_PAD, wide), BF), ((padded, wide), F32)],
        normed, normed_pair, back, back_pair,
        held_row, held_pair, held_col, router, w_in, w_out,
    )
    moe = pair_sum(moe)
    sums = pair_sum(sums)
    gate_sums = pair_sum(jnp.concatenate([gate_sums, gate_sums], axis=-1))[:, :LANES]
    output, partial, grad_hidden, grad_dense, grad_small = call(
        backward_kernel,
        [(flat, BF), (flat, BF), (flat, F32), ((4, local, width), F32), ((16, width), F32)],
        [],
        rows, attended, back, moe, sums, gate_sums,
        qkv, mixed, w_qkv, w_proj, router, gain_one, gain_two,
    )
    grad_images, grad_gain = call(
        last_kernel,
        [(flat, F32), ((8, width), F32)],
        [],
        rows, pair_sum(partial), grad_hidden, gain_one,
    )
    dense = grad_dense.reshape(2, 2 * local, width)
    small = jnp.stack([grad_small, jnp.pad(grad_gain, ((0, 8), (0, 0)))])
    dense = jnp.concatenate([dense, small], axis=1).astype(BF)
    whole = swap_sum(main, dense)
    rows_main = main.shape[0]
    experts = whole[:, :rows_main].reshape(SPECIALIST_TOTAL, 2, width, width)
    grads = whole[:, rows_main : rows_main + 2 * local].reshape(4, local, width)
    small = whole[:, rows_main + 2 * local :]
    return output, grad_images, experts[:, 0], experts[:, 1], grads, small


(
    ATT_RS, ATT_Y, ATT_AG, Z_X, Z_CORE, D_RS, G_RS, D_Y, G_Y, D_AG,
    O_RS, O_Y, O_AG, B_RS, B_Y, B_AG, COT, COT_Y, COT_CORE, DENSE, HELD,
) = range(21)


def step_kernel(
    images, cotangent, held, held_col, w_qkv, w_proj, vectors, w_in, w_out,
    output, grad_images, out_in, out_out, out_grads, out_small,
    held_pair, router, back_pair, tokens, tokens_pair, attended, partial, qkv, mixed,
    core_a, far_a, core_d, far_d, core_o, far_o, core_g, far_g, gate_part, gate_sum,
    gates, gates_pair, slots, inner, active, grads, sent, total, slot_in, slot_out,
    grad_dense, grad_small, grad_last, main, landed, middle_ring, dense_x,
    sends, recvs, weight_sems, send_low, recv_low, send_mid, recv_mid, send_down, recv_down,
    send_pair, recv_pair, keep, out_sems,
):
    place = lax.axis_index("dp")
    spot = lax.axis_index("tensor")
    x = lax.rem(place, 2)
    z = place // 2
    c = lax.rem(spot, 2)
    y = spot // 2
    inside = jnp.logical_or(z == 1, z == 2)
    outside = jnp.logical_not(inside)
    core = {"tensor": spot + 1 - 2 * c}
    far = {"tensor": spot + 2 - 4 * y}
    pair = {"dp": place + 1 - 2 * x}
    line = {"dp": (z + 1 - 2 * lax.rem(z, 2)) * 2 + x}
    middle = {"dp": (3 - z) * 2 + x}
    width = images.shape[1]
    half = width // 2
    count = images.shape[0] // SEQ_PAD
    pieces = main.shape[0] // PIECE
    per_expert = 2 * width // PIECE
    mine = pl.ds(pl.multiple_of(c * half, LANES), half)
    other = pl.ds(pl.multiple_of((1 - c) * half, LANES), half)
    local = w_proj.shape[0]
    gain_one, gain_two = vectors.at[0:1], vectors.at[1:2]
    dense = active
    dense_landed, dense_middle = inner.at[:DENSE_HALF], inner.at[DENSE_HALF : 2 * DENSE_HALF]

    barrier = pltpu.get_barrier_semaphore()
    for peer in (core, far, pair, line):
        pl.semaphore_signal(barrier, inc=1, device_id=peer, device_id_type=MESH)

    @pl.when(inside)
    def _():
        pl.semaphore_signal(barrier, inc=1, device_id=middle, device_id_type=MESH)

    def load(k):
        expert = lax.rem(x + k // PAIRED, 2) * PAIRED + k % PAIRED
        return [
            pltpu.make_async_copy(w_in.at[expert], slot_in.at[k % 2], weight_sems.at[0, k % 2]),
            pltpu.make_async_copy(w_out.at[expert], slot_out.at[k % 2], weight_sems.at[1, k % 2]),
        ]

    for k in range(2):
        for copy in load(k):
            copy.start()
    router[...] = vectors[8:16, :].astype(BF)
    grad_dense[...] = jnp.zeros_like(grad_dense)
    grad_small[...] = jnp.zeros_like(grad_small)
    grad_last[...] = jnp.zeros_like(grad_last)

    @pl.when(inside)
    def _():
        pl.semaphore_wait(barrier, 5)

    @pl.when(outside)
    def _():
        pl.semaphore_wait(barrier, 4)

    def remote(src, dst, send, recv, peer):
        return pltpu.make_async_remote_copy(
            src_ref=src, dst_ref=dst, send_sem=send, recv_sem=recv,
            device_id=peer, device_id_type=MESH,
        )

    def channel(k, i, src, dst, peer):
        return remote(src, dst, sends.at[k, i], recvs.at[k, i], peer)

    def rs_copy(k, i, part, got):
        return channel(k, i, part.at[image_rows(i), other], got.at[image_rows(i), :], core)

    def far_copy(k, i, part, got):
        return channel(k, i, part.at[image_rows(i), mine], got.at[image_rows(i), :], far)

    def give_copy(k, i, result):
        view = result.at[image_rows(i), mine]
        return channel(k, i, view, view, core)

    def join_core(ks, i, part, near, got):
        at = image_rows(i)
        rs_copy(ks[0], i, part, near).wait_recv()
        rows = part[at, mine].astype(F32) + near[at, :].astype(F32)
        part[at, mine] = rows.astype(BF)
        far_copy(ks[1], i, part, got).start()

    def join_far(ks, i, part, got, result):
        at = image_rows(i)
        far_copy(ks[1], i, part, got).wait_recv()
        rows = part[at, mine].astype(F32) + got[at, :].astype(F32)
        result[at, mine] = rows.astype(BF)
        give_copy(ks[2], i, result).start()

    def sent_all(ks, part, near, got, result):
        def wait(i):
            rs_copy(ks[0], i, part, near).wait_send()
            far_copy(ks[1], i, part, got).wait_send()
            give_copy(ks[2], i, result).wait_send()

        loop(count, wait)

    def staged(step, lag, body):
        i = step - lag
        if isinstance(i, int):
            if 0 <= i < count:
                body(i)
            return

        @pl.when(jnp.logical_and(i >= 0, i < count))
        def _():
            body(i)

    held_copy = channel(HELD, 0, held, held_pair, pair)
    held_copy.start()

    def cot_copy(i):
        at = image_rows(i)
        return channel(COT, i, cotangent.at[at, mine], back_pair.at[at, mine], pair)

    def cot_far(i):
        view = back_pair.at[image_rows(i), mine]
        return channel(COT_Y, i, view, view, far)

    def cot_give(i):
        view = back_pair.at[image_rows(i), mine]
        return channel(COT_CORE, i, view, view, core)

    def shared(i):
        return i < count - 1

    def direct(i):
        return jnp.logical_or(lax.rem(i, 2) == y, i == count - 1)

    def cot_send(i):
        @pl.when(direct(i))
        def _():
            cot_copy(i).start()

    def cot_pass(i):
        @pl.when(direct(i))
        def _():
            cot_copy(i).wait()
            cot_give(i).start()

            @pl.when(shared(i))
            def _():
                cot_far(i).start()

    def cot_land(i):
        @pl.when(jnp.logical_not(direct(i)))
        def _():
            cot_far(i).wait_recv()
            cot_give(i).start()

    def cot_end(i):
        cot_give(i).wait()

        @pl.when(jnp.logical_and(direct(i), shared(i)))
        def _():
            cot_far(i).wait_send()

    loop(count, cot_send)

    att = (ATT_RS, ATT_Y, ATT_AG)

    def token_copy(i):
        at = image_rows(i)
        return channel(Z_X, i, tokens.at[at, mine], tokens_pair.at[at, mine], pair)

    def token_give(i):
        view = tokens_pair.at[image_rows(i), mine]
        return channel(Z_CORE, i, view, view, core)

    def attention_step(step):
        def first(i):
            attention_image(i, images, w_qkv, w_proj, gain_one, partial, qkv, mixed)
            rs_copy(ATT_RS, i, partial, core_a).start()

        def norm(i):
            give_copy(ATT_AG, i, attended).wait_recv()
            second_norm_image(i, images, attended, gain_two, tokens)
            token_copy(i).start()

        staged(step, 0, first)
        staged(step, 1, lambda i: join_core(att, i, partial, core_a, far_a))
        staged(step, 2, lambda i: join_far(att, i, partial, far_a, attended))
        staged(step, 3, norm)

        @pl.when(step == count + 1)
        def _():
            loop(count, cot_pass)

    loop(count + 3, attention_step)
    gates[...] = softmax_of(dot(router[...], tokens[...], 1, 1), 0)

    def dense_half(side):
        return pl.ds(pl.multiple_of(side * DENSE_HALF, 16), DENSE_HALF)

    def piece(n):
        if isinstance(n, int) and n >= pieces:
            start, size = DENSE_CUTS[n - pieces]
            at = pl.ds(start, size)
            views = [ref.at[at, :] for ref in (dense.at[dense_half(x)], dense_landed, dense_middle)]
            if size == 16:
                return views + [out_small.at[x]]
            at = pl.ds(start % local, size)
            return views + [out_grads.at[2 * x + start // local, at, :]]
        at = pl.ds(pl.multiple_of(n * PIECE, PIECE), PIECE)
        return [main.at[at, :], landed.at[at, :], middle_ring.at[lax.rem(n, RING)], None]

    def out_views(n):
        if isinstance(n, int) and n >= pieces:
            return [(None, piece(n)[3])]
        per_kind = width // PIECE
        expert = x * PAIRED + n // per_expert
        kind = lax.rem(n // per_kind, 2)
        at = pl.ds(pl.multiple_of(lax.rem(n, per_kind) * PIECE, PIECE), PIECE)
        return [(kind == 0, out_in.at[expert, at, :]), (kind == 1, out_out.at[expert, at, :])]

    def low_copy(n):
        own, got, _, _ = piece(n)
        return remote(own, got, send_low.at[n], recv_low.at[n], line)

    def mid_copy(n):
        own, _, got, _ = piece(n)
        return remote(own, got, send_mid.at[n], recv_mid.at[n], middle)

    def down_copy(n):
        _, done, _, _ = piece(n)
        return remote(done, done, send_down.at[n], recv_down.at[n], line)

    def each_out(n, act):
        done = piece(n)[1]
        for when, view in out_views(n):
            copies = (
                remote(done, view, send_pair.at[n], recv_pair.at[n], pair),
                pltpu.make_async_copy(done, view, keep.at[n]),
            )
            if when is None:
                act(*copies)
            else:
                pl.when(when)(functools.partial(act, *copies))

    def publish(n):
        def act(swap, own):
            swap.start()
            own.start()

        each_out(n, act)

    def add_piece(to, left, right):
        rows = to.shape[0]
        size = 64 if rows % 64 == 0 else 48 if rows % 48 == 0 else 16

        def add(i):
            at = pl.ds(pl.multiple_of(i * size, 16), size)
            to[at, :] = (left[at, :].astype(F32) + right[at, :].astype(F32)).astype(BF)

        loop(rows // size, add)

    last = pieces + len(DENSE_CUTS)

    def tick(n):
        def when(n, body):
            if isinstance(n, int):
                if 0 <= n < last:
                    body(n)
            else:
                pl.when(n >= 0)(functools.partial(body, n))

        def gather(n):
            own, got, _, _ = piece(n)
            low_copy(n).wait_recv()
            add_piece(own, own, got)
            mid_copy(n).start()

        def finish(n):
            own, done, got, _ = piece(n)
            mid_copy(n).wait_recv()
            add_piece(done, own, got)
            down_copy(n).start()
            publish(n)

        def forward(n):
            down_copy(n).wait_recv()
            publish(n)

        @pl.when(inside)
        def _():
            when(n, gather)
            when(n - LAG, finish)

        @pl.when(outside)
        def _():
            when(n - 2 * LAG, forward)

    def lift(n):
        @pl.when(outside)
        def _():
            low_copy(n).start()

    factors = (slots, inner, active, grads)
    turn = 0
    final = (grads.at[: count * SEQ_PAD], slots.at[: count * SEQ_PAD], gate_part)
    moe_part, sum_part, _ = final
    dee = (D_RS, D_Y, D_AG)
    oh = (O_RS, O_Y, O_AG)
    moe, sums = tokens_pair, back_pair

    def gate_near(i):
        at = image_rows(i)
        return channel(G_RS, i, gate_part.at[at, :], core_g.at[at, :], core)

    def gate_far(i):
        at = image_rows(i)
        return channel(G_Y, i, gate_sum.at[at, :], far_g.at[at, :], far)

    def send_parts(i):
        rs_copy(D_RS, i, sum_part, core_d).start()
        gate_near(i).start()
        rs_copy(O_RS, i, moe_part, core_o).start()

    for k in range(SPECIALIST_TOTAL):
        expert = lax.rem(x + k // PAIRED, 2) * PAIRED + k % PAIRED
        weights = (slot_in.at[k % 2], slot_out.at[k % 2])
        for copy in load(k):
            copy.wait()
        kept = factors if k < PAIRED else None
        base = turn
        expert_rows(
            expert, tokens, cotangent, held, gates, *weights, kept, 0, sent,
            (lambda i, base=base: tick(base + i)) if k else None,
        )
        if k:
            turn += 2
        ends = k == SPECIALIST_TOTAL - 1
        if k == 0:

            def give(i):
                token_copy(i).wait_recv()
                token_give(i).start()

            loop(count, give)
            loop(count, cot_land)
            return_rows(expert, held_col, sent, total, True, None, None, 0, 2)
            loop(count, lambda i: token_give(i).wait_recv())
            loop(count, cot_end)
            held_copy.wait()
            gates_pair[...] = softmax_of(dot(router[...], tokens_pair[...], 1, 1), 0)
        else:
            return_rows(
                expert, held_col, sent, total, False, final if ends else None,
                send_parts if ends else None,
            )
            tick(turn)
            turn += 1
        if k < PAIRED:
            base = turn
            expert_rows(
                expert, tokens_pair, back_pair, held_pair, gates_pair, *weights, kept, CAP_PAD, None,
                (lambda i, base=base: tick(base + i)) if k else None,
            )
            if k:
                turn += 2
            for copy in load(k + 2):
                copy.start()
            per_step = 256 // PIECE
            for kind, (left, right) in enumerate(((slots, inner), (active, grads))):
                first = k * per_expert + kind * (width // PIECE)

                def after(i, first=first):
                    for j in range(per_step):
                        lift(first + i * per_step + j)

                weight_rows(left, right, main, (2 * k + kind) * width, after)
            if k == 0:
                return_rows(expert, held_col, sent, total, True, None, None, 2)
                tick(turn)
                turn += 1
        if k == PAIRED - 1:

            def tokens_sent(i):
                token_copy(i).wait_send()
                token_give(i).wait_send()

            loop(count, tokens_sent)
            sent_all(att, partial, core_a, far_a, attended)

    bee = (B_RS, B_Y, B_AG)

    def backward_step(step):
        def gates_core(i):
            join_core(dee, i, sum_part, core_d, far_d)
            at = image_rows(i)
            gate_near(i).wait_recv()
            rows = gate_part[at, :].astype(F32) + core_g[at, :].astype(F32)
            gate_sum[at, :] = rows.astype(BF)
            gate_far(i).start()

        def gates_all(i):
            join_far(dee, i, sum_part, far_d, sums)
            at = image_rows(i)
            gate_far(i).wait()
            rows = gate_sum[at, :].astype(F32) + far_g[at, :].astype(F32)
            gate_sum[at, :] = rows.astype(BF)

        def back(i):
            give_copy(D_AG, i, sums).wait()
            backward_image(
                i, images, attended, cotangent, sums, gate_sum, qkv, mixed, w_qkv, w_proj, router,
                gain_one, gain_two, partial, total, grad_dense, grad_small,
            )
            rs_copy(B_RS, i, partial, core_a).start()

        staged(step, 0, gates_core)
        staged(step, 1, gates_all)
        staged(step, 2, back)
        staged(step, 3, lambda i: join_core(bee, i, partial, core_a, far_a))
        staged(step, 4, lambda i: join_far(bee, i, partial, far_a, sums))
        staged(step, 5, finish)

    def grads_out(i):
        at = image_rows(i)
        return pltpu.make_async_copy(
            total.at[at, pl.ds(width, width)], grad_images.at[at, :], out_sems.at[0, i]
        )

    def rows_out(i):
        at = image_rows(i)
        return pltpu.make_async_copy(moe.at[at, :], output.at[at, :], out_sems.at[1, i])

    def finish(i):
        give_copy(B_AG, i, sums).wait_recv()
        last_image(i, images, sums, total, gain_one, total, width, grad_last)
        grads_out(i).start()

    def emit(i):
        give_copy(O_AG, i, moe).wait()
        output_image(i, images, attended, moe, moe)
        rows_out(i).start()

    base = turn

    def backward_turn(step):
        turns = base + step + jnp.maximum(step - 2, 0)
        tick(turns)
        backward_step(step)

        @pl.when(step >= 2)
        def _():
            tick(turns + 1)

    loop(count + 2, backward_turn)
    turn += 2 * count + 2

    def pack(i):
        start = i // 2 * DENSE_HALF + lax.rem(i, 2) * local
        dense[pl.ds(pl.multiple_of(start, 16), local), :] = grad_dense[i].astype(BF)

    def dense_view(i, side=0):
        start, size = DENSE_CUTS[i]
        return pl.ds(pl.multiple_of(side * DENSE_HALF + start, 16), size)

    def dense_copy(i):
        at = dense_view(i)
        return channel(DENSE, i, dense.at[dense_view(i, 1 - x), :], dense_x.at[at, :], pair)

    def dense_join(i):
        at = dense_view(i)
        dense_copy(i).wait()
        own = dense_view(i, x)
        dense[own, :] = (dense[own, :].astype(F32) + dense_x[at, :].astype(F32)).astype(BF)
        lift(pieces + i)

    small = len(DENSE_CUTS) - 1
    loop(4, pack)
    for i in range(small):
        dense_copy(i).start()
    join_core(bee, count - 1, partial, core_a, far_a)
    loop(count, lambda i: join_core(oh, i, moe_part, core_o, far_o))
    while turn < pieces:
        tick(turn)
        turn += 1
    for i in range(count - 2, count):
        join_far(bee, i, partial, far_a, sums)
        finish(i - 1)
    finish(count - 1)
    for side, rows in enumerate((grad_small, grad_last)):
        dense[dense_view(small, side), :] = rows[...].astype(BF)
    dense_copy(small).start()
    for i in range(len(DENSE_CUTS)):
        dense_join(i)
        tick(turn)
        turn += 1
        join_far(oh, i, moe_part, far_o, moe)
        if i:
            emit(i - 1)
    emit(count - 1)
    while turn < last + 2 * LAG:
        tick(turn)
        turn += 1

    def rest(i):
        rs_copy(D_RS, i, sum_part, core_d).wait_send()
        far_copy(D_Y, i, sum_part, far_d).wait_send()
        gate_near(i).wait_send()
        rs_copy(O_RS, i, moe_part, core_o).wait_send()
        far_copy(O_Y, i, moe_part, far_o).wait_send()
        grads_out(i).wait()
        rows_out(i).wait()

    loop(count, rest)
    sent_all(bee, partial, core_a, far_a, sums)

    def settle(n):
        @pl.when(outside)
        def _():
            low_copy(n).wait_send()

        @pl.when(inside)
        def _():
            mid_copy(n).wait_send()
            down_copy(n).wait_send()

        def act(swap, own):
            swap.wait()
            own.wait()

        each_out(n, act)

    loop(pieces, settle)
    for n in range(pieces, last):
        settle(n)


def eight_step(rows, back, held_row, held_col, w_qkv, w_proj, router, w_in, w_out, gain_one, gain_two):
    padded, width = rows.shape
    local = w_proj.shape[0]
    count = padded // SEQ_PAD
    half = width // 2
    gap = jnp.zeros((6, width), F32)
    vectors = jnp.concatenate([gain_one, gain_two, gap, router.astype(F32), gap[:4]])
    wide = 2 * width + LANES
    pieces = 4 * width // PIECE
    last = pieces + len(DENSE_CUTS)
    vmem = pl.BlockSpec(memory_space=pltpu.VMEM)
    hbm = pl.BlockSpec(memory_space=pl.ANY)
    flat = ((padded, width), BF)
    part = ((padded, half), BF)
    thin = ((padded, LANES), BF)
    square = (width, width)
    scratch = [((8, padded), jnp.int32), ((8, width), BF)] + [flat] * 5 + [((3, padded, local), BF), ((padded, local), BF)]
    scratch += [part] * 6 + [thin] * 4
    scratch += [((8, padded), F32)] * 2 + [((2 * CAP_PAD, width), BF)] * 4
    scratch += [((CAP_PAD, wide), BF), ((padded, wide), F32), ((2, *square), BF), ((2, *square), BF)]
    scratch += [((4, local, width), F32)] + [((16, width), F32)] * 2
    scratch += [((4 * width, width), BF)] * 2 + [((RING, PIECE, width), BF)]
    scratch += [((DENSE_HALF, width), BF)]
    dma = pltpu.SemaphoreType.DMA
    sems = [dma((21, count))] * 2 + [dma((2, 2))] + [dma((last,))] * 9 + [dma((2, count))]
    outs = [(flat[0], BF), (flat[0], F32)] + [((SPECIALIST_TOTAL, *square), BF)] * 2
    outs += [((4, local, width), BF), ((2, 16, width), BF)]
    return pl.pallas_call(
        step_kernel,
        out_shape=tuple(jax.ShapeDtypeStruct(shape, kind) for shape, kind in outs),
        in_specs=[vmem] * 7 + [hbm] * 2,
        out_specs=tuple(hbm for _ in outs),
        scratch_shapes=[pltpu.VMEM(shape, kind) for shape, kind in scratch] + sems,
        compiler_params=pltpu.CompilerParams(
            collective_id=0, has_side_effects=True, vmem_limit_bytes=VMEM_LIMIT
        ),
        cost_estimate=pl.CostEstimate(flops=6 * 10**10, bytes_accessed=10**8, transcendentals=0),
    )(
        rows, back, held_row, held_col, w_qkv, w_proj, vectors, w_in, w_out
    )


def per_device(
    images,
    w_qkv,
    w_proj,
    w_router,
    w_in,
    w_out,
    gain_one,
    gain_two,
    routes,
    order,
    counts,
    cotangent,
):
    img_count, seq_len, width = images.shape
    tokens = img_count * seq_len
    routes_g = routes.reshape(tokens, TOPK)
    held, kept_pairs = route_slots(routes_g, order[0], counts[0])
    held = jnp.pad(
        held.reshape(img_count, seq_len, SPECIALIST_TOTAL),
        ((0, 0), (0, SEQ_PAD - seq_len), (0, LANES - SPECIALIST_TOTAL)),
        constant_values=-1,
    )
    padded = img_count * SEQ_PAD
    held_col = held.reshape(padded, LANES)
    held_row = held_col[:, :8].T
    pads = ((0, 0), (0, SEQ_PAD - seq_len), (0, 0))
    rows = jnp.pad(images, pads).reshape(padded, width)
    back = jnp.pad(cotangent, pads).reshape(padded, width)
    step = eight_step if lax.axis_size("dp") == 8 else plain_step
    output, grad_images, grad_in, grad_out, grads, small = step(
        rows, back, held_row, held_col, w_qkv.swapaxes(1, 2), w_proj, w_router.T, w_in, w_out,
        gain_one[None], gain_two[None],
    )
    cube = (img_count, SEQ_PAD, width)
    return (
        output.reshape(cube)[:, :seq_len],
        grad_images.reshape(cube)[:, :seq_len],
        grads[:3].astype(F32).transpose(0, 2, 1),
        grads[3].astype(F32),
        small[0, :SPECIALIST_TOTAL].astype(F32).T,
        grad_in.astype(F32),
        grad_out.astype(F32),
        small[1, 0].astype(F32),
        small[0, 8].astype(F32),
        kept_pairs.reshape(img_count, seq_len, TOPK),
    )


def solution(mesh):
    return jax.shard_map(
        per_device,
        mesh=mesh,
        in_specs=(
            P("dp", None, None),
            P(None, None, "tensor"),
            P("tensor", None),
            P(),
            P(None, None, "tensor"),
            P(None, "tensor", None),
            P(),
            P(),
            P("dp", None, None),
            P("dp", None),
            P("dp"),
            P("dp", None, None),
        ),
        out_specs=(
            P("dp", None, None),
            P("dp", None, None),
            P(None, None, "tensor"),
            P("tensor", None),
            P(),
            P(None, None, "tensor"),
            P(None, "tensor", None),
            P(),
            P(),
            P("dp", None, None),
        ),
        check_vma=False,
    )
```

```python
import functools

import jax
import jax.numpy as jnp
from jax import lax
from jax.experimental import pallas as pl
from jax.experimental.pallas import tpu as pltpu
from jax.sharding import PartitionSpec as P

HD = 64
SPECIALIST_TOTAL = 4
TOPK = 2
SEQ = 197
SEQ_PAD = 208
CAP = 616
CAP_PAD = 640
TILE = 320
PAIRED = SPECIALIST_TOTAL // 2
LANES = 128
PIECE = 128
PER_TURN = 1
RING = 6
LAG = 2
FORWARD = 4
DENSE_CUTS = ((0, 96), (96, 96), (192, 96), (288, 96), (384, 16))
DENSE_HALF = 400


EPSILON = 1e-06
SCALE = 0.125
BF = jnp.bfloat16
F32 = jnp.float32
MESH = pl.DeviceIdType.MESH
VMEM_LIMIT = 63 * 2**20


def dot(left, right, left_dim=1, right_dim=0):
    return lax.dot_general(
        left, right, (((left_dim,), (right_dim,)), ((), ())), preferred_element_type=F32
    )


def lane_ids(shape):
    return lax.broadcasted_iota(jnp.int32, shape, len(shape) - 1)


def standardize(rows):
    center = jnp.mean(rows, axis=-1, keepdims=True)
    centred = rows - center
    spread = jnp.mean(centred * centred, axis=-1, keepdims=True)
    root = lax.rsqrt(spread + EPSILON)
    return centred * root, root


def norm_back(grad, plain, root, gain):
    grad = grad * gain
    first = jnp.mean(grad, axis=-1, keepdims=True)
    second = jnp.mean(grad * plain, axis=-1, keepdims=True)
    return root * (grad - first - plain * second)


def route_slots(routes_g, order_g, count_g):
    tokens = routes_g.shape[0]
    positions = jnp.arange(tokens, dtype=jnp.int32)
    in_image = (positions // SEQ < count_g).astype(jnp.int32)
    capacity_now = (5 * TOPK * count_g * SEQ + 4 * SPECIALIST_TOTAL - 1) // (4 * SPECIALIST_TOTAL)
    spots = order_g[:, None] == positions[None, :]
    place = jnp.sum(jnp.where(spots, positions[:, None], 0), axis=0)
    earlier = (place[None, :] < place[:, None]).astype(BF)
    experts = jnp.arange(SPECIALIST_TOTAL, dtype=jnp.int32)
    marks = (routes_g[:, :, None] == experts).astype(jnp.int32) * in_image[:, None, None]
    marks = marks.reshape(tokens, TOPK * SPECIALIST_TOTAL)
    before = jnp.dot(earlier, marks.astype(BF), preferred_element_type=F32)
    before = before.reshape(tokens, TOPK, SPECIALIST_TOTAL).astype(jnp.int32)
    marks = marks.reshape(tokens, TOPK, SPECIALIST_TOTAL)
    first_total = jnp.sum(marks[:, 0, :], axis=0)
    before = before + jnp.stack([jnp.zeros_like(first_total), first_total])[None]
    slot_of = jnp.sum(before * marks, axis=-1)
    kept_pairs = in_image[:, None] * (slot_of < capacity_now).astype(jnp.int32)
    held = jnp.max(jnp.where((marks * kept_pairs[:, :, None]) > 0, before, -1), axis=1)
    return (held, kept_pairs)


def pair_sum(partial):
    n_t = lax.axis_size("tensor")
    core = lax.axis_index("tensor") % 2
    half = partial.shape[-1] // 2
    other = [(i, i ^ 1) for i in range(n_t)]
    mine = lax.dynamic_slice_in_dim(partial, core * half, half, partial.ndim - 1)
    gone = lax.dynamic_slice_in_dim(partial, (1 - core) * half, half, partial.ndim - 1)
    got = lax.ppermute(gone, "tensor", other)
    total = (mine.astype(F32) + got.astype(F32)).astype(BF)
    step = 2
    while step < n_t:
        got = lax.ppermute(total, "tensor", [(i, i ^ step) for i in range(n_t)])
        total = (total.astype(F32) + got.astype(F32)).astype(BF)
        step *= 2
    back = lax.ppermute(total, "tensor", other)
    return jnp.where(
        core == 0,
        jnp.concatenate([total, back], axis=-1),
        jnp.concatenate([back, total], axis=-1),
    )


def head_mask(shape, head):
    return lane_ids(shape) // HD == head


def image_rows(i):
    return pl.ds(pl.multiple_of(i * SEQ_PAD, 16), SEQ_PAD)


def attend(query, key, head):
    alone = jnp.where(head_mask(query.shape, head), query, jnp.zeros_like(query))
    scores = dot(alone, key, 1, 1) * SCALE
    scores = jnp.where(lane_ids(scores.shape) < SEQ, scores, -jnp.inf)
    powers = jnp.exp(scores - jnp.max(scores, axis=-1, keepdims=True))
    return powers / jnp.sum(powers, axis=-1, keepdims=True)


def attention_image(i, images, w_qkv, w_proj, gain, partial, qkv, mixed):
    at = image_rows(i)
    plain, _ = standardize(images[at, :].astype(F32))
    normed = (plain * gain[...]).astype(BF)
    for s in range(3):
        qkv[s, at, :] = dot(normed, w_qkv[s], 1, 1).astype(BF)
    query, key, value = (qkv[s, at, :] for s in range(3))
    result = jnp.zeros(query.shape, F32)
    for head in range(query.shape[1] // HD):
        weights = attend(query, key, head).astype(BF)
        result = jnp.where(head_mask(query.shape, head), dot(weights, value), result)
    result = result.astype(BF)
    mixed[at, :] = result
    partial[at, :] = dot(result, w_proj[...]).astype(BF)


def softmax_of(logits, axis):
    ids = lax.broadcasted_iota(jnp.int32, logits.shape, axis)
    logits = jnp.where(ids < SPECIALIST_TOTAL, logits, -jnp.inf)
    powers = jnp.exp(logits - jnp.max(logits, axis=axis, keepdims=True))
    return powers / jnp.sum(powers, axis=axis, keepdims=True)


def second_norm_image(i, images, attended, gain, normed):
    at = image_rows(i)
    plain, _ = standardize(images[at, :].astype(F32) + attended[at, :].astype(F32))
    normed[at, :] = (plain * gain[...]).astype(BF)


def gelu_both(rows):
    inner = 0.7978845608028654 * (rows + 0.044715 * rows * rows * rows)
    curve = jnp.tanh(inner)
    half = 0.5 * (1.0 + curve)
    slope = half + 0.5 * rows * (1.0 - curve * curve) * (
        0.7978845608028654 * (1.0 + 3.0 * 0.044715 * rows * rows)
    )
    return rows * half, slope


def expert_rows(expert, tokens, back, held, gates, w_in, w_out, factors, offset, sent, tick):
    width = tokens.shape[1]
    row = held[pl.ds(expert, 1), :]
    gate = gates[pl.ds(expert, 1), :]

    def tile(i, carry):
        ids = lax.broadcasted_iota(jnp.int32, (TILE, row.shape[1]), 0) + i * TILE
        hit = ids == row
        pick = jnp.where(hit, 1.0, 0.0).astype(BF)
        scale = jnp.sum(jnp.where(hit, gate, 0.0), axis=1, keepdims=True)
        buffer = dot(pick, tokens[...]).astype(BF)
        raw = dot(pick, back[...])
        grad = (scale * raw).astype(BF)
        value, slope = gelu_both(dot(buffer, w_in[...]))
        value = value.astype(BF)
        delta = (dot(grad, w_out[...], 1, 1) * slope).astype(BF)
        if factors is not None:
            at = pl.ds(pl.multiple_of(offset + i * TILE, 16), TILE)
            for ref, rows in zip(factors, (buffer, delta, value, grad)):
                ref[at, :] = rows
        if sent is not None:
            at = pl.ds(pl.multiple_of(i * TILE, 16), TILE)
            out = dot(value, w_out[...]).astype(BF).astype(F32)
            share = jnp.sum(out * raw, axis=1, keepdims=True)
            sent[at, :width] = (scale * out).astype(BF)
            sent[at, width : 2 * width] = dot(delta, w_in[...], 1, 1).astype(BF)
            lane = lane_ids((TILE, LANES)) == expert
            sent[at, 2 * width :] = jnp.where(lane, share, 0.0).astype(BF)
        if tick is not None:
            tick(i)
        return carry

    lax.fori_loop(0, CAP_PAD // TILE, tile, 0)


def return_rows(expert, held_col, sent, total, fresh, final, after, first=0, stop=None):
    def image(i, carry):
        at = image_rows(i)
        column = held_col[at, :]
        column = jnp.sum(
            jnp.where(lane_ids(column.shape) == expert, column, 0), axis=1, keepdims=True
        )
        pick = jnp.where(lane_ids((SEQ_PAD, CAP_PAD)) == column, 1.0, 0.0).astype(BF)
        back = dot(pick, sent[...])
        if final is None:
            total[at, :] = back if fresh else total[at, :] + back
        else:
            back = back + total[at, :]
            start = 0
            for ref in final:
                ref[at, :] = back[:, start : start + ref.shape[1]].astype(BF)
                start += ref.shape[1]
        if after is not None:
            after(i)
        return carry

    lax.fori_loop(first, stop or total.shape[0] // SEQ_PAD, image, 0)


def weight_rows(left, right, final, start, after):
    def step(i, carry):
        rows = pl.ds(pl.multiple_of(i * 256, 256), 256)
        to = pl.ds(pl.multiple_of(start + i * 256, 256), 256)
        final[to, :] = dot(left[:, rows], right[...], 0, 0).astype(BF)
        if after is not None:
            after(i)
        return carry

    lax.fori_loop(0, left.shape[1] // 256, step, 0)


def backward_image(
    i, images, attended, cotangent, sums, gate_sums, qkv, mixed, w_qkv, w_proj, w_router,
    gain_one, gain_two, partial, grad_hidden, grad_dense, grad_small,
):
    width = images.shape[1]
    at = image_rows(i)
    router = w_router[...]
    rows = images[at, :].astype(F32)
    plain, root = standardize(rows + attended[at, :].astype(F32))
    normed = (plain * gain_two[...]).astype(BF)
    gates = softmax_of(dot(normed, router, 1, 1), 1)
    grad_gates = gate_sums[at, :].astype(F32)[:, :8]
    grad_logits = gates * (grad_gates - jnp.sum(gates * grad_gates, axis=-1, keepdims=True))
    high = grad_logits.astype(BF)
    low = (grad_logits - high.astype(F32)).astype(BF)
    delta = sums[at, :].astype(F32) + (dot(high, router) + dot(low, router))
    grad_small[0:8, :] += dot(high, normed, 0, 0) + dot(low, normed, 0, 0)
    grad_small[8:9, :] += jnp.sum(delta * plain, axis=0, keepdims=True)
    grad = cotangent[at, :].astype(F32) + norm_back(delta, plain, root, gain_two[...])
    grad_hidden[at, :width] = grad
    grad = grad.astype(BF)
    grad_dense[3] += dot(mixed[at, :], grad, 0, 0)
    grad_mixed = dot(grad, w_proj[...], 1, 1).astype(BF)
    query, key, value = (qkv[s, at, :] for s in range(3))
    parts = [jnp.zeros(query.shape, F32) for _ in range(3)]
    for head in range(query.shape[1] // HD):
        mask = head_mask(query.shape, head)
        weights = attend(query, key, head)
        alone = jnp.where(mask, grad_mixed, jnp.zeros_like(grad_mixed))
        grad_weights = dot(alone, value, 1, 1)
        center = jnp.sum(weights * grad_weights, axis=-1, keepdims=True)
        scores = (weights * (grad_weights - center)).astype(BF)
        parts[0] = jnp.where(mask, dot(scores, key) * SCALE, parts[0])
        parts[1] = jnp.where(mask, dot(scores, query, 0, 0) * SCALE, parts[1])
        parts[2] = jnp.where(mask, dot(weights.astype(BF), grad_mixed, 0, 0), parts[2])
    first, _ = standardize(rows)
    first = (first * gain_one[...]).astype(BF)
    back = jnp.zeros((SEQ_PAD, width), F32)
    for s in range(3):
        part = parts[s].astype(BF)
        grad_dense[s] += dot(part, first, 0, 0)
        back = back + dot(part, w_qkv[s])
    partial[at, :] = back.astype(BF)


def output_image(i, images, attended, moe, output):
    at = image_rows(i)
    hidden = images[at, :].astype(F32) + attended[at, :].astype(F32)
    output[at, :] = (hidden + moe[at, :].astype(F32)).astype(BF)


def last_image(i, images, sums, grad_hidden, gain, grad_images, start, grad_gain):
    width = images.shape[1]
    at = image_rows(i)
    plain, root = standardize(images[at, :].astype(F32))
    delta = sums[at, :].astype(F32)
    grad_gain[0:1, :] += jnp.sum(delta * plain, axis=0, keepdims=True)
    grad = grad_hidden[at, :width] + norm_back(delta, plain, root, gain[...])
    grad_images[at, start : start + width] = grad


def loop(count, body):
    def step(i, carry):
        body(i)
        return carry

    lax.fori_loop(0, count, step, 0)


def attention_kernel(images, w_qkv, w_proj, gain, partial, qkv, mixed):
    loop(
        images.shape[0] // SEQ_PAD,
        lambda i: attention_image(i, images, w_qkv, w_proj, gain, partial, qkv, mixed),
    )


def second_norm_kernel(images, attended, gain, normed):
    loop(
        images.shape[0] // SEQ_PAD, lambda i: second_norm_image(i, images, attended, gain, normed)
    )


def expert_kernel(
    tokens, tokens_pair, back, back_pair, held, held_pair, held_col, w_router, w_in, w_out,
    moe, sums, gate_sums, main,
    gates, gates_pair, slots, inner, active, grads, sent, total,
):
    x = lax.rem(lax.axis_index("dp"), 2)
    gates[...] = softmax_of(dot(w_router[...], tokens[...], 1, 1), 0)
    gates_pair[...] = softmax_of(dot(w_router[...], tokens_pair[...], 1, 1), 0)
    width = tokens.shape[1]
    factors = (slots, inner, active, grads)
    for k in range(SPECIALIST_TOTAL):
        expert = lax.rem(x + k // PAIRED, 2) * PAIRED + k % PAIRED
        weights = (w_in.at[expert], w_out.at[expert])
        mine = factors if k < PAIRED else None
        expert_rows(expert, tokens, back, held, gates, *weights, mine, 0, sent, None)
        final = (moe, sums, gate_sums) if k == SPECIALIST_TOTAL - 1 else None
        return_rows(expert, held_col, sent, total, k == 0, final, None)
        if k < PAIRED:
            expert_rows(
                expert, tokens_pair, back_pair, held_pair, gates_pair, *weights, mine, CAP_PAD, None, None
            )
            weight_rows(slots, inner, main, 2 * k * width, None)
            weight_rows(active, grads, main, (2 * k + 1) * width, None)


def backward_kernel(
    images, attended, cotangent, moe, sums, gate_sums, qkv, mixed, w_qkv, w_proj, w_router,
    gain_one, gain_two,
    output, partial, grad_hidden, grad_dense, grad_small,
):
    grad_dense[...] = jnp.zeros_like(grad_dense)
    grad_small[...] = jnp.zeros_like(grad_small)

    def image(i):
        backward_image(
            i, images, attended, cotangent, sums, gate_sums, qkv, mixed, w_qkv, w_proj, w_router,
            gain_one, gain_two, partial, grad_hidden, grad_dense, grad_small,
        )
        output_image(i, images, attended, moe, output)

    loop(images.shape[0] // SEQ_PAD, image)


def last_kernel(images, sums, grad_hidden, gain, grad_images, grad_gain):
    grad_gain[...] = jnp.zeros_like(grad_gain)
    loop(
        images.shape[0] // SEQ_PAD,
        lambda i: last_image(i, images, sums, grad_hidden, gain, grad_images, 0, grad_gain),
    )


def call(kernel, outs, scratch, *args, flops=0):
    vmem = pl.BlockSpec(memory_space=pltpu.VMEM)
    return pl.pallas_call(
        kernel,
        out_shape=tuple(jax.ShapeDtypeStruct(shape, kind) for shape, kind in outs),
        in_specs=[vmem] * len(args),
        out_specs=tuple(vmem for _ in outs),
        scratch_shapes=[pltpu.VMEM(shape, kind) for shape, kind in scratch],
        compiler_params=pltpu.CompilerParams(vmem_limit_bytes=VMEM_LIMIT),
        cost_estimate=pl.CostEstimate(flops=flops, bytes_accessed=10**7, transcendentals=0),
    )(*args)


def swap_sum(main, dense):
    n_dp = lax.axis_size("dp")
    x = lax.axis_index("dp") % 2

    def swap(value, step):
        return lax.ppermute(value, "dp", [(i, i ^ step) for i in range(n_dp)])

    gone = lax.dynamic_index_in_dim(dense, 1 - x, 0, keepdims=False)
    mine = lax.dynamic_index_in_dim(dense, x, 0, keepdims=False)
    joined = (mine.astype(F32) + swap(gone, 1).astype(F32)).astype(BF)
    total = jnp.concatenate([main, joined], axis=0)
    step = 2
    while step < n_dp:
        total = (total.astype(F32) + swap(total, step).astype(F32)).astype(BF)
        step *= 2
    other = swap(total, 1)
    return jnp.where(x == 0, jnp.stack([total, other]), jnp.stack([other, total]))


def plain_step(rows, back, held_row, held_col, w_qkv, w_proj, router, w_in, w_out, gain_one, gain_two):
    pads = ((0, 0), (0, SEQ_PAD - rows.shape[1]), (0, 0))
    width = rows.shape[2]
    rows, back = (jnp.pad(each, pads).reshape(-1, width) for each in (rows, back))
    padded = rows.shape[0]
    gain_one, gain_two = gain_one[None], gain_two[None]
    local = w_proj.shape[0]
    router = jnp.pad(router, ((0, 8 - SPECIALIST_TOTAL), (0, 0)))
    n_dp = lax.axis_size("dp")
    swap = [(i, i ^ 1) for i in range(n_dp)]
    flat = (padded, width)
    held_pair = lax.ppermute(held_row, "dp", swap)
    back_pair = lax.ppermute(back, "dp", swap)
    partial, qkv, mixed = call(
        attention_kernel,
        [(flat, BF), ((3, padded, local), BF), ((padded, local), BF)],
        [],
        rows, w_qkv, w_proj, gain_one,
    )
    attended = pair_sum(partial)
    (normed,) = call(second_norm_kernel, [(flat, BF)], [], rows, attended, gain_two)
    normed_pair = lax.ppermute(normed, "dp", swap)
    wide = 2 * width + LANES
    moe, sums, gate_sums, main = call(
        expert_kernel,
        [(flat, BF), (flat, BF), ((padded, LANES), BF), ((4 * width, width), BF)],
        [((8, padded), F32)] * 2
        + [((2 * CAP_PAD, width), BF)] * 4
        + [((CAP_PAD, wide), BF), ((padded, wide), F32)],
        normed, normed_pair, back, back_pair,
        held_row, held_pair, held_col, router, w_in, w_out,
    )
    moe = pair_sum(moe)
    sums = pair_sum(sums)
    gate_sums = pair_sum(jnp.concatenate([gate_sums, gate_sums], axis=-1))[:, :LANES]
    output, partial, grad_hidden, grad_dense, grad_small = call(
        backward_kernel,
        [(flat, BF), (flat, BF), (flat, F32), ((4, local, width), F32), ((16, width), F32)],
        [],
        rows, attended, back, moe, sums, gate_sums,
        qkv, mixed, w_qkv, w_proj, router, gain_one, gain_two,
    )
    grad_images, grad_gain = call(
        last_kernel,
        [(flat, F32), ((8, width), F32)],
        [],
        rows, pair_sum(partial), grad_hidden, gain_one,
    )
    dense = grad_dense.reshape(2, 2 * local, width)
    small = jnp.stack([grad_small, jnp.pad(grad_gain, ((0, 8), (0, 0)))])
    dense = jnp.concatenate([dense, small], axis=1).astype(BF)
    whole = swap_sum(main, dense)
    rows_main = main.shape[0]
    experts = whole[:, :rows_main].reshape(SPECIALIST_TOTAL, 2, width, width)
    grads = whole[:, rows_main : rows_main + 2 * local].reshape(4, local, width)
    small = whole[:, rows_main + 2 * local :]
    return output, grad_images, experts[:, 0], experts[:, 1], grads, small


(
    ATT_RS, ATT_Y, ATT_AG, Z_X, Z_CORE, D_RS, G_RS, D_Y, G_Y, D_AG,
    O_RS, O_Y, O_AG, B_RS, B_Y, B_AG, COT, COT_Y, COT_CORE, DENSE, HELD,
) = range(21)


def step_kernel(
    held, held_col, w_qkv, w_proj, gain_first, gain_second, router_in, images_in, cotangent_in, w_in, w_out,
    output, grad_images, out_in, out_out, out_grads, out_small,
    images, cotangent, stage, stage_sems, wide_router, gain_one, gain_two,
    held_pair, router, back_pair, tokens, tokens_pair, attended, partial, qkv, mixed,
    core_a, far_a, core_d, far_d, core_o, far_o, core_g, far_g, gate_part, gate_sum,
    gates, gates_pair, slots, inner, active, grads, sent, total, slot_in, slot_out,
    grad_dense, grad_small, grad_last, main, landed, middle_ring, dense_x,
    sends, recvs, weight_sems, send_low, recv_low, send_mid, recv_mid, send_down, recv_down,
    send_pair, recv_pair, keep, out_sems,
):
    place = lax.axis_index("dp")
    spot = lax.axis_index("tensor")
    x = lax.rem(place, 2)
    z = place // 2
    c = lax.rem(spot, 2)
    y = spot // 2
    inside = jnp.logical_or(z == 1, z == 2)
    outside = jnp.logical_not(inside)
    core = {"tensor": spot + 1 - 2 * c}
    far = {"tensor": spot + 2 - 4 * y}
    pair = {"dp": place + 1 - 2 * x}
    line = {"dp": (z + 1 - 2 * lax.rem(z, 2)) * 2 + x}
    middle = {"dp": (3 - z) * 2 + x}
    width = images.shape[1]
    half = width // 2
    count = images.shape[0] // SEQ_PAD
    pieces = main.shape[0] // PIECE
    per_expert = 2 * width // PIECE
    mine = pl.ds(pl.multiple_of(c * half, LANES), half)
    other = pl.ds(pl.multiple_of((1 - c) * half, LANES), half)
    local = w_proj.shape[0]
    dense = active
    dense_landed, dense_middle = inner.at[:DENSE_HALF], inner.at[DENSE_HALF : 2 * DENSE_HALF]

    barrier = pltpu.get_barrier_semaphore()
    for peer in (core, far, pair, line):
        pl.semaphore_signal(barrier, inc=1, device_id=peer, device_id_type=MESH)

    @pl.when(inside)
    def _():
        pl.semaphore_signal(barrier, inc=1, device_id=middle, device_id_type=MESH)

    def load(k):
        expert = lax.rem(x + k // PAIRED, 2) * PAIRED + k % PAIRED
        return [
            pltpu.make_async_copy(w_in.at[expert], slot_in.at[k % 2], weight_sems.at[0, k % 2]),
            pltpu.make_async_copy(w_out.at[expert], slot_out.at[k % 2], weight_sems.at[1, k % 2]),
        ]

    def fetch(k, i):
        source = (cotangent_in, images_in)[k]
        return pltpu.make_async_copy(source.at[i], stage.at[k, i % 2], stage_sems.at[k, i % 2])

    for k in range(2):
        for i in range(2):
            fetch(k, i).start()
    for k in range(2):
        for copy in load(k):
            copy.start()
    wide_router[...] = jnp.zeros_like(wide_router)
    wide_router[:SPECIALIST_TOTAL, :] = router_in[...].astype(F32)
    router[...] = wide_router[...].astype(BF)
    gain_one[...] = gain_first[...][None]
    gain_two[...] = gain_second[...][None]
    grad_dense[...] = jnp.zeros_like(grad_dense)
    grad_small[...] = jnp.zeros_like(grad_small)
    grad_last[...] = jnp.zeros_like(grad_last)

    for i in range(count):
        for k, target in enumerate((cotangent, images)):
            fetch(k, i).wait()
            rows = stage[k, i % 2].astype(F32)
            rows = jnp.concatenate([rows, jnp.zeros((SEQ_PAD - SEQ, width), F32)])
            target[image_rows(i), :] = rows.astype(BF)
            if i + 2 < count:
                fetch(k, i + 2).start()

    @pl.when(inside)
    def _():
        pl.semaphore_wait(barrier, 5)

    @pl.when(outside)
    def _():
        pl.semaphore_wait(barrier, 4)

    def remote(src, dst, send, recv, peer):
        return pltpu.make_async_remote_copy(
            src_ref=src, dst_ref=dst, send_sem=send, recv_sem=recv,
            device_id=peer, device_id_type=MESH,
        )

    def channel(k, i, src, dst, peer):
        return remote(src, dst, sends.at[k, i], recvs.at[k, i], peer)

    def rs_copy(k, i, part, got):
        return channel(k, i, part.at[image_rows(i), other], got.at[image_rows(i), :], core)

    def far_copy(k, i, part, got):
        return channel(k, i, part.at[image_rows(i), mine], got.at[image_rows(i), :], far)

    def give_copy(k, i, result):
        view = result.at[image_rows(i), mine]
        return channel(k, i, view, view, core)

    def join_core(ks, i, part, near, got):
        at = image_rows(i)
        rs_copy(ks[0], i, part, near).wait_recv()
        rows = part[at, mine].astype(F32) + near[at, :].astype(F32)
        part[at, mine] = rows.astype(BF)
        far_copy(ks[1], i, part, got).start()

    def join_far(ks, i, part, got, result):
        at = image_rows(i)
        far_copy(ks[1], i, part, got).wait_recv()
        rows = part[at, mine].astype(F32) + got[at, :].astype(F32)
        result[at, mine] = rows.astype(BF)
        give_copy(ks[2], i, result).start()

    def sent_all(ks, part, near, got, result):
        def wait(i):
            rs_copy(ks[0], i, part, near).wait_send()
            far_copy(ks[1], i, part, got).wait_send()
            give_copy(ks[2], i, result).wait_send()

        loop(count, wait)

    def staged(step, lag, body):
        i = step - lag
        if isinstance(i, int):
            if 0 <= i < count:
                body(i)
            return

        @pl.when(jnp.logical_and(i >= 0, i < count))
        def _():
            body(i)

    held_copy = channel(HELD, 0, held, held_pair, pair)
    held_copy.start()

    def cot_copy(i):
        at = image_rows(i)
        return channel(COT, i, cotangent.at[at, mine], back_pair.at[at, mine], pair)

    def cot_far(i):
        view = back_pair.at[image_rows(i), mine]
        return channel(COT_Y, i, view, view, far)

    def cot_give(i):
        view = back_pair.at[image_rows(i), mine]
        return channel(COT_CORE, i, view, view, core)

    def shared(i):
        return i < count - 1

    def direct(i):
        return jnp.logical_or(lax.rem(i, 2) == y, i == count - 1)

    def cot_send(i):
        @pl.when(direct(i))
        def _():
            cot_copy(i).start()

    def cot_pass(i):
        @pl.when(direct(i))
        def _():
            cot_copy(i).wait()
            cot_give(i).start()

            @pl.when(shared(i))
            def _():
                cot_far(i).start()

    def cot_land(i):
        @pl.when(jnp.logical_not(direct(i)))
        def _():
            cot_far(i).wait_recv()
            cot_give(i).start()

    def cot_end(i):
        cot_give(i).wait()

        @pl.when(jnp.logical_and(direct(i), shared(i)))
        def _():
            cot_far(i).wait_send()

    loop(count, cot_send)

    att = (ATT_RS, ATT_Y, ATT_AG)

    def token_copy(i):
        at = image_rows(i)
        return channel(Z_X, i, tokens.at[at, mine], tokens_pair.at[at, mine], pair)

    def token_give(i):
        view = tokens_pair.at[image_rows(i), mine]
        return channel(Z_CORE, i, view, view, core)

    def attention_step(step):
        def first(i):
            attention_image(i, images, w_qkv, w_proj, gain_one, partial, qkv, mixed)
            rs_copy(ATT_RS, i, partial, core_a).start()

        def norm(i):
            give_copy(ATT_AG, i, attended).wait_recv()
            second_norm_image(i, images, attended, gain_two, tokens)
            token_copy(i).start()

        staged(step, 0, first)
        staged(step, 1, lambda i: join_core(att, i, partial, core_a, far_a))
        staged(step, 2, lambda i: join_far(att, i, partial, far_a, attended))
        staged(step, 3, norm)

        @pl.when(step == count + 1)
        def _():
            loop(count, cot_pass)

    loop(count + 3, attention_step)
    gates[...] = softmax_of(dot(router[...], tokens[...], 1, 1), 0)

    def dense_half(side):
        return pl.ds(pl.multiple_of(side * DENSE_HALF, 16), DENSE_HALF)

    def piece(n):
        if isinstance(n, int) and n >= pieces:
            start, size = DENSE_CUTS[n - pieces]
            at = pl.ds(start, size)
            views = [ref.at[at, :] for ref in (dense.at[dense_half(x)], dense_landed, dense_middle)]
            if size == 16:
                return views + [out_small.at[x]]
            at = pl.ds(start % local, size)
            return views + [out_grads.at[2 * x + start // local, at, :]]
        at = pl.ds(pl.multiple_of(n * PIECE, PIECE), PIECE)
        return [main.at[at, :], landed.at[at, :], middle_ring.at[lax.rem(n, RING)], None]

    def out_views(n):
        if isinstance(n, int) and n >= pieces:
            return [(None, piece(n)[3])]
        per_kind = width // PIECE
        expert = x * PAIRED + n // per_expert
        kind = lax.rem(n // per_kind, 2)
        at = pl.ds(pl.multiple_of(lax.rem(n, per_kind) * PIECE, PIECE), PIECE)
        return [(kind == 0, out_in.at[expert, at, :]), (kind == 1, out_out.at[expert, at, :])]

    def low_copy(n):
        own, got, _, _ = piece(n)
        return remote(own, got, send_low.at[n], recv_low.at[n], line)

    def mid_copy(n):
        own, _, got, _ = piece(n)
        return remote(own, got, send_mid.at[n], recv_mid.at[n], middle)

    def down_copy(n):
        _, done, _, _ = piece(n)
        return remote(done, done, send_down.at[n], recv_down.at[n], line)

    def each_out(n, act):
        done = piece(n)[1]
        for when, view in out_views(n):
            copies = (
                remote(done, view, send_pair.at[n], recv_pair.at[n], pair),
                pltpu.make_async_copy(done, view, keep.at[n]),
            )
            if when is None:
                act(*copies)
            else:
                pl.when(when)(functools.partial(act, *copies))

    def publish(n):
        def act(swap, own):
            swap.start()
            own.start()

        each_out(n, act)

    def add_piece(to, left, right):
        rows = to.shape[0]
        size = 64 if rows % 64 == 0 else 48 if rows % 48 == 0 else 16

        def add(i):
            at = pl.ds(pl.multiple_of(i * size, 16), size)
            to[at, :] = (left[at, :].astype(F32) + right[at, :].astype(F32)).astype(BF)

        loop(rows // size, add)

    last = pieces + len(DENSE_CUTS)

    main_turns = pieces // PER_TURN

    def tick(n):
        if isinstance(n, int) and n >= main_turns:
            turn_piece(pieces + n - main_turns)
        else:
            for j in range(PER_TURN):
                turn_piece(n * PER_TURN + j)

    def turn_piece(n):
        def when(n, body):
            if isinstance(n, int):
                if 0 <= n < last:
                    body(n)
            else:
                pl.when(n >= 0)(functools.partial(body, n))

        def gather(n):
            own, got, _, _ = piece(n)
            low_copy(n).wait_recv()
            add_piece(own, own, got)
            mid_copy(n).start()

        def finish(n):
            own, done, got, _ = piece(n)
            mid_copy(n).wait_recv()
            add_piece(done, own, got)
            down_copy(n).start()
            publish(n)

        def forward(n):
            down_copy(n).wait_recv()
            publish(n)

        @pl.when(inside)
        def _():
            when(n, gather)
            when(n - LAG, finish)

        @pl.when(outside)
        def _():
            when(n - FORWARD, forward)

    def lift(n):
        @pl.when(outside)
        def _():
            low_copy(n).start()

    factors = (slots, inner, active, grads)
    turn = 0
    final = (grads.at[: count * SEQ_PAD], slots.at[: count * SEQ_PAD], gate_part)
    moe_part, sum_part, _ = final
    dee = (D_RS, D_Y, D_AG)
    oh = (O_RS, O_Y, O_AG)
    moe, sums = tokens_pair, back_pair

    def gate_near(i):
        at = image_rows(i)
        return channel(G_RS, i, gate_part.at[at, :], core_g.at[at, :], core)

    def gate_far(i):
        at = image_rows(i)
        return channel(G_Y, i, gate_sum.at[at, :], far_g.at[at, :], far)

    def send_parts(i):
        rs_copy(D_RS, i, sum_part, core_d).start()
        gate_near(i).start()
        rs_copy(O_RS, i, moe_part, core_o).start()

    for k in range(SPECIALIST_TOTAL):
        expert = lax.rem(x + k // PAIRED, 2) * PAIRED + k % PAIRED
        weights = (slot_in.at[k % 2], slot_out.at[k % 2])
        for copy in load(k):
            copy.wait()
        kept = factors if k < PAIRED else None
        base = turn
        expert_rows(
            expert, tokens, cotangent, held, gates, *weights, kept, 0, sent,
            (lambda i, base=base: tick(base + i)) if k else None,
        )
        if k:
            turn += 2
        ends = k == SPECIALIST_TOTAL - 1
        if k == 0:

            def give(i):
                token_copy(i).wait_recv()
                token_give(i).start()

            loop(count, give)
            loop(count, cot_land)
            return_rows(expert, held_col, sent, total, True, None, None, 0, 2)
            loop(count, lambda i: token_give(i).wait_recv())
            loop(count, cot_end)
            held_copy.wait()
            gates_pair[...] = softmax_of(dot(router[...], tokens_pair[...], 1, 1), 0)
        else:
            return_rows(
                expert, held_col, sent, total, False, final if ends else None,
                send_parts if ends else None,
            )
            tick(turn)
            turn += 1
        if k < PAIRED:
            base = turn
            expert_rows(
                expert, tokens_pair, back_pair, held_pair, gates_pair, *weights, kept, CAP_PAD, None,
                (lambda i, base=base: tick(base + i)) if k else None,
            )
            if k:
                turn += 2
            for copy in load(k + 2):
                copy.start()
            per_step = 256 // PIECE
            for kind, (left, right) in enumerate(((slots, inner), (active, grads))):
                first = k * per_expert + kind * (width // PIECE)

                def after(i, first=first):
                    for j in range(per_step):
                        lift(first + i * per_step + j)

                weight_rows(left, right, main, (2 * k + kind) * width, after)
            if k == 0:
                return_rows(expert, held_col, sent, total, True, None, None, 2)
                tick(turn)
                turn += 1
        if k == PAIRED - 1:

            def tokens_sent(i):
                token_copy(i).wait_send()
                token_give(i).wait_send()

            loop(count, tokens_sent)
            sent_all(att, partial, core_a, far_a, attended)

    bee = (B_RS, B_Y, B_AG)

    def backward_step(step):
        def gates_core(i):
            join_core(dee, i, sum_part, core_d, far_d)
            at = image_rows(i)
            gate_near(i).wait_recv()
            rows = gate_part[at, :].astype(F32) + core_g[at, :].astype(F32)
            gate_sum[at, :] = rows.astype(BF)
            gate_far(i).start()

        def gates_all(i):
            join_far(dee, i, sum_part, far_d, sums)
            at = image_rows(i)
            gate_far(i).wait()
            rows = gate_sum[at, :].astype(F32) + far_g[at, :].astype(F32)
            gate_sum[at, :] = rows.astype(BF)

        def back(i):
            give_copy(D_AG, i, sums).wait()
            backward_image(
                i, images, attended, cotangent, sums, gate_sum, qkv, mixed, w_qkv, w_proj, router,
                gain_one, gain_two, partial, total, grad_dense, grad_small,
            )
            rs_copy(B_RS, i, partial, core_a).start()

        staged(step, 0, gates_core)
        staged(step, 1, gates_all)
        staged(step, 2, back)
        staged(step, 3, lambda i: join_core(bee, i, partial, core_a, far_a))
        staged(step, 4, lambda i: join_far(bee, i, partial, far_a, sums))
        staged(step, 5, finish)

    def grads_out(i):
        at = image_rows(i)
        return pltpu.make_async_copy(
            total.at[at, pl.ds(width, width)], grad_images.at[at, :], out_sems.at[0, i]
        )

    def rows_out(i):
        at = image_rows(i)
        return pltpu.make_async_copy(moe.at[at, :], output.at[at, :], out_sems.at[1, i])

    def finish(i):
        give_copy(B_AG, i, sums).wait_recv()
        last_image(i, images, sums, total, gain_one, total, width, grad_last)
        grads_out(i).start()

    def emit(i):
        give_copy(O_AG, i, moe).wait()
        output_image(i, images, attended, moe, moe)
        rows_out(i).start()

    base = turn

    def backward_turn(step):
        turns = base + step + jnp.maximum(step - 2, 0)
        tick(turns)
        backward_step(step)

        @pl.when(step >= 2)
        def _():
            tick(turns + 1)

    loop(count + 2, backward_turn)
    turn += 2 * count + 2

    def pack(i):
        start = i // 2 * DENSE_HALF + lax.rem(i, 2) * local
        dense[pl.ds(pl.multiple_of(start, 16), local), :] = grad_dense[i].astype(BF)

    def dense_view(i, side=0):
        start, size = DENSE_CUTS[i]
        return pl.ds(pl.multiple_of(side * DENSE_HALF + start, 16), size)

    def dense_copy(i):
        at = dense_view(i)
        return channel(DENSE, i, dense.at[dense_view(i, 1 - x), :], dense_x.at[at, :], pair)

    def dense_join(i):
        at = dense_view(i)
        dense_copy(i).wait()
        own = dense_view(i, x)
        dense[own, :] = (dense[own, :].astype(F32) + dense_x[at, :].astype(F32)).astype(BF)
        lift(pieces + i)

    small = len(DENSE_CUTS) - 1
    loop(4, pack)
    for i in range(small):
        dense_copy(i).start()
    join_core(bee, count - 1, partial, core_a, far_a)
    loop(count, lambda i: join_core(oh, i, moe_part, core_o, far_o))
    while turn < main_turns:
        tick(turn)
        turn += 1
    for i in range(count - 2, count):
        join_far(bee, i, partial, far_a, sums)
        finish(i - 1)
    finish(count - 1)
    for side, rows in enumerate((grad_small, grad_last)):
        dense[dense_view(small, side), :] = rows[...].astype(BF)
    dense_copy(small).start()
    for i in range(len(DENSE_CUTS)):
        dense_join(i)
        tick(turn)
        turn += 1
        join_far(oh, i, moe_part, far_o, moe)
        if i:
            emit(i - 1)
    emit(count - 1)
    while turn + pieces - main_turns < last + max(LAG, FORWARD):
        tick(turn)
        turn += 1

    def rest(i):
        rs_copy(D_RS, i, sum_part, core_d).wait_send()
        far_copy(D_Y, i, sum_part, far_d).wait_send()
        gate_near(i).wait_send()
        rs_copy(O_RS, i, moe_part, core_o).wait_send()
        far_copy(O_Y, i, moe_part, far_o).wait_send()
        grads_out(i).wait()
        rows_out(i).wait()

    loop(count, rest)
    sent_all(bee, partial, core_a, far_a, sums)

    def settle(n):
        @pl.when(outside)
        def _():
            low_copy(n).wait_send()

        @pl.when(inside)
        def _():
            mid_copy(n).wait_send()
            down_copy(n).wait_send()

        def act(swap, own):
            swap.wait()
            own.wait()

        each_out(n, act)

    loop(pieces, settle)
    for n in range(pieces, last):
        settle(n)


def eight_step(rows, back, held_row, held_col, w_qkv, w_proj, router, w_in, w_out, gain_one, gain_two):
    count, seq_len, width = rows.shape
    padded = count * SEQ_PAD
    local = w_proj.shape[0]
    half = width // 2
    wide = 2 * width + LANES
    pieces = 4 * width // PIECE
    last = pieces + len(DENSE_CUTS)
    vmem = pl.BlockSpec(memory_space=pltpu.VMEM)
    hbm = pl.BlockSpec(memory_space=pl.ANY)
    flat = ((padded, width), BF)
    part = ((padded, half), BF)
    thin = ((padded, LANES), BF)
    square = (width, width)
    start = [flat, flat, ((2, 2, seq_len, width), BF)]
    early = [((8, width), F32), ((1, width), F32), ((1, width), F32)]
    scratch = [((8, padded), jnp.int32), ((8, width), BF)] + [flat] * 5 + [((3, padded, local), BF), ((padded, local), BF)]
    scratch += [part] * 6 + [thin] * 4
    scratch += [((8, padded), F32)] * 2 + [((2 * CAP_PAD, width), BF)] * 4
    scratch += [((CAP_PAD, wide), BF), ((padded, wide), F32), ((2, *square), BF), ((2, *square), BF)]
    scratch += [((4, local, width), F32)] + [((16, width), F32)] * 2
    scratch += [((4 * width, width), BF)] * 2 + [((RING, PIECE, width), BF)]
    scratch += [((DENSE_HALF, width), BF)]
    dma = pltpu.SemaphoreType.DMA
    sems = [dma((21, count))] * 2 + [dma((2, 2))] + [dma((last,))] * 9 + [dma((2, count))]
    outs = [(flat[0], BF), (flat[0], F32)] + [((SPECIALIST_TOTAL, *square), BF)] * 2
    outs += [((4, local, width), BF), ((2, 16, width), BF)]
    return pl.pallas_call(
        step_kernel,
        out_shape=tuple(jax.ShapeDtypeStruct(shape, kind) for shape, kind in outs),
        in_specs=[vmem] * 7 + [hbm] * 4,
        out_specs=tuple(hbm for _ in outs),
        scratch_shapes=[pltpu.VMEM(*each) for each in start]
        + [dma((2, 2))]
        + [pltpu.VMEM(*each) for each in early + scratch]
        + sems,
        compiler_params=pltpu.CompilerParams(
            collective_id=0, has_side_effects=True, vmem_limit_bytes=VMEM_LIMIT
        ),
        cost_estimate=pl.CostEstimate(flops=6 * 10**10, bytes_accessed=10**8, transcendentals=0),
    )(
        held_row, held_col, w_qkv, w_proj, gain_one, gain_two, router, rows, back, w_in, w_out
    )


def trim_kernel(
    images_count, output, grad_images, grad_in, grad_out, grads, small,
    output_to, images_to, in_to, out_to, qkv_to, proj_to, router_to, first_to, second_to,
):
    turn = pl.program_id(0)
    in_to[...] = grad_in[...].astype(F32)
    out_to[...] = grad_out[...].astype(F32)

    @pl.when(turn < images_count)
    def _():
        output_to[0] = output[0][:SEQ]
        images_to[0] = grad_images[0][:SEQ]

    @pl.when(turn < 4)
    def _():
        rows = grads[0].astype(F32)

        @pl.when(turn < 3)
        def _():
            qkv_to[0] = rows

        @pl.when(turn == 3)
        def _():
            proj_to[...] = rows

    @pl.when(turn == 0)
    def _():
        rows = small[...].astype(F32)
        router_to[...] = rows[0, :SPECIALIST_TOTAL]
        second_to[...] = rows[0, 8]
        first_to[...] = rows[1, 0]


def trim(output, grad_images, grad_in, grad_out, grads, small):
    experts, width, _ = grad_in.shape
    local = grads.shape[1]
    images = output.shape[0]
    turns = 12
    rows = experts * width // turns
    cube = lambda size, count: pl.BlockSpec(
        (1, size, width), lambda i: (jnp.minimum(i, count - 1), 0, 0)
    )
    tall = pl.BlockSpec((rows, width), lambda i: (i, 0))
    whole = lambda *shape: pl.BlockSpec(shape, lambda i: (0,) * len(shape))
    flat = (experts * width, width)
    shapes = [(output.shape[0], SEQ, width), (output.shape[0], SEQ, width), flat, flat]
    shapes += [(3, local, width), (local, width), (experts, width), (width,), (width,)]
    kinds = [BF] + [F32] * 8
    got = pl.pallas_call(
        functools.partial(trim_kernel, images),
        grid=(turns,),
        out_shape=tuple(jax.ShapeDtypeStruct(a, b) for a, b in zip(shapes, kinds)),
        in_specs=[
            cube(SEQ_PAD, images), cube(SEQ_PAD, images), tall, tall, cube(local, 4),
            whole(*small.shape),
        ],
        out_specs=(
            cube(SEQ, images), cube(SEQ, images), tall, tall, cube(local, 3),
            whole(local, width), whole(experts, width), whole(width), whole(width),
        ),
        compiler_params=pltpu.CompilerParams(vmem_limit_bytes=VMEM_LIMIT),
        cost_estimate=pl.CostEstimate(flops=0, bytes_accessed=4 * 10**7, transcendentals=0),
    )(output, grad_images, grad_in.reshape(flat), grad_out.reshape(flat), grads, small)
    shape = (experts, width, width)
    return (*got[:2], got[2].reshape(shape), got[3].reshape(shape), *got[4:])


def per_device(
    images,
    w_qkv,
    w_proj,
    w_router,
    w_in,
    w_out,
    gain_one,
    gain_two,
    routes,
    order,
    counts,
    cotangent,
):
    img_count, seq_len, width = images.shape
    tokens = img_count * seq_len
    routes_g = routes.reshape(tokens, TOPK)
    held, kept_pairs = route_slots(routes_g, order[0], counts[0])
    held = jnp.pad(
        held.reshape(img_count, seq_len, SPECIALIST_TOTAL),
        ((0, 0), (0, SEQ_PAD - seq_len), (0, LANES - SPECIALIST_TOTAL)),
        constant_values=-1,
    )
    padded = img_count * SEQ_PAD
    held_col = held.reshape(padded, LANES)
    held_row = held_col[:, :8].T
    step = eight_step if lax.axis_size("dp") == 8 else plain_step
    output, grad_images, grad_in, grad_out, grads, small = step(
        images, cotangent, held_row, held_col, w_qkv.swapaxes(1, 2), w_proj, w_router.T, w_in, w_out,
        gain_one, gain_two,
    )
    cube = (img_count, SEQ_PAD, width)
    output, grad_images, grad_in, grad_out, grad_qkv, grad_proj, grad_router, first, second = trim(
        output.reshape(cube), grad_images.reshape(cube), grad_in, grad_out, grads, small
    )
    return (
        output,
        grad_images,
        grad_qkv.transpose(0, 2, 1),
        grad_proj,
        grad_router.T,
        grad_in,
        grad_out,
        first,
        second,
        kept_pairs.reshape(img_count, seq_len, TOPK),
    )


def solution(mesh):
    return jax.shard_map(
        per_device,
        mesh=mesh,
        in_specs=(
            P("dp", None, None),
            P(None, None, "tensor"),
            P("tensor", None),
            P(),
            P(None, None, "tensor"),
            P(None, "tensor", None),
            P(),
            P(),
            P("dp", None, None),
            P("dp", None),
            P("dp"),
            P("dp", None, None),
        ),
        out_specs=(
            P("dp", None, None),
            P("dp", None, None),
            P(None, None, "tensor"),
            P("tensor", None),
            P(),
            P(None, None, "tensor"),
            P(None, "tensor", None),
            P(),
            P(),
            P("dp", None, None),
        ),
        check_vma=False,
    )
```

```python
import functools

import jax
import jax.numpy as jnp
from jax import lax
from jax.experimental import pallas as pl
from jax.experimental.pallas import tpu as pltpu
from jax.sharding import PartitionSpec as P

HD = 64
SPECIALIST_TOTAL = 4
TOPK = 2
SEQ = 197
SEQ_PAD = 208
CAP = 616
CAP_PAD = 640
TILE = 320
PAIRED = SPECIALIST_TOTAL // 2
LANES = 128
PIECE = 128
PER_TURN = 1
RING = 6
LAG = 2
FORWARD = 4
DENSE_CUTS = ((0, 96), (96, 96), (192, 96), (288, 96), (384, 16))
DENSE_HALF = 400


EPSILON = 1e-06
SCALE = 0.125
BF = jnp.bfloat16
F32 = jnp.float32
MESH = pl.DeviceIdType.MESH
VMEM_LIMIT = 63 * 2**20


def dot(left, right, left_dim=1, right_dim=0):
    return lax.dot_general(
        left, right, (((left_dim,), (right_dim,)), ((), ())), preferred_element_type=F32
    )


def lane_ids(shape):
    return lax.broadcasted_iota(jnp.int32, shape, len(shape) - 1)


def standardize(rows):
    center = jnp.mean(rows, axis=-1, keepdims=True)
    centred = rows - center
    spread = jnp.mean(centred * centred, axis=-1, keepdims=True)
    root = lax.rsqrt(spread + EPSILON)
    return centred * root, root


def norm_back(grad, plain, root, gain):
    grad = grad * gain
    first = jnp.mean(grad, axis=-1, keepdims=True)
    second = jnp.mean(grad * plain, axis=-1, keepdims=True)
    return root * (grad - first - plain * second)


def route_slots(routes_g, order_g, count_g):
    tokens = routes_g.shape[0]
    positions = jnp.arange(tokens, dtype=jnp.int32)
    in_image = (positions // SEQ < count_g).astype(jnp.int32)
    capacity_now = (5 * TOPK * count_g * SEQ + 4 * SPECIALIST_TOTAL - 1) // (4 * SPECIALIST_TOTAL)
    spots = order_g[:, None] == positions[None, :]
    place = jnp.sum(jnp.where(spots, positions[:, None], 0), axis=0)
    earlier = (place[None, :] < place[:, None]).astype(BF)
    experts = jnp.arange(SPECIALIST_TOTAL, dtype=jnp.int32)
    marks = (routes_g[:, :, None] == experts).astype(jnp.int32) * in_image[:, None, None]
    marks = marks.reshape(tokens, TOPK * SPECIALIST_TOTAL)
    before = jnp.dot(earlier, marks.astype(BF), preferred_element_type=F32)
    before = before.reshape(tokens, TOPK, SPECIALIST_TOTAL).astype(jnp.int32)
    marks = marks.reshape(tokens, TOPK, SPECIALIST_TOTAL)
    first_total = jnp.sum(marks[:, 0, :], axis=0)
    before = before + jnp.stack([jnp.zeros_like(first_total), first_total])[None]
    slot_of = jnp.sum(before * marks, axis=-1)
    kept_pairs = in_image[:, None] * (slot_of < capacity_now).astype(jnp.int32)
    held = jnp.max(jnp.where((marks * kept_pairs[:, :, None]) > 0, before, -1), axis=1)
    return (held, kept_pairs)


def pair_sum(partial):
    n_t = lax.axis_size("tensor")
    core = lax.axis_index("tensor") % 2
    half = partial.shape[-1] // 2
    other = [(i, i ^ 1) for i in range(n_t)]
    mine = lax.dynamic_slice_in_dim(partial, core * half, half, partial.ndim - 1)
    gone = lax.dynamic_slice_in_dim(partial, (1 - core) * half, half, partial.ndim - 1)
    got = lax.ppermute(gone, "tensor", other)
    total = (mine.astype(F32) + got.astype(F32)).astype(BF)
    step = 2
    while step < n_t:
        got = lax.ppermute(total, "tensor", [(i, i ^ step) for i in range(n_t)])
        total = (total.astype(F32) + got.astype(F32)).astype(BF)
        step *= 2
    back = lax.ppermute(total, "tensor", other)
    return jnp.where(
        core == 0,
        jnp.concatenate([total, back], axis=-1),
        jnp.concatenate([back, total], axis=-1),
    )


def head_mask(shape, head):
    return lane_ids(shape) // HD == head


def image_rows(i):
    return pl.ds(pl.multiple_of(i * SEQ_PAD, 16), SEQ_PAD)


def attend(query, key, head):
    alone = jnp.where(head_mask(query.shape, head), query, jnp.zeros_like(query))
    scores = dot(alone, key, 1, 1) * SCALE
    scores = jnp.where(lane_ids(scores.shape) < SEQ, scores, -jnp.inf)
    powers = jnp.exp(scores - jnp.max(scores, axis=-1, keepdims=True))
    return powers / jnp.sum(powers, axis=-1, keepdims=True)


def attention_image(i, images, w_qkv, w_proj, gain, partial, qkv, mixed):
    at = image_rows(i)
    plain, _ = standardize(images[at, :].astype(F32))
    normed = (plain * gain[...]).astype(BF)
    for s in range(3):
        qkv[s, at, :] = dot(normed, w_qkv[s], 1, 1).astype(BF)
    query, key, value = (qkv[s, at, :] for s in range(3))
    result = jnp.zeros(query.shape, F32)
    for head in range(query.shape[1] // HD):
        weights = attend(query, key, head).astype(BF)
        result = jnp.where(head_mask(query.shape, head), dot(weights, value), result)
    result = result.astype(BF)
    mixed[at, :] = result
    partial[at, :] = dot(result, w_proj[...]).astype(BF)


def softmax_of(logits, axis):
    ids = lax.broadcasted_iota(jnp.int32, logits.shape, axis)
    logits = jnp.where(ids < SPECIALIST_TOTAL, logits, -jnp.inf)
    powers = jnp.exp(logits - jnp.max(logits, axis=axis, keepdims=True))
    return powers / jnp.sum(powers, axis=axis, keepdims=True)


def second_norm_image(i, images, attended, gain, normed):
    at = image_rows(i)
    plain, _ = standardize(images[at, :].astype(F32) + attended[at, :].astype(F32))
    normed[at, :] = (plain * gain[...]).astype(BF)


def gelu_both(rows):
    inner = 0.7978845608028654 * (rows + 0.044715 * rows * rows * rows)
    curve = jnp.tanh(inner)
    half = 0.5 * (1.0 + curve)
    slope = half + 0.5 * rows * (1.0 - curve * curve) * (
        0.7978845608028654 * (1.0 + 3.0 * 0.044715 * rows * rows)
    )
    return rows * half, slope


def expert_rows(
    expert, tokens, back, held, gates, w_in, w_out, factors, offset, sent, tick, ahead=False
):
    width = tokens.shape[1]
    row = held[pl.ds(expert, 1), :]
    gate = gates[pl.ds(expert, 1), :]

    def tile(i, carry):
        ids = lax.broadcasted_iota(jnp.int32, (TILE, row.shape[1]), 0) + i * TILE
        hit = ids == row
        pick = jnp.where(hit, 1.0, 0.0).astype(BF)
        scale = jnp.sum(jnp.where(hit, gate, 0.0), axis=1, keepdims=True)
        buffer = dot(pick, tokens[...]).astype(BF)
        if ahead:
            at = pl.ds(pl.multiple_of(offset + i * TILE, 16), TILE)
            raw = factors[3][at, :].astype(F32)
        else:
            raw = dot(pick, back[...])
        grad = (scale * raw).astype(BF)
        value, slope = gelu_both(dot(buffer, w_in[...]))
        value = value.astype(BF)
        delta = (dot(grad, w_out[...], 1, 1) * slope).astype(BF)
        if factors is not None:
            at = pl.ds(pl.multiple_of(offset + i * TILE, 16), TILE)
            for ref, rows in zip(factors, (buffer, delta, value, grad)):
                ref[at, :] = rows
        if sent is not None:
            at = pl.ds(pl.multiple_of(i * TILE, 16), TILE)
            out = dot(value, w_out[...]).astype(BF).astype(F32)
            share = jnp.sum(out * raw, axis=1, keepdims=True)
            sent[at, :width] = (scale * out).astype(BF)
            sent[at, width : 2 * width] = dot(delta, w_in[...], 1, 1).astype(BF)
            lane = lane_ids((TILE, LANES)) == expert
            sent[at, 2 * width :] = jnp.where(lane, share, 0.0).astype(BF)
        if tick is not None:
            tick(i)
        return carry

    lax.fori_loop(0, CAP_PAD // TILE, tile, 0)


def raw_rows(expert, back, held, grads, offset):
    row = held[pl.ds(expert, 1), :]

    def tile(i, carry):
        ids = lax.broadcasted_iota(jnp.int32, (TILE, row.shape[1]), 0) + i * TILE
        pick = jnp.where(ids == row, 1.0, 0.0).astype(BF)
        at = pl.ds(pl.multiple_of(offset + i * TILE, 16), TILE)
        grads[at, :] = dot(pick, back[...]).astype(BF)
        return carry

    lax.fori_loop(0, CAP_PAD // TILE, tile, 0)


def return_rows(expert, held_col, sent, total, fresh, final, after, first=0, stop=None):
    def image(i, carry):
        at = image_rows(i)
        column = held_col[at, :]
        column = jnp.sum(
            jnp.where(lane_ids(column.shape) == expert, column, 0), axis=1, keepdims=True
        )
        pick = jnp.where(lane_ids((SEQ_PAD, CAP_PAD)) == column, 1.0, 0.0).astype(BF)
        back = dot(pick, sent[...])
        if final is None:
            total[at, :] = back if fresh else total[at, :] + back
        else:
            back = back + total[at, :]
            start = 0
            for ref in final:
                ref[at, :] = back[:, start : start + ref.shape[1]].astype(BF)
                start += ref.shape[1]
        if after is not None:
            after(i)
        return carry

    lax.fori_loop(first, stop or total.shape[0] // SEQ_PAD, image, 0)


def weight_rows(left, right, final, start, after):
    def step(i, carry):
        rows = pl.ds(pl.multiple_of(i * 256, 256), 256)
        to = pl.ds(pl.multiple_of(start + i * 256, 256), 256)
        final[to, :] = dot(left[:, rows], right[...], 0, 0).astype(BF)
        if after is not None:
            after(i)
        return carry

    lax.fori_loop(0, left.shape[1] // 256, step, 0)


def backward_image(
    i, images, attended, cotangent, sums, gate_sums, qkv, mixed, w_qkv, w_proj, w_router,
    gain_one, gain_two, partial, grad_hidden, grad_dense, grad_small,
):
    width = images.shape[1]
    at = image_rows(i)
    router = w_router[...]
    rows = images[at, :].astype(F32)
    plain, root = standardize(rows + attended[at, :].astype(F32))
    normed = (plain * gain_two[...]).astype(BF)
    gates = softmax_of(dot(normed, router, 1, 1), 1)
    grad_gates = gate_sums[at, :].astype(F32)[:, :8]
    grad_logits = gates * (grad_gates - jnp.sum(gates * grad_gates, axis=-1, keepdims=True))
    high = grad_logits.astype(BF)
    low = (grad_logits - high.astype(F32)).astype(BF)
    delta = sums[at, :].astype(F32) + (dot(high, router) + dot(low, router))
    grad_small[0:8, :] += dot(high, normed, 0, 0) + dot(low, normed, 0, 0)
    grad_small[8:9, :] += jnp.sum(delta * plain, axis=0, keepdims=True)
    grad = cotangent[at, :].astype(F32) + norm_back(delta, plain, root, gain_two[...])
    grad_hidden[at, :width] = grad
    grad = grad.astype(BF)
    grad_dense[3] += dot(mixed[at, :], grad, 0, 0)
    grad_mixed = dot(grad, w_proj[...], 1, 1).astype(BF)
    query, key, value = (qkv[s, at, :] for s in range(3))
    parts = [jnp.zeros(query.shape, F32) for _ in range(3)]
    for head in range(query.shape[1] // HD):
        mask = head_mask(query.shape, head)
        weights = attend(query, key, head)
        alone = jnp.where(mask, grad_mixed, jnp.zeros_like(grad_mixed))
        grad_weights = dot(alone, value, 1, 1)
        center = jnp.sum(weights * grad_weights, axis=-1, keepdims=True)
        scores = (weights * (grad_weights - center)).astype(BF)
        parts[0] = jnp.where(mask, dot(scores, key) * SCALE, parts[0])
        parts[1] = jnp.where(mask, dot(scores, query, 0, 0) * SCALE, parts[1])
        parts[2] = jnp.where(mask, dot(weights.astype(BF), grad_mixed, 0, 0), parts[2])
    first, _ = standardize(rows)
    first = (first * gain_one[...]).astype(BF)
    back = jnp.zeros((SEQ_PAD, width), F32)
    for s in range(3):
        part = parts[s].astype(BF)
        grad_dense[s] += dot(part, first, 0, 0)
        back = back + dot(part, w_qkv[s])
    partial[at, :] = back.astype(BF)


def output_image(i, images, attended, moe, output):
    at = image_rows(i)
    hidden = images[at, :].astype(F32) + attended[at, :].astype(F32)
    output[at, :] = (hidden + moe[at, :].astype(F32)).astype(BF)


def last_image(i, images, sums, grad_hidden, gain, grad_images, start, grad_gain):
    width = images.shape[1]
    at = image_rows(i)
    plain, root = standardize(images[at, :].astype(F32))
    delta = sums[at, :].astype(F32)
    grad_gain[0:1, :] += jnp.sum(delta * plain, axis=0, keepdims=True)
    grad = grad_hidden[at, :width] + norm_back(delta, plain, root, gain[...])
    grad_images[at, start : start + width] = grad


def loop(count, body):
    def step(i, carry):
        body(i)
        return carry

    lax.fori_loop(0, count, step, 0)


def attention_kernel(images, w_qkv, w_proj, gain, partial, qkv, mixed):
    loop(
        images.shape[0] // SEQ_PAD,
        lambda i: attention_image(i, images, w_qkv, w_proj, gain, partial, qkv, mixed),
    )


def second_norm_kernel(images, attended, gain, normed):
    loop(
        images.shape[0] // SEQ_PAD, lambda i: second_norm_image(i, images, attended, gain, normed)
    )


def expert_kernel(
    tokens, tokens_pair, back, back_pair, held, held_pair, held_col, w_router, w_in, w_out,
    moe, sums, gate_sums, main,
    gates, gates_pair, slots, inner, active, grads, sent, total,
):
    x = lax.rem(lax.axis_index("dp"), 2)
    gates[...] = softmax_of(dot(w_router[...], tokens[...], 1, 1), 0)
    gates_pair[...] = softmax_of(dot(w_router[...], tokens_pair[...], 1, 1), 0)
    width = tokens.shape[1]
    factors = (slots, inner, active, grads)
    for k in range(SPECIALIST_TOTAL):
        expert = lax.rem(x + k // PAIRED, 2) * PAIRED + k % PAIRED
        weights = (w_in.at[expert], w_out.at[expert])
        mine = factors if k < PAIRED else None
        expert_rows(expert, tokens, back, held, gates, *weights, mine, 0, sent, None)
        final = (moe, sums, gate_sums) if k == SPECIALIST_TOTAL - 1 else None
        return_rows(expert, held_col, sent, total, k == 0, final, None)
        if k < PAIRED:
            expert_rows(
                expert, tokens_pair, back_pair, held_pair, gates_pair, *weights, mine, CAP_PAD, None, None
            )
            weight_rows(slots, inner, main, 2 * k * width, None)
            weight_rows(active, grads, main, (2 * k + 1) * width, None)


def backward_kernel(
    images, attended, cotangent, moe, sums, gate_sums, qkv, mixed, w_qkv, w_proj, w_router,
    gain_one, gain_two,
    output, partial, grad_hidden, grad_dense, grad_small,
):
    grad_dense[...] = jnp.zeros_like(grad_dense)
    grad_small[...] = jnp.zeros_like(grad_small)

    def image(i):
        backward_image(
            i, images, attended, cotangent, sums, gate_sums, qkv, mixed, w_qkv, w_proj, w_router,
            gain_one, gain_two, partial, grad_hidden, grad_dense, grad_small,
        )
        output_image(i, images, attended, moe, output)

    loop(images.shape[0] // SEQ_PAD, image)


def last_kernel(images, sums, grad_hidden, gain, grad_images, grad_gain):
    grad_gain[...] = jnp.zeros_like(grad_gain)
    loop(
        images.shape[0] // SEQ_PAD,
        lambda i: last_image(i, images, sums, grad_hidden, gain, grad_images, 0, grad_gain),
    )


def call(kernel, outs, scratch, *args, flops=0):
    vmem = pl.BlockSpec(memory_space=pltpu.VMEM)
    return pl.pallas_call(
        kernel,
        out_shape=tuple(jax.ShapeDtypeStruct(shape, kind) for shape, kind in outs),
        in_specs=[vmem] * len(args),
        out_specs=tuple(vmem for _ in outs),
        scratch_shapes=[pltpu.VMEM(shape, kind) for shape, kind in scratch],
        compiler_params=pltpu.CompilerParams(vmem_limit_bytes=VMEM_LIMIT),
        cost_estimate=pl.CostEstimate(flops=flops, bytes_accessed=10**7, transcendentals=0),
    )(*args)


def swap_sum(main, dense):
    n_dp = lax.axis_size("dp")
    x = lax.axis_index("dp") % 2

    def swap(value, step):
        return lax.ppermute(value, "dp", [(i, i ^ step) for i in range(n_dp)])

    gone = lax.dynamic_index_in_dim(dense, 1 - x, 0, keepdims=False)
    mine = lax.dynamic_index_in_dim(dense, x, 0, keepdims=False)
    joined = (mine.astype(F32) + swap(gone, 1).astype(F32)).astype(BF)
    total = jnp.concatenate([main, joined], axis=0)
    step = 2
    while step < n_dp:
        total = (total.astype(F32) + swap(total, step).astype(F32)).astype(BF)
        step *= 2
    other = swap(total, 1)
    return jnp.where(x == 0, jnp.stack([total, other]), jnp.stack([other, total]))


def plain_step(rows, back, held_row, held_col, w_qkv, w_proj, router, w_in, w_out, gain_one, gain_two):
    pads = ((0, 0), (0, SEQ_PAD - rows.shape[1]), (0, 0))
    width = rows.shape[2]
    rows, back = (jnp.pad(each, pads).reshape(-1, width) for each in (rows, back))
    padded = rows.shape[0]
    gain_one, gain_two = gain_one[None], gain_two[None]
    local = w_proj.shape[0]
    router = jnp.pad(router, ((0, 8 - SPECIALIST_TOTAL), (0, 0)))
    n_dp = lax.axis_size("dp")
    swap = [(i, i ^ 1) for i in range(n_dp)]
    flat = (padded, width)
    held_pair = lax.ppermute(held_row, "dp", swap)
    back_pair = lax.ppermute(back, "dp", swap)
    partial, qkv, mixed = call(
        attention_kernel,
        [(flat, BF), ((3, padded, local), BF), ((padded, local), BF)],
        [],
        rows, w_qkv, w_proj, gain_one,
    )
    attended = pair_sum(partial)
    (normed,) = call(second_norm_kernel, [(flat, BF)], [], rows, attended, gain_two)
    normed_pair = lax.ppermute(normed, "dp", swap)
    wide = 2 * width + LANES
    moe, sums, gate_sums, main = call(
        expert_kernel,
        [(flat, BF), (flat, BF), ((padded, LANES), BF), ((4 * width, width), BF)],
        [((8, padded), F32)] * 2
        + [((2 * CAP_PAD, width), BF)] * 4
        + [((CAP_PAD, wide), BF), ((padded, wide), F32)],
        normed, normed_pair, back, back_pair,
        held_row, held_pair, held_col, router, w_in, w_out,
    )
    moe = pair_sum(moe)
    sums = pair_sum(sums)
    gate_sums = pair_sum(jnp.concatenate([gate_sums, gate_sums], axis=-1))[:, :LANES]
    output, partial, grad_hidden, grad_dense, grad_small = call(
        backward_kernel,
        [(flat, BF), (flat, BF), (flat, F32), ((4, local, width), F32), ((16, width), F32)],
        [],
        rows, attended, back, moe, sums, gate_sums,
        qkv, mixed, w_qkv, w_proj, router, gain_one, gain_two,
    )
    grad_images, grad_gain = call(
        last_kernel,
        [(flat, F32), ((8, width), F32)],
        [],
        rows, pair_sum(partial), grad_hidden, gain_one,
    )
    dense = grad_dense.reshape(2, 2 * local, width)
    small = jnp.stack([grad_small, jnp.pad(grad_gain, ((0, 8), (0, 0)))])
    dense = jnp.concatenate([dense, small], axis=1).astype(BF)
    whole = swap_sum(main, dense)
    rows_main = main.shape[0]
    experts = whole[:, :rows_main].reshape(SPECIALIST_TOTAL, 2, width, width)
    grads = whole[:, rows_main : rows_main + 2 * local].reshape(4, local, width)
    small = whole[:, rows_main + 2 * local :]
    return output, grad_images, experts[:, 0], experts[:, 1], grads, small


(
    ATT_RS, ATT_Y, ATT_AG, Z_X, Z_CORE, D_RS, G_RS, D_Y, G_Y, D_AG,
    O_RS, O_Y, O_AG, B_RS, B_Y, B_AG, COT, COT_Y, COT_CORE, DENSE, HELD,
) = range(21)


def step_kernel(
    held, held_col, w_qkv, w_proj, gain_first, gain_second, router_in, images_in, cotangent_in, w_in, w_out,
    output, grad_images, out_in, out_out, out_grads, out_small,
    images, cotangent, stage, stage_sems, wide_router, gain_one, gain_two,
    held_pair, router, back_pair, tokens, tokens_pair, attended, partial, qkv, mixed,
    core_a, far_a, core_d, far_d, core_o, far_o, core_g, far_g, gate_part, gate_sum,
    gates, gates_pair, slots, inner, active, grads, sent, total, slot_in, slot_out,
    grad_dense, grad_small, grad_last, main, landed, middle_ring, dense_x,
    sends, recvs, weight_sems, send_low, recv_low, send_mid, recv_mid, send_down, recv_down,
    send_pair, recv_pair, keep, out_sems,
):
    place = lax.axis_index("dp")
    spot = lax.axis_index("tensor")
    x = lax.rem(place, 2)
    z = place // 2
    c = lax.rem(spot, 2)
    y = spot // 2
    inside = jnp.logical_or(z == 1, z == 2)
    outside = jnp.logical_not(inside)
    core = {"tensor": spot + 1 - 2 * c}
    far = {"tensor": spot + 2 - 4 * y}
    pair = {"dp": place + 1 - 2 * x}
    line = {"dp": (z + 1 - 2 * lax.rem(z, 2)) * 2 + x}
    middle = {"dp": (3 - z) * 2 + x}
    width = images.shape[1]
    half = width // 2
    count = images.shape[0] // SEQ_PAD
    pieces = main.shape[0] // PIECE
    per_expert = 2 * width // PIECE
    mine = pl.ds(pl.multiple_of(c * half, LANES), half)
    other = pl.ds(pl.multiple_of((1 - c) * half, LANES), half)
    local = w_proj.shape[0]
    dense = active
    dense_landed, dense_middle = inner.at[:DENSE_HALF], inner.at[DENSE_HALF : 2 * DENSE_HALF]

    barrier = pltpu.get_barrier_semaphore()
    for peer in (core, far, pair, line):
        pl.semaphore_signal(barrier, inc=1, device_id=peer, device_id_type=MESH)

    @pl.when(inside)
    def _():
        pl.semaphore_signal(barrier, inc=1, device_id=middle, device_id_type=MESH)

    def load(k):
        expert = lax.rem(x + k // PAIRED, 2) * PAIRED + k % PAIRED
        return [
            pltpu.make_async_copy(w_in.at[expert], slot_in.at[k % 2], weight_sems.at[0, k % 2]),
            pltpu.make_async_copy(w_out.at[expert], slot_out.at[k % 2], weight_sems.at[1, k % 2]),
        ]

    def fetch(k, i):
        source = (cotangent_in, images_in)[k]
        return pltpu.make_async_copy(source.at[i], stage.at[k, i % 2], stage_sems.at[k, i % 2])

    for k in range(2):
        for i in range(2):
            fetch(k, i).start()
    for k in range(2):
        for copy in load(k):
            copy.start()
    wide_router[...] = jnp.zeros_like(wide_router)
    wide_router[:SPECIALIST_TOTAL, :] = router_in[...].astype(F32)
    router[...] = wide_router[...].astype(BF)
    gain_one[...] = gain_first[...][None]
    gain_two[...] = gain_second[...][None]
    grad_dense[...] = jnp.zeros_like(grad_dense)
    grad_small[...] = jnp.zeros_like(grad_small)
    grad_last[...] = jnp.zeros_like(grad_last)

    for i in range(count):
        for k, target in enumerate((cotangent, images)):
            fetch(k, i).wait()
            rows = stage[k, i % 2].astype(F32)
            rows = jnp.concatenate([rows, jnp.zeros((SEQ_PAD - SEQ, width), F32)])
            target[image_rows(i), :] = rows.astype(BF)
            if i + 2 < count:
                fetch(k, i + 2).start()
    attention_image(0, images, w_qkv, w_proj, gain_one, partial, qkv, mixed)

    @pl.when(inside)
    def _():
        pl.semaphore_wait(barrier, 5)

    @pl.when(outside)
    def _():
        pl.semaphore_wait(barrier, 4)

    def remote(src, dst, send, recv, peer):
        return pltpu.make_async_remote_copy(
            src_ref=src, dst_ref=dst, send_sem=send, recv_sem=recv,
            device_id=peer, device_id_type=MESH,
        )

    def channel(k, i, src, dst, peer):
        return remote(src, dst, sends.at[k, i], recvs.at[k, i], peer)

    def rs_copy(k, i, part, got):
        return channel(k, i, part.at[image_rows(i), other], got.at[image_rows(i), :], core)

    def far_copy(k, i, part, got):
        return channel(k, i, part.at[image_rows(i), mine], got.at[image_rows(i), :], far)

    def give_copy(k, i, result):
        view = result.at[image_rows(i), mine]
        return channel(k, i, view, view, core)

    def join_core(ks, i, part, near, got):
        at = image_rows(i)
        rs_copy(ks[0], i, part, near).wait_recv()
        rows = part[at, mine].astype(F32) + near[at, :].astype(F32)
        part[at, mine] = rows.astype(BF)
        far_copy(ks[1], i, part, got).start()

    def join_far(ks, i, part, got, result):
        at = image_rows(i)
        far_copy(ks[1], i, part, got).wait_recv()
        rows = part[at, mine].astype(F32) + got[at, :].astype(F32)
        result[at, mine] = rows.astype(BF)
        give_copy(ks[2], i, result).start()

    def sent_all(ks, part, near, got, result):
        def wait(i):
            rs_copy(ks[0], i, part, near).wait_send()
            far_copy(ks[1], i, part, got).wait_send()
            give_copy(ks[2], i, result).wait_send()

        loop(count, wait)

    def staged(step, lag, body):
        i = step - lag
        if isinstance(i, int):
            if 0 <= i < count:
                body(i)
            return

        @pl.when(jnp.logical_and(i >= 0, i < count))
        def _():
            body(i)

    held_copy = channel(HELD, 0, held, held_pair, pair)
    held_copy.start()

    def cot_copy(i):
        at = image_rows(i)
        return channel(COT, i, cotangent.at[at, mine], back_pair.at[at, mine], pair)

    def cot_far(i):
        view = back_pair.at[image_rows(i), mine]
        return channel(COT_Y, i, view, view, far)

    def cot_give(i):
        view = back_pair.at[image_rows(i), mine]
        return channel(COT_CORE, i, view, view, core)

    def shared(i):
        return i < count - 1

    def direct(i):
        return jnp.logical_or(lax.rem(i, 2) == y, i == count - 1)

    def cot_send(i):
        @pl.when(direct(i))
        def _():
            cot_copy(i).start()

    def cot_pass(i):
        @pl.when(direct(i))
        def _():
            cot_copy(i).wait()
            cot_give(i).start()

            @pl.when(shared(i))
            def _():
                cot_far(i).start()

    def cot_land(i):
        @pl.when(jnp.logical_not(direct(i)))
        def _():
            cot_far(i).wait_recv()
            cot_give(i).start()

    def cot_end(i):
        cot_give(i).wait()

        @pl.when(jnp.logical_and(direct(i), shared(i)))
        def _():
            cot_far(i).wait_send()

    loop(count, cot_send)

    att = (ATT_RS, ATT_Y, ATT_AG)

    def token_copy(i):
        at = image_rows(i)
        return channel(Z_X, i, tokens.at[at, mine], tokens_pair.at[at, mine], pair)

    def token_give(i):
        view = tokens_pair.at[image_rows(i), mine]
        return channel(Z_CORE, i, view, view, core)

    def attention_step(step):
        def first(i):
            @pl.when(i > 0)
            def _():
                attention_image(i, images, w_qkv, w_proj, gain_one, partial, qkv, mixed)

            rs_copy(ATT_RS, i, partial, core_a).start()

        def norm(i):
            give_copy(ATT_AG, i, attended).wait_recv()
            second_norm_image(i, images, attended, gain_two, tokens)
            token_copy(i).start()

        staged(step, 0, first)
        staged(step, 1, lambda i: join_core(att, i, partial, core_a, far_a))
        staged(step, 2, lambda i: join_far(att, i, partial, far_a, attended))
        staged(step, 3, norm)

        @pl.when(step == count + 1)
        def _():
            loop(count, cot_pass)

    loop(count + 3, attention_step)
    gates[...] = softmax_of(dot(router[...], tokens[...], 1, 1), 0)

    def dense_half(side):
        return pl.ds(pl.multiple_of(side * DENSE_HALF, 16), DENSE_HALF)

    def piece(n):
        if isinstance(n, int) and n >= pieces:
            start, size = DENSE_CUTS[n - pieces]
            at = pl.ds(start, size)
            views = [ref.at[at, :] for ref in (dense.at[dense_half(x)], dense_landed, dense_middle)]
            if size == 16:
                return views + [out_small.at[x]]
            at = pl.ds(start % local, size)
            return views + [out_grads.at[2 * x + start // local, at, :]]
        at = pl.ds(pl.multiple_of(n * PIECE, PIECE), PIECE)
        return [main.at[at, :], landed.at[at, :], middle_ring.at[lax.rem(n, RING)], None]

    def out_views(n):
        if isinstance(n, int) and n >= pieces:
            return [(None, piece(n)[3])]
        per_kind = width // PIECE
        expert = x * PAIRED + n // per_expert
        kind = lax.rem(n // per_kind, 2)
        at = pl.ds(pl.multiple_of(lax.rem(n, per_kind) * PIECE, PIECE), PIECE)
        return [(kind == 0, out_in.at[expert, at, :]), (kind == 1, out_out.at[expert, at, :])]

    def low_copy(n):
        own, got, _, _ = piece(n)
        return remote(own, got, send_low.at[n], recv_low.at[n], line)

    def mid_copy(n):
        own, _, got, _ = piece(n)
        return remote(own, got, send_mid.at[n], recv_mid.at[n], middle)

    def down_copy(n):
        _, done, _, _ = piece(n)
        return remote(done, done, send_down.at[n], recv_down.at[n], line)

    def each_out(n, act):
        done = piece(n)[1]
        for when, view in out_views(n):
            copies = (
                remote(done, view, send_pair.at[n], recv_pair.at[n], pair),
                pltpu.make_async_copy(done, view, keep.at[n]),
            )
            if when is None:
                act(*copies)
            else:
                pl.when(when)(functools.partial(act, *copies))

    def publish(n):
        def act(swap, own):
            swap.start()
            own.start()

        each_out(n, act)

    def add_piece(to, left, right):
        rows = to.shape[0]
        size = 64 if rows % 64 == 0 else 48 if rows % 48 == 0 else 16

        def add(i):
            at = pl.ds(pl.multiple_of(i * size, 16), size)
            to[at, :] = (left[at, :].astype(F32) + right[at, :].astype(F32)).astype(BF)

        loop(rows // size, add)

    last = pieces + len(DENSE_CUTS)

    main_turns = pieces // PER_TURN

    def tick(n):
        if isinstance(n, int) and n >= main_turns:
            turn_piece(pieces + n - main_turns)
        else:
            for j in range(PER_TURN):
                turn_piece(n * PER_TURN + j)

    def turn_piece(n, start=0, stop=last):
        def when(n, body):
            if isinstance(n, int):
                if start <= n < stop:
                    body(n)
            else:
                pl.when(n >= 0)(functools.partial(body, n))

        def gather(n):
            own, got, _, _ = piece(n)
            low_copy(n).wait_recv()
            add_piece(own, own, got)
            mid_copy(n).start()

        def finish(n):
            own, done, got, _ = piece(n)
            mid_copy(n).wait_recv()
            add_piece(done, own, got)
            down_copy(n).start()
            publish(n)

        def forward(n):
            down_copy(n).wait_recv()
            publish(n)

        @pl.when(inside)
        def _():
            when(n, gather)
            when(n - LAG, finish)

        @pl.when(outside)
        def _():
            when(n - FORWARD, forward)

    def lift(n):
        @pl.when(outside)
        def _():
            low_copy(n).start()

    factors = (slots, inner, active, grads)
    turn = 0
    final = (grads.at[: count * SEQ_PAD], slots.at[: count * SEQ_PAD], gate_part)
    moe_part, sum_part, _ = final
    dee = (D_RS, D_Y, D_AG)
    oh = (O_RS, O_Y, O_AG)
    moe, sums = tokens_pair, back_pair

    def gate_near(i):
        at = image_rows(i)
        return channel(G_RS, i, gate_part.at[at, :], core_g.at[at, :], core)

    def gate_far(i):
        at = image_rows(i)
        return channel(G_Y, i, gate_sum.at[at, :], far_g.at[at, :], far)

    def send_parts(i):
        rs_copy(D_RS, i, sum_part, core_d).start()
        gate_near(i).start()
        rs_copy(O_RS, i, moe_part, core_o).start()

    for k in range(SPECIALIST_TOTAL):
        expert = lax.rem(x + k // PAIRED, 2) * PAIRED + k % PAIRED
        weights = (slot_in.at[k % 2], slot_out.at[k % 2])
        for copy in load(k):
            copy.wait()
        kept = factors if k < PAIRED else None
        base = turn

        def give(i):
            token_copy(i).wait_recv()
            token_give(i).start()

        def give_first(i):
            @pl.when(i == 0)
            def _():
                loop(count - 2, give)

        expert_rows(
            expert, tokens, cotangent, held, gates, *weights, kept, 0, sent,
            (lambda i, base=base: tick(base + i)) if k else give_first,
        )
        if k:
            turn += 2
        ends = k == SPECIALIST_TOTAL - 1
        if k == 0:
            for i in range(count - 2, count):
                give(i)
            loop(count, cot_land)
            return_rows(expert, held_col, sent, total, True, None, None, 0, 2)
            loop(count, cot_end)
            held_copy.wait()
            raw_rows(expert, back_pair, held_pair, grads, CAP_PAD)
            loop(count, lambda i: token_give(i).wait_recv())
            gates_pair[...] = softmax_of(dot(router[...], tokens_pair[...], 1, 1), 0)
        else:
            return_rows(
                expert, held_col, sent, total, False, final if ends else None,
                send_parts if ends else None,
            )
            tick(turn)
            turn += 1
        if k < PAIRED:
            base = turn
            expert_rows(
                expert, tokens_pair, back_pair, held_pair, gates_pair, *weights, kept, CAP_PAD, None,
                (lambda i, base=base: tick(base + i)) if k else None, k == 0,
            )
            if k:
                turn += 2
            for copy in load(k + 2):
                copy.start()
            per_step = 256 // PIECE
            for kind, (left, right) in enumerate(((slots, inner), (active, grads))):
                first = k * per_expert + kind * (width // PIECE)

                def after(i, first=first):
                    for j in range(per_step):
                        lift(first + i * per_step + j)

                weight_rows(left, right, main, (2 * k + kind) * width, after)
            if k == 0:
                return_rows(expert, held_col, sent, total, True, None, None, 2, 4)
                tick(turn)
                turn += 1
                return_rows(expert, held_col, sent, total, True, None, None, 4)
        if k == PAIRED - 1:

            def tokens_sent(i):
                token_copy(i).wait_send()
                token_give(i).wait_send()

            loop(count, tokens_sent)
            sent_all(att, partial, core_a, far_a, attended)

    bee = (B_RS, B_Y, B_AG)

    def backward_step(step):
        def gates_core(i):
            join_core(dee, i, sum_part, core_d, far_d)
            at = image_rows(i)
            gate_near(i).wait_recv()
            rows = gate_part[at, :].astype(F32) + core_g[at, :].astype(F32)
            gate_sum[at, :] = rows.astype(BF)
            gate_far(i).start()

        def gates_all(i):
            join_far(dee, i, sum_part, far_d, sums)
            at = image_rows(i)
            gate_far(i).wait()
            rows = gate_sum[at, :].astype(F32) + far_g[at, :].astype(F32)
            gate_sum[at, :] = rows.astype(BF)

        def back(i):
            give_copy(D_AG, i, sums).wait()
            backward_image(
                i, images, attended, cotangent, sums, gate_sum, qkv, mixed, w_qkv, w_proj, router,
                gain_one, gain_two, partial, total, grad_dense, grad_small,
            )
            rs_copy(B_RS, i, partial, core_a).start()

        staged(step, 0, gates_core)
        staged(step, 1, gates_all)
        staged(step, 2, back)
        staged(step, 3, lambda i: join_core(bee, i, partial, core_a, far_a))
        staged(step, 4, lambda i: join_far(bee, i, partial, far_a, sums))
        staged(step, 5, finish)

    def grads_out(i):
        at = image_rows(i)
        return pltpu.make_async_copy(
            total.at[at, pl.ds(width, width)], grad_images.at[at, :], out_sems.at[0, i]
        )

    def rows_out(i):
        at = image_rows(i)
        return pltpu.make_async_copy(moe.at[at, :], output.at[at, :], out_sems.at[1, i])

    def finish(i):
        give_copy(B_AG, i, sums).wait_recv()
        last_image(i, images, sums, total, gain_one, total, width, grad_last)
        grads_out(i).start()

    def emit(i):
        give_copy(O_AG, i, moe).wait()
        output_image(i, images, attended, moe, moe)
        rows_out(i).start()

    base = turn

    def backward_turn(step):
        turns = base + step + jnp.maximum(step - 2, 0)
        tick(turns)
        backward_step(step)

        @pl.when(step >= 2)
        def _():
            tick(turns + 1)

    loop(count + 2, backward_turn)
    turn += 2 * count + 2

    def pack(i):
        start = i // 2 * DENSE_HALF + lax.rem(i, 2) * local
        dense[pl.ds(pl.multiple_of(start, 16), local), :] = grad_dense[i].astype(BF)

    def dense_view(i, side=0):
        start, size = DENSE_CUTS[i]
        return pl.ds(pl.multiple_of(side * DENSE_HALF + start, 16), size)

    def dense_copy(i):
        at = dense_view(i)
        return channel(DENSE, i, dense.at[dense_view(i, 1 - x), :], dense_x.at[at, :], pair)

    def dense_join(i):
        at = dense_view(i)
        dense_copy(i).wait()
        own = dense_view(i, x)
        dense[own, :] = (dense[own, :].astype(F32) + dense_x[at, :].astype(F32)).astype(BF)
        lift(pieces + i)

    small = len(DENSE_CUTS) - 1
    loop(4, pack)
    for i in range(small):
        dense_copy(i).start()
    join_core(bee, count - 1, partial, core_a, far_a)
    loop(count, lambda i: join_core(oh, i, moe_part, core_o, far_o))
    while turn < main_turns:
        tick(turn)
        turn += 1

    def drain(n):
        turn_piece(pieces + n, 0, pieces)

    drain(0)
    join_far(bee, count - 2, partial, far_a, sums)
    finish(count - 3)
    drain(1)
    join_far(bee, count - 1, partial, far_a, sums)
    finish(count - 2)
    finish(count - 1)
    for side, rows in enumerate((grad_small, grad_last)):
        dense[dense_view(small, side), :] = rows[...].astype(BF)
    dense_copy(small).start()
    for n in range(2, FORWARD):
        drain(n)
    for i in range(len(DENSE_CUTS)):
        dense_join(i)
        turn_piece(pieces + i, pieces)
    for n in range(len(DENSE_CUTS), len(DENSE_CUTS) + FORWARD):
        turn_piece(pieces + n, pieces)
    for i in range(count):
        join_far(oh, i, moe_part, far_o, moe)
        if i:
            emit(i - 1)
    emit(count - 1)

    def rest(i):
        rs_copy(D_RS, i, sum_part, core_d).wait_send()
        far_copy(D_Y, i, sum_part, far_d).wait_send()
        gate_near(i).wait_send()
        rs_copy(O_RS, i, moe_part, core_o).wait_send()
        far_copy(O_Y, i, moe_part, far_o).wait_send()
        grads_out(i).wait()
        rows_out(i).wait()

    loop(count, rest)
    sent_all(bee, partial, core_a, far_a, sums)

    def settle(n):
        @pl.when(outside)
        def _():
            low_copy(n).wait_send()

        @pl.when(inside)
        def _():
            mid_copy(n).wait_send()
            down_copy(n).wait_send()

        def act(swap, own):
            swap.wait()
            own.wait()

        each_out(n, act)

    loop(pieces, settle)
    for n in range(pieces, last):
        settle(n)


def eight_step(rows, back, held_row, held_col, w_qkv, w_proj, router, w_in, w_out, gain_one, gain_two):
    count, seq_len, width = rows.shape
    padded = count * SEQ_PAD
    local = w_proj.shape[0]
    half = width // 2
    wide = 2 * width + LANES
    pieces = 4 * width // PIECE
    last = pieces + len(DENSE_CUTS)
    vmem = pl.BlockSpec(memory_space=pltpu.VMEM)
    hbm = pl.BlockSpec(memory_space=pl.ANY)
    flat = ((padded, width), BF)
    part = ((padded, half), BF)
    thin = ((padded, LANES), BF)
    square = (width, width)
    start = [flat, flat, ((2, 2, seq_len, width), BF)]
    early = [((8, width), F32), ((1, width), F32), ((1, width), F32)]
    scratch = [((8, padded), jnp.int32), ((8, width), BF)] + [flat] * 5 + [((3, padded, local), BF), ((padded, local), BF)]
    scratch += [part] * 6 + [thin] * 4
    scratch += [((8, padded), F32)] * 2 + [((2 * CAP_PAD, width), BF)] * 4
    scratch += [((CAP_PAD, wide), BF), ((padded, wide), F32), ((2, *square), BF), ((2, *square), BF)]
    scratch += [((4, local, width), F32)] + [((16, width), F32)] * 2
    scratch += [((4 * width, width), BF)] * 2 + [((RING, PIECE, width), BF)]
    scratch += [((DENSE_HALF, width), BF)]
    dma = pltpu.SemaphoreType.DMA
    sems = [dma((21, count))] * 2 + [dma((2, 2))] + [dma((last,))] * 9 + [dma((2, count))]
    outs = [(flat[0], BF), (flat[0], F32)] + [((SPECIALIST_TOTAL, *square), BF)] * 2
    outs += [((4, local, width), BF), ((2, 16, width), BF)]
    return pl.pallas_call(
        step_kernel,
        out_shape=tuple(jax.ShapeDtypeStruct(shape, kind) for shape, kind in outs),
        in_specs=[vmem] * 7 + [hbm] * 4,
        out_specs=tuple(hbm for _ in outs),
        scratch_shapes=[pltpu.VMEM(*each) for each in start]
        + [dma((2, 2))]
        + [pltpu.VMEM(*each) for each in early + scratch]
        + sems,
        compiler_params=pltpu.CompilerParams(
            collective_id=0, has_side_effects=True, vmem_limit_bytes=VMEM_LIMIT
        ),
        cost_estimate=pl.CostEstimate(flops=6 * 10**10, bytes_accessed=10**8, transcendentals=0),
    )(
        held_row, held_col, w_qkv, w_proj, gain_one, gain_two, router, rows, back, w_in, w_out
    )


def trim_kernel(
    images_count, output, grad_images, grad_in, grad_out, grads, small,
    output_to, images_to, in_to, out_to, qkv_to, proj_to, router_to, first_to, second_to,
):
    turn = pl.program_id(0)
    in_to[...] = grad_in[...].astype(F32)
    out_to[...] = grad_out[...].astype(F32)

    @pl.when(turn < images_count)
    def _():
        output_to[0] = output[0][:SEQ]
        images_to[0] = grad_images[0][:SEQ]

    @pl.when(turn < 4)
    def _():
        rows = grads[0].astype(F32)

        @pl.when(turn < 3)
        def _():
            qkv_to[0] = rows

        @pl.when(turn == 3)
        def _():
            proj_to[...] = rows

    @pl.when(turn == 0)
    def _():
        rows = small[...].astype(F32)
        router_to[...] = rows[0, :SPECIALIST_TOTAL]
        second_to[...] = rows[0, 8]
        first_to[...] = rows[1, 0]


def trim(output, grad_images, grad_in, grad_out, grads, small):
    experts, width, _ = grad_in.shape
    local = grads.shape[1]
    images = output.shape[0]
    turns = 8
    rows = experts * width // turns
    cube = lambda size, count: pl.BlockSpec(
        (1, size, width), lambda i: (jnp.minimum(i, count - 1), 0, 0)
    )
    tall = pl.BlockSpec((rows, width), lambda i: (i, 0))
    whole = lambda *shape: pl.BlockSpec(shape, lambda i: (0,) * len(shape))
    flat = (experts * width, width)
    shapes = [(output.shape[0], SEQ, width), (output.shape[0], SEQ, width), flat, flat]
    shapes += [(3, local, width), (local, width), (experts, width), (width,), (width,)]
    kinds = [BF] + [F32] * 8
    got = pl.pallas_call(
        functools.partial(trim_kernel, images),
        grid=(turns,),
        out_shape=tuple(jax.ShapeDtypeStruct(a, b) for a, b in zip(shapes, kinds)),
        in_specs=[
            cube(SEQ_PAD, images), cube(SEQ_PAD, images), tall, tall, cube(local, 4),
            whole(*small.shape),
        ],
        out_specs=(
            cube(SEQ, images), cube(SEQ, images), tall, tall, cube(local, 3),
            whole(local, width), whole(experts, width), whole(width), whole(width),
        ),
        compiler_params=pltpu.CompilerParams(vmem_limit_bytes=VMEM_LIMIT),
        cost_estimate=pl.CostEstimate(flops=0, bytes_accessed=4 * 10**7, transcendentals=0),
    )(output, grad_images, grad_in.reshape(flat), grad_out.reshape(flat), grads, small)
    shape = (experts, width, width)
    return (*got[:2], got[2].reshape(shape), got[3].reshape(shape), *got[4:])


def per_device(
    images,
    w_qkv,
    w_proj,
    w_router,
    w_in,
    w_out,
    gain_one,
    gain_two,
    routes,
    order,
    counts,
    cotangent,
):
    img_count, seq_len, width = images.shape
    tokens = img_count * seq_len
    routes_g = routes.reshape(tokens, TOPK)
    held, kept_pairs = route_slots(routes_g, order[0], counts[0])
    held = jnp.pad(
        held.reshape(img_count, seq_len, SPECIALIST_TOTAL),
        ((0, 0), (0, SEQ_PAD - seq_len), (0, LANES - SPECIALIST_TOTAL)),
        constant_values=-1,
    )
    padded = img_count * SEQ_PAD
    held_col = held.reshape(padded, LANES)
    held_row = held_col[:, :8].T
    step = eight_step if lax.axis_size("dp") == 8 else plain_step
    output, grad_images, grad_in, grad_out, grads, small = step(
        images, cotangent, held_row, held_col, w_qkv.swapaxes(1, 2), w_proj, w_router.T, w_in, w_out,
        gain_one, gain_two,
    )
    cube = (img_count, SEQ_PAD, width)
    output, grad_images, grad_in, grad_out, grad_qkv, grad_proj, grad_router, first, second = trim(
        output.reshape(cube), grad_images.reshape(cube), grad_in, grad_out, grads, small
    )
    return (
        output,
        grad_images,
        grad_qkv.transpose(0, 2, 1),
        grad_proj,
        grad_router.T,
        grad_in,
        grad_out,
        first,
        second,
        kept_pairs.reshape(img_count, seq_len, TOPK),
    )


def solution(mesh):
    return jax.shard_map(
        per_device,
        mesh=mesh,
        in_specs=(
            P("dp", None, None),
            P(None, None, "tensor"),
            P("tensor", None),
            P(),
            P(None, None, "tensor"),
            P(None, "tensor", None),
            P(),
            P(),
            P("dp", None, None),
            P("dp", None),
            P("dp"),
            P("dp", None, None),
        ),
        out_specs=(
            P("dp", None, None),
            P("dp", None, None),
            P(None, None, "tensor"),
            P("tensor", None),
            P(),
            P(None, None, "tensor"),
            P(None, "tensor", None),
            P(),
            P(),
            P("dp", None, None),
        ),
        check_vma=False,
    )
```

```python
import functools

import jax
import jax.numpy as jnp
from jax import lax
from jax.experimental import pallas as pl
from jax.experimental.pallas import tpu as pltpu
from jax.sharding import PartitionSpec as P

HD = 64
SPECIALIST_TOTAL = 4
TOPK = 2
SEQ = 197
SEQ_PAD = 208
CAP = 616
CAP_PAD = 640
TILE = 320
PAIRED = SPECIALIST_TOTAL // 2
LANES = 128
PIECE = 128
PER_TURN = 1
RING = 6
LAG = 2
FORWARD = 4
DENSE_CUTS = ((0, 96), (96, 96), (192, 96), (288, 96), (384, 16))
DENSE_HALF = 400


EPSILON = 1e-06
SCALE = 0.125
BF = jnp.bfloat16
F32 = jnp.float32
MESH = pl.DeviceIdType.MESH
VMEM_LIMIT = 63 * 2**20


def dot(left, right, left_dim=1, right_dim=0):
    return lax.dot_general(
        left, right, (((left_dim,), (right_dim,)), ((), ())), preferred_element_type=F32
    )


def lane_ids(shape):
    return lax.broadcasted_iota(jnp.int32, shape, len(shape) - 1)


def standardize(rows):
    center = jnp.mean(rows, axis=-1, keepdims=True)
    centred = rows - center
    spread = jnp.mean(centred * centred, axis=-1, keepdims=True)
    root = lax.rsqrt(spread + EPSILON)
    return centred * root, root


def norm_back(grad, plain, root, gain):
    grad = grad * gain
    first = jnp.mean(grad, axis=-1, keepdims=True)
    second = jnp.mean(grad * plain, axis=-1, keepdims=True)
    return root * (grad - first - plain * second)


def route_slots(routes_g, order_g, count_g):
    tokens = routes_g.shape[0]
    positions = jnp.arange(tokens, dtype=jnp.int32)
    in_image = (positions // SEQ < count_g).astype(jnp.int32)
    capacity_now = (5 * TOPK * count_g * SEQ + 4 * SPECIALIST_TOTAL - 1) // (4 * SPECIALIST_TOTAL)
    spots = order_g[:, None] == positions[None, :]
    place = jnp.sum(jnp.where(spots, positions[:, None], 0), axis=0)
    earlier = (place[None, :] < place[:, None]).astype(BF)
    experts = jnp.arange(SPECIALIST_TOTAL, dtype=jnp.int32)
    marks = (routes_g[:, :, None] == experts).astype(jnp.int32) * in_image[:, None, None]
    marks = marks.reshape(tokens, TOPK * SPECIALIST_TOTAL)
    before = jnp.dot(earlier, marks.astype(BF), preferred_element_type=F32)
    before = before.reshape(tokens, TOPK, SPECIALIST_TOTAL).astype(jnp.int32)
    marks = marks.reshape(tokens, TOPK, SPECIALIST_TOTAL)
    first_total = jnp.sum(marks[:, 0, :], axis=0)
    before = before + jnp.stack([jnp.zeros_like(first_total), first_total])[None]
    slot_of = jnp.sum(before * marks, axis=-1)
    kept_pairs = in_image[:, None] * (slot_of < capacity_now).astype(jnp.int32)
    held = jnp.max(jnp.where((marks * kept_pairs[:, :, None]) > 0, before, -1), axis=1)
    return (held, kept_pairs)


def pair_sum(partial):
    n_t = lax.axis_size("tensor")
    core = lax.axis_index("tensor") % 2
    half = partial.shape[-1] // 2
    other = [(i, i ^ 1) for i in range(n_t)]
    mine = lax.dynamic_slice_in_dim(partial, core * half, half, partial.ndim - 1)
    gone = lax.dynamic_slice_in_dim(partial, (1 - core) * half, half, partial.ndim - 1)
    got = lax.ppermute(gone, "tensor", other)
    total = (mine.astype(F32) + got.astype(F32)).astype(BF)
    step = 2
    while step < n_t:
        got = lax.ppermute(total, "tensor", [(i, i ^ step) for i in range(n_t)])
        total = (total.astype(F32) + got.astype(F32)).astype(BF)
        step *= 2
    back = lax.ppermute(total, "tensor", other)
    return jnp.where(
        core == 0,
        jnp.concatenate([total, back], axis=-1),
        jnp.concatenate([back, total], axis=-1),
    )


def head_mask(shape, head):
    return lane_ids(shape) // HD == head


def image_rows(i):
    return pl.ds(pl.multiple_of(i * SEQ_PAD, 16), SEQ_PAD)


def attend(query, key, head):
    alone = jnp.where(head_mask(query.shape, head), query, jnp.zeros_like(query))
    scores = dot(alone, key, 1, 1) * SCALE
    scores = jnp.where(lane_ids(scores.shape) < SEQ, scores, -jnp.inf)
    powers = jnp.exp(scores - jnp.max(scores, axis=-1, keepdims=True))
    return powers / jnp.sum(powers, axis=-1, keepdims=True)


def attention_image(i, images, w_qkv, w_proj, gain, partial, qkv, mixed):
    at = image_rows(i)
    plain, _ = standardize(images[at, :].astype(F32))
    normed = (plain * gain[...]).astype(BF)
    for s in range(3):
        qkv[s, at, :] = dot(normed, w_qkv[s], 1, 1).astype(BF)
    query, key, value = (qkv[s, at, :] for s in range(3))
    result = jnp.zeros(query.shape, F32)
    for head in range(query.shape[1] // HD):
        weights = attend(query, key, head).astype(BF)
        result = jnp.where(head_mask(query.shape, head), dot(weights, value), result)
    result = result.astype(BF)
    mixed[at, :] = result
    partial[at, :] = dot(result, w_proj[...]).astype(BF)


def softmax_of(logits, axis):
    ids = lax.broadcasted_iota(jnp.int32, logits.shape, axis)
    logits = jnp.where(ids < SPECIALIST_TOTAL, logits, -jnp.inf)
    powers = jnp.exp(logits - jnp.max(logits, axis=axis, keepdims=True))
    return powers / jnp.sum(powers, axis=axis, keepdims=True)


def second_norm_image(i, images, attended, gain, normed):
    at = image_rows(i)
    plain, _ = standardize(images[at, :].astype(F32) + attended[at, :].astype(F32))
    normed[at, :] = (plain * gain[...]).astype(BF)


def gelu_both(rows):
    inner = 0.7978845608028654 * (rows + 0.044715 * rows * rows * rows)
    curve = jnp.tanh(inner)
    half = 0.5 * (1.0 + curve)
    slope = half + 0.5 * rows * (1.0 - curve * curve) * (
        0.7978845608028654 * (1.0 + 3.0 * 0.044715 * rows * rows)
    )
    return rows * half, slope


def expert_rows(expert, tokens, back, held, gates, w_in, w_out, factors, offset, sent, tick):
    width = tokens.shape[1]
    row = held[pl.ds(expert, 1), :]
    gate = gates[pl.ds(expert, 1), :]

    def tile(i, carry):
        ids = lax.broadcasted_iota(jnp.int32, (TILE, row.shape[1]), 0) + i * TILE
        hit = ids == row
        pick = jnp.where(hit, 1.0, 0.0).astype(BF)
        scale = jnp.sum(jnp.where(hit, gate, 0.0), axis=1, keepdims=True)
        buffer = dot(pick, tokens[...]).astype(BF)
        raw = dot(pick, back[...])
        grad = (scale * raw).astype(BF)
        value, slope = gelu_both(dot(buffer, w_in[...]))
        value = value.astype(BF)
        delta = (dot(grad, w_out[...], 1, 1) * slope).astype(BF)
        if factors is not None:
            at = pl.ds(pl.multiple_of(offset + i * TILE, 16), TILE)
            for ref, rows in zip(factors, (buffer, delta, value, grad)):
                ref[at, :] = rows
        if sent is not None:
            at = pl.ds(pl.multiple_of(i * TILE, 16), TILE)
            out = dot(value, w_out[...]).astype(BF).astype(F32)
            share = jnp.sum(out * raw, axis=1, keepdims=True)
            sent[at, :width] = (scale * out).astype(BF)
            sent[at, width : 2 * width] = dot(delta, w_in[...], 1, 1).astype(BF)
            lane = lane_ids((TILE, LANES)) == expert
            sent[at, 2 * width :] = jnp.where(lane, share, 0.0).astype(BF)
        if tick is not None:
            tick(i)
        return carry

    lax.fori_loop(0, CAP_PAD // TILE, tile, 0)


def return_rows(expert, held_col, sent, total, fresh, final, after, first=0, stop=None):
    def image(i, carry):
        at = image_rows(i)
        column = held_col[at, :]
        column = jnp.sum(
            jnp.where(lane_ids(column.shape) == expert, column, 0), axis=1, keepdims=True
        )
        pick = jnp.where(lane_ids((SEQ_PAD, CAP_PAD)) == column, 1.0, 0.0).astype(BF)
        back = dot(pick, sent[...])
        if final is None:
            total[at, :] = back if fresh else total[at, :] + back
        else:
            back = back + total[at, :]
            start = 0
            for ref in final:
                ref[at, :] = back[:, start : start + ref.shape[1]].astype(BF)
                start += ref.shape[1]
        if after is not None:
            after(i)
        return carry

    lax.fori_loop(first, stop or total.shape[0] // SEQ_PAD, image, 0)


def weight_rows(left, right, final, start, after):
    def step(i, carry):
        rows = pl.ds(pl.multiple_of(i * 256, 256), 256)
        to = pl.ds(pl.multiple_of(start + i * 256, 256), 256)
        final[to, :] = dot(left[:, rows], right[...], 0, 0).astype(BF)
        if after is not None:
            after(i)
        return carry

    lax.fori_loop(0, left.shape[1] // 256, step, 0)


def backward_image(
    i, images, attended, cotangent, sums, gate_sums, qkv, mixed, w_qkv, w_proj, w_router,
    gain_one, gain_two, partial, grad_hidden, grad_dense, grad_small,
):
    width = images.shape[1]
    at = image_rows(i)
    router = w_router[...]
    rows = images[at, :].astype(F32)
    plain, root = standardize(rows + attended[at, :].astype(F32))
    normed = (plain * gain_two[...]).astype(BF)
    gates = softmax_of(dot(normed, router, 1, 1), 1)
    grad_gates = gate_sums[at, :].astype(F32)[:, :8]
    grad_logits = gates * (grad_gates - jnp.sum(gates * grad_gates, axis=-1, keepdims=True))
    high = grad_logits.astype(BF)
    low = (grad_logits - high.astype(F32)).astype(BF)
    delta = sums[at, :].astype(F32) + (dot(high, router) + dot(low, router))
    grad_small[0:8, :] += dot(high, normed, 0, 0) + dot(low, normed, 0, 0)
    grad_small[8:9, :] += jnp.sum(delta * plain, axis=0, keepdims=True)
    grad = cotangent[at, :].astype(F32) + norm_back(delta, plain, root, gain_two[...])
    grad_hidden[at, :width] = grad
    grad = grad.astype(BF)
    grad_dense[3] += dot(mixed[at, :], grad, 0, 0)
    grad_mixed = dot(grad, w_proj[...], 1, 1).astype(BF)
    query, key, value = (qkv[s, at, :] for s in range(3))
    parts = [jnp.zeros(query.shape, F32) for _ in range(3)]
    for head in range(query.shape[1] // HD):
        mask = head_mask(query.shape, head)
        weights = attend(query, key, head)
        alone = jnp.where(mask, grad_mixed, jnp.zeros_like(grad_mixed))
        grad_weights = dot(alone, value, 1, 1)
        center = jnp.sum(weights * grad_weights, axis=-1, keepdims=True)
        scores = (weights * (grad_weights - center)).astype(BF)
        parts[0] = jnp.where(mask, dot(scores, key) * SCALE, parts[0])
        parts[1] = jnp.where(mask, dot(scores, query, 0, 0) * SCALE, parts[1])
        parts[2] = jnp.where(mask, dot(weights.astype(BF), grad_mixed, 0, 0), parts[2])
    first, _ = standardize(rows)
    first = (first * gain_one[...]).astype(BF)
    back = jnp.zeros((SEQ_PAD, width), F32)
    for s in range(3):
        part = parts[s].astype(BF)
        grad_dense[s] += dot(part, first, 0, 0)
        back = back + dot(part, w_qkv[s])
    partial[at, :] = back.astype(BF)


def output_image(i, images, attended, moe, output):
    at = image_rows(i)
    hidden = images[at, :].astype(F32) + attended[at, :].astype(F32)
    output[at, :] = (hidden + moe[at, :].astype(F32)).astype(BF)


def last_image(i, images, sums, grad_hidden, gain, grad_images, start, grad_gain):
    width = images.shape[1]
    at = image_rows(i)
    plain, root = standardize(images[at, :].astype(F32))
    delta = sums[at, :].astype(F32)
    grad_gain[0:1, :] += jnp.sum(delta * plain, axis=0, keepdims=True)
    grad = grad_hidden[at, :width] + norm_back(delta, plain, root, gain[...])
    grad_images[at, start : start + width] = grad


def loop(count, body):
    def step(i, carry):
        body(i)
        return carry

    lax.fori_loop(0, count, step, 0)


def attention_kernel(images, w_qkv, w_proj, gain, partial, qkv, mixed):
    loop(
        images.shape[0] // SEQ_PAD,
        lambda i: attention_image(i, images, w_qkv, w_proj, gain, partial, qkv, mixed),
    )


def second_norm_kernel(images, attended, gain, normed):
    loop(
        images.shape[0] // SEQ_PAD, lambda i: second_norm_image(i, images, attended, gain, normed)
    )


def expert_kernel(
    tokens, tokens_pair, back, back_pair, held, held_pair, held_col, w_router, w_in, w_out,
    moe, sums, gate_sums, main,
    gates, gates_pair, slots, inner, active, grads, sent, total,
):
    x = lax.rem(lax.axis_index("dp"), 2)
    gates[...] = softmax_of(dot(w_router[...], tokens[...], 1, 1), 0)
    gates_pair[...] = softmax_of(dot(w_router[...], tokens_pair[...], 1, 1), 0)
    width = tokens.shape[1]
    factors = (slots, inner, active, grads)
    for k in range(SPECIALIST_TOTAL):
        expert = lax.rem(x + k // PAIRED, 2) * PAIRED + k % PAIRED
        weights = (w_in.at[expert], w_out.at[expert])
        mine = factors if k < PAIRED else None
        expert_rows(expert, tokens, back, held, gates, *weights, mine, 0, sent, None)
        final = (moe, sums, gate_sums) if k == SPECIALIST_TOTAL - 1 else None
        return_rows(expert, held_col, sent, total, k == 0, final, None)
        if k < PAIRED:
            expert_rows(
                expert, tokens_pair, back_pair, held_pair, gates_pair, *weights, mine, CAP_PAD, None, None
            )
            weight_rows(slots, inner, main, 2 * k * width, None)
            weight_rows(active, grads, main, (2 * k + 1) * width, None)


def backward_kernel(
    images, attended, cotangent, moe, sums, gate_sums, qkv, mixed, w_qkv, w_proj, w_router,
    gain_one, gain_two,
    output, partial, grad_hidden, grad_dense, grad_small,
):
    grad_dense[...] = jnp.zeros_like(grad_dense)
    grad_small[...] = jnp.zeros_like(grad_small)

    def image(i):
        backward_image(
            i, images, attended, cotangent, sums, gate_sums, qkv, mixed, w_qkv, w_proj, w_router,
            gain_one, gain_two, partial, grad_hidden, grad_dense, grad_small,
        )
        output_image(i, images, attended, moe, output)

    loop(images.shape[0] // SEQ_PAD, image)


def last_kernel(images, sums, grad_hidden, gain, grad_images, grad_gain):
    grad_gain[...] = jnp.zeros_like(grad_gain)
    loop(
        images.shape[0] // SEQ_PAD,
        lambda i: last_image(i, images, sums, grad_hidden, gain, grad_images, 0, grad_gain),
    )


def call(kernel, outs, scratch, *args, flops=0):
    vmem = pl.BlockSpec(memory_space=pltpu.VMEM)
    return pl.pallas_call(
        kernel,
        out_shape=tuple(jax.ShapeDtypeStruct(shape, kind) for shape, kind in outs),
        in_specs=[vmem] * len(args),
        out_specs=tuple(vmem for _ in outs),
        scratch_shapes=[pltpu.VMEM(shape, kind) for shape, kind in scratch],
        compiler_params=pltpu.CompilerParams(vmem_limit_bytes=VMEM_LIMIT),
        cost_estimate=pl.CostEstimate(flops=flops, bytes_accessed=10**7, transcendentals=0),
    )(*args)


def swap_sum(main, dense):
    n_dp = lax.axis_size("dp")
    x = lax.axis_index("dp") % 2

    def swap(value, step):
        return lax.ppermute(value, "dp", [(i, i ^ step) for i in range(n_dp)])

    gone = lax.dynamic_index_in_dim(dense, 1 - x, 0, keepdims=False)
    mine = lax.dynamic_index_in_dim(dense, x, 0, keepdims=False)
    joined = (mine.astype(F32) + swap(gone, 1).astype(F32)).astype(BF)
    total = jnp.concatenate([main, joined], axis=0)
    step = 2
    while step < n_dp:
        total = (total.astype(F32) + swap(total, step).astype(F32)).astype(BF)
        step *= 2
    other = swap(total, 1)
    return jnp.where(x == 0, jnp.stack([total, other]), jnp.stack([other, total]))


def plain_step(rows, back, held_row, held_col, w_qkv, w_proj, router, w_in, w_out, gain_one, gain_two):
    pads = ((0, 0), (0, SEQ_PAD - rows.shape[1]), (0, 0))
    width = rows.shape[2]
    rows, back = (jnp.pad(each, pads).reshape(-1, width) for each in (rows, back))
    padded = rows.shape[0]
    gain_one, gain_two = gain_one[None], gain_two[None]
    local = w_proj.shape[0]
    router = jnp.pad(router, ((0, 8 - SPECIALIST_TOTAL), (0, 0)))
    n_dp = lax.axis_size("dp")
    swap = [(i, i ^ 1) for i in range(n_dp)]
    flat = (padded, width)
    held_pair = lax.ppermute(held_row, "dp", swap)
    back_pair = lax.ppermute(back, "dp", swap)
    partial, qkv, mixed = call(
        attention_kernel,
        [(flat, BF), ((3, padded, local), BF), ((padded, local), BF)],
        [],
        rows, w_qkv, w_proj, gain_one,
    )
    attended = pair_sum(partial)
    (normed,) = call(second_norm_kernel, [(flat, BF)], [], rows, attended, gain_two)
    normed_pair = lax.ppermute(normed, "dp", swap)
    wide = 2 * width + LANES
    moe, sums, gate_sums, main = call(
        expert_kernel,
        [(flat, BF), (flat, BF), ((padded, LANES), BF), ((4 * width, width), BF)],
        [((8, padded), F32)] * 2
        + [((2 * CAP_PAD, width), BF)] * 4
        + [((CAP_PAD, wide), BF), ((padded, wide), F32)],
        normed, normed_pair, back, back_pair,
        held_row, held_pair, held_col, router, w_in, w_out,
    )
    moe = pair_sum(moe)
    sums = pair_sum(sums)
    gate_sums = pair_sum(jnp.concatenate([gate_sums, gate_sums], axis=-1))[:, :LANES]
    output, partial, grad_hidden, grad_dense, grad_small = call(
        backward_kernel,
        [(flat, BF), (flat, BF), (flat, F32), ((4, local, width), F32), ((16, width), F32)],
        [],
        rows, attended, back, moe, sums, gate_sums,
        qkv, mixed, w_qkv, w_proj, router, gain_one, gain_two,
    )
    grad_images, grad_gain = call(
        last_kernel,
        [(flat, F32), ((8, width), F32)],
        [],
        rows, pair_sum(partial), grad_hidden, gain_one,
    )
    dense = grad_dense.reshape(2, 2 * local, width)
    small = jnp.stack([grad_small, jnp.pad(grad_gain, ((0, 8), (0, 0)))])
    dense = jnp.concatenate([dense, small], axis=1).astype(BF)
    whole = swap_sum(main, dense)
    rows_main = main.shape[0]
    experts = whole[:, :rows_main].reshape(SPECIALIST_TOTAL, 2, width, width)
    grads = whole[:, rows_main : rows_main + 2 * local].reshape(4, local, width)
    small = whole[:, rows_main + 2 * local :]
    return output, grad_images, experts[:, 0], experts[:, 1], grads, small


(
    ATT_RS, ATT_Y, ATT_AG, Z_X, Z_CORE, D_RS, G_RS, D_Y, G_Y, D_AG,
    O_RS, O_Y, O_AG, B_RS, B_Y, B_AG, COT, COT_Y, COT_CORE, DENSE, HELD,
) = range(21)


def step_kernel(
    held, held_col, w_qkv, w_proj, gain_first, gain_second, router_in, images_in, cotangent_in, w_in, w_out,
    output, grad_images, out_in, out_out, out_grads, out_small,
    images, cotangent, stage, stage_sems, wide_router, gain_one, gain_two,
    held_pair, router, back_pair, tokens, tokens_pair, attended, partial, qkv, mixed,
    core_a, far_a, core_d, far_d, core_o, far_o, core_g, far_g, gate_part, gate_sum,
    gates, gates_pair, slots, inner, active, grads, sent, total, slot_in, slot_out,
    grad_dense, grad_small, grad_last, main, landed, middle_ring, dense_x,
    sends, recvs, weight_sems, send_low, recv_low, send_mid, recv_mid, send_down, recv_down,
    send_pair, recv_pair, keep, out_sems,
):
    place = lax.axis_index("dp")
    spot = lax.axis_index("tensor")
    x = lax.rem(place, 2)
    z = place // 2
    c = lax.rem(spot, 2)
    y = spot // 2
    inside = jnp.logical_or(z == 1, z == 2)
    outside = jnp.logical_not(inside)
    core = {"tensor": spot + 1 - 2 * c}
    far = {"tensor": spot + 2 - 4 * y}
    pair = {"dp": place + 1 - 2 * x}
    line = {"dp": (z + 1 - 2 * lax.rem(z, 2)) * 2 + x}
    middle = {"dp": (3 - z) * 2 + x}
    width = images.shape[1]
    half = width // 2
    count = images.shape[0] // SEQ_PAD
    pieces = main.shape[0] // PIECE
    per_expert = 2 * width // PIECE
    mine = pl.ds(pl.multiple_of(c * half, LANES), half)
    other = pl.ds(pl.multiple_of((1 - c) * half, LANES), half)
    local = w_proj.shape[0]
    dense = active
    dense_landed, dense_middle = inner.at[:DENSE_HALF], inner.at[DENSE_HALF : 2 * DENSE_HALF]

    barrier = pltpu.get_barrier_semaphore()
    for peer in (core, far, pair, line):
        pl.semaphore_signal(barrier, inc=1, device_id=peer, device_id_type=MESH)

    @pl.when(inside)
    def _():
        pl.semaphore_signal(barrier, inc=1, device_id=middle, device_id_type=MESH)

    def load(k):
        expert = lax.rem(x + k // PAIRED, 2) * PAIRED + k % PAIRED
        return [
            pltpu.make_async_copy(w_in.at[expert], slot_in.at[k % 2], weight_sems.at[0, k % 2]),
            pltpu.make_async_copy(w_out.at[expert], slot_out.at[k % 2], weight_sems.at[1, k % 2]),
        ]

    def fetch(k, i):
        source = (cotangent_in, images_in)[k]
        return pltpu.make_async_copy(source.at[i], stage.at[k, i % 2], stage_sems.at[k, i % 2])

    for k in range(2):
        for i in range(2):
            fetch(k, i).start()
    for k in range(2):
        for copy in load(k):
            copy.start()
    wide_router[...] = jnp.zeros_like(wide_router)
    wide_router[:SPECIALIST_TOTAL, :] = router_in[...].astype(F32)
    router[...] = wide_router[...].astype(BF)
    gain_one[...] = gain_first[...][None]
    gain_two[...] = gain_second[...][None]
    grad_dense[...] = jnp.zeros_like(grad_dense)
    grad_small[...] = jnp.zeros_like(grad_small)
    grad_last[...] = jnp.zeros_like(grad_last)

    for i in range(count):
        for k, target in enumerate((cotangent, images)):
            fetch(k, i).wait()
            rows = stage[k, i % 2].astype(F32)
            rows = jnp.concatenate([rows, jnp.zeros((SEQ_PAD - SEQ, width), F32)])
            target[image_rows(i), :] = rows.astype(BF)
            if i + 2 < count:
                fetch(k, i + 2).start()

    @pl.when(inside)
    def _():
        pl.semaphore_wait(barrier, 5)

    @pl.when(outside)
    def _():
        pl.semaphore_wait(barrier, 4)

    def remote(src, dst, send, recv, peer):
        return pltpu.make_async_remote_copy(
            src_ref=src, dst_ref=dst, send_sem=send, recv_sem=recv,
            device_id=peer, device_id_type=MESH,
        )

    def channel(k, i, src, dst, peer):
        return remote(src, dst, sends.at[k, i], recvs.at[k, i], peer)

    def rs_copy(k, i, part, got):
        return channel(k, i, part.at[image_rows(i), other], got.at[image_rows(i), :], core)

    def far_copy(k, i, part, got):
        return channel(k, i, part.at[image_rows(i), mine], got.at[image_rows(i), :], far)

    def give_copy(k, i, result):
        view = result.at[image_rows(i), mine]
        return channel(k, i, view, view, core)

    def join_core(ks, i, part, near, got):
        at = image_rows(i)
        rs_copy(ks[0], i, part, near).wait_recv()
        rows = part[at, mine].astype(F32) + near[at, :].astype(F32)
        part[at, mine] = rows.astype(BF)
        far_copy(ks[1], i, part, got).start()

    def join_far(ks, i, part, got, result):
        at = image_rows(i)
        far_copy(ks[1], i, part, got).wait_recv()
        rows = part[at, mine].astype(F32) + got[at, :].astype(F32)
        result[at, mine] = rows.astype(BF)
        give_copy(ks[2], i, result).start()

    def sent_all(ks, part, near, got, result):
        def wait(i):
            rs_copy(ks[0], i, part, near).wait_send()
            far_copy(ks[1], i, part, got).wait_send()
            give_copy(ks[2], i, result).wait_send()

        loop(count, wait)

    def staged(step, lag, body):
        i = step - lag
        if isinstance(i, int):
            if 0 <= i < count:
                body(i)
            return

        @pl.when(jnp.logical_and(i >= 0, i < count))
        def _():
            body(i)

    held_copy = channel(HELD, 0, held, held_pair, pair)
    held_copy.start()

    def cot_copy(i):
        at = image_rows(i)
        return channel(COT, i, cotangent.at[at, mine], back_pair.at[at, mine], pair)

    def cot_far(i):
        view = back_pair.at[image_rows(i), mine]
        return channel(COT_Y, i, view, view, far)

    def cot_give(i):
        view = back_pair.at[image_rows(i), mine]
        return channel(COT_CORE, i, view, view, core)

    def shared(i):
        return i < count - 1

    def direct(i):
        return jnp.logical_or(lax.rem(i, 2) == y, i == count - 1)

    def cot_send(i):
        @pl.when(direct(i))
        def _():
            cot_copy(i).start()

    def cot_pass(i):
        @pl.when(direct(i))
        def _():
            cot_copy(i).wait()
            cot_give(i).start()

            @pl.when(shared(i))
            def _():
                cot_far(i).start()

    def cot_land(i):
        @pl.when(jnp.logical_not(direct(i)))
        def _():
            cot_far(i).wait_recv()
            cot_give(i).start()

    def cot_end(i):
        cot_give(i).wait()

        @pl.when(jnp.logical_and(direct(i), shared(i)))
        def _():
            cot_far(i).wait_send()

    loop(count, cot_send)

    att = (ATT_RS, ATT_Y, ATT_AG)

    def token_copy(i):
        at = image_rows(i)
        return channel(Z_X, i, tokens.at[at, mine], tokens_pair.at[at, mine], pair)

    def token_give(i):
        view = tokens_pair.at[image_rows(i), mine]
        return channel(Z_CORE, i, view, view, core)

    def attention_step(step):
        def first(i):
            attention_image(i, images, w_qkv, w_proj, gain_one, partial, qkv, mixed)
            rs_copy(ATT_RS, i, partial, core_a).start()

        def norm(i):
            give_copy(ATT_AG, i, attended).wait_recv()
            second_norm_image(i, images, attended, gain_two, tokens)
            token_copy(i).start()

        staged(step, 0, first)
        staged(step, 1, lambda i: join_core(att, i, partial, core_a, far_a))
        staged(step, 2, lambda i: join_far(att, i, partial, far_a, attended))
        staged(step, 3, norm)

        @pl.when(step == count + 1)
        def _():
            loop(count, cot_pass)

    loop(count + 3, attention_step)
    gates[...] = softmax_of(dot(router[...], tokens[...], 1, 1), 0)

    def dense_half(side):
        return pl.ds(pl.multiple_of(side * DENSE_HALF, 16), DENSE_HALF)

    def piece(n):
        if isinstance(n, int) and n >= pieces:
            start, size = DENSE_CUTS[n - pieces]
            at = pl.ds(start, size)
            views = [ref.at[at, :] for ref in (dense.at[dense_half(x)], dense_landed, dense_middle)]
            if size == 16:
                return views + [out_small.at[x]]
            at = pl.ds(start % local, size)
            return views + [out_grads.at[2 * x + start // local, at, :]]
        at = pl.ds(pl.multiple_of(n * PIECE, PIECE), PIECE)
        return [main.at[at, :], landed.at[at, :], middle_ring.at[lax.rem(n, RING)], None]

    def out_views(n):
        if isinstance(n, int) and n >= pieces:
            return [(None, piece(n)[3])]
        per_kind = width // PIECE
        expert = x * PAIRED + n // per_expert
        kind = lax.rem(n // per_kind, 2)
        at = pl.ds(pl.multiple_of(lax.rem(n, per_kind) * PIECE, PIECE), PIECE)
        return [(kind == 0, out_in.at[expert, at, :]), (kind == 1, out_out.at[expert, at, :])]

    def low_copy(n):
        own, got, _, _ = piece(n)
        return remote(own, got, send_low.at[n], recv_low.at[n], line)

    def mid_copy(n):
        own, _, got, _ = piece(n)
        return remote(own, got, send_mid.at[n], recv_mid.at[n], middle)

    def down_copy(n):
        _, done, _, _ = piece(n)
        return remote(done, done, send_down.at[n], recv_down.at[n], line)

    def each_out(n, act):
        done = piece(n)[1]
        for when, view in out_views(n):
            copies = (
                remote(done, view, send_pair.at[n], recv_pair.at[n], pair),
                pltpu.make_async_copy(done, view, keep.at[n]),
            )
            if when is None:
                act(*copies)
            else:
                pl.when(when)(functools.partial(act, *copies))

    def publish(n):
        def act(swap, own):
            swap.start()
            own.start()

        each_out(n, act)

    def add_piece(to, left, right):
        rows = to.shape[0]
        size = 64 if rows % 64 == 0 else 48 if rows % 48 == 0 else 16

        def add(i):
            at = pl.ds(pl.multiple_of(i * size, 16), size)
            to[at, :] = (left[at, :].astype(F32) + right[at, :].astype(F32)).astype(BF)

        loop(rows // size, add)

    last = pieces + len(DENSE_CUTS)

    main_turns = pieces // PER_TURN

    def tick(n):
        if isinstance(n, int) and n >= main_turns:
            turn_piece(pieces + n - main_turns)
        else:
            for j in range(PER_TURN):
                turn_piece(n * PER_TURN + j)

    def turn_piece(n):
        def when(n, body):
            if isinstance(n, int):
                if 0 <= n < last:
                    body(n)
            else:
                pl.when(n >= 0)(functools.partial(body, n))

        def gather(n):
            own, got, _, _ = piece(n)
            low_copy(n).wait_recv()
            add_piece(own, own, got)
            mid_copy(n).start()

        def finish(n):
            own, done, got, _ = piece(n)
            mid_copy(n).wait_recv()
            add_piece(done, own, got)
            down_copy(n).start()
            publish(n)

        def forward(n):
            down_copy(n).wait_recv()
            publish(n)

        @pl.when(inside)
        def _():
            when(n, gather)
            when(n - LAG, finish)

        @pl.when(outside)
        def _():
            when(n - FORWARD, forward)

    def lift(n):
        @pl.when(outside)
        def _():
            low_copy(n).start()

    factors = (slots, inner, active, grads)
    turn = 0
    final = (grads.at[: count * SEQ_PAD], slots.at[: count * SEQ_PAD], gate_part)
    moe_part, sum_part, _ = final
    dee = (D_RS, D_Y, D_AG)
    oh = (O_RS, O_Y, O_AG)
    moe, sums = tokens_pair, back_pair

    def gate_near(i):
        at = image_rows(i)
        return channel(G_RS, i, gate_part.at[at, :], core_g.at[at, :], core)

    def gate_far(i):
        at = image_rows(i)
        return channel(G_Y, i, gate_sum.at[at, :], far_g.at[at, :], far)

    def send_parts(i):
        rs_copy(D_RS, i, sum_part, core_d).start()
        gate_near(i).start()
        rs_copy(O_RS, i, moe_part, core_o).start()

    for k in range(SPECIALIST_TOTAL):
        expert = lax.rem(x + k // PAIRED, 2) * PAIRED + k % PAIRED
        weights = (slot_in.at[k % 2], slot_out.at[k % 2])
        for copy in load(k):
            copy.wait()
        kept = factors if k < PAIRED else None
        base = turn
        expert_rows(
            expert, tokens, cotangent, held, gates, *weights, kept, 0, sent,
            (lambda i, base=base: tick(base + i)) if k else None,
        )
        if k:
            turn += 2
        ends = k == SPECIALIST_TOTAL - 1
        if k == 0:

            def give(i):
                token_copy(i).wait_recv()
                token_give(i).start()

            loop(count, give)
            loop(count, cot_land)
            return_rows(expert, held_col, sent, total, True, None, None, 0, 2)
            loop(count, lambda i: token_give(i).wait_recv())
            loop(count, cot_end)
            held_copy.wait()
            gates_pair[...] = softmax_of(dot(router[...], tokens_pair[...], 1, 1), 0)
        else:
            return_rows(
                expert, held_col, sent, total, False, final if ends else None,
                send_parts if ends else None,
            )
            tick(turn)
            turn += 1
        if k < PAIRED:
            base = turn
            expert_rows(
                expert, tokens_pair, back_pair, held_pair, gates_pair, *weights, kept, CAP_PAD, None,
                (lambda i, base=base: tick(base + i)) if k else None,
            )
            if k:
                turn += 2
            for copy in load(k + 2):
                copy.start()
            per_step = 256 // PIECE
            for kind, (left, right) in enumerate(((slots, inner), (active, grads))):
                first = k * per_expert + kind * (width // PIECE)

                def after(i, first=first):
                    for j in range(per_step):
                        lift(first + i * per_step + j)

                weight_rows(left, right, main, (2 * k + kind) * width, after)
            if k == 0:
                return_rows(expert, held_col, sent, total, True, None, None, 2)
                tick(turn)
                turn += 1
        if k == PAIRED - 1:

            def tokens_sent(i):
                token_copy(i).wait_send()
                token_give(i).wait_send()

            loop(count, tokens_sent)
            sent_all(att, partial, core_a, far_a, attended)

    bee = (B_RS, B_Y, B_AG)

    def backward_step(step):
        def gates_core(i):
            join_core(dee, i, sum_part, core_d, far_d)
            at = image_rows(i)
            gate_near(i).wait_recv()
            rows = gate_part[at, :].astype(F32) + core_g[at, :].astype(F32)
            gate_sum[at, :] = rows.astype(BF)
            gate_far(i).start()

        def gates_all(i):
            join_far(dee, i, sum_part, far_d, sums)
            at = image_rows(i)
            gate_far(i).wait()
            rows = gate_sum[at, :].astype(F32) + far_g[at, :].astype(F32)
            gate_sum[at, :] = rows.astype(BF)

        def back(i):
            give_copy(D_AG, i, sums).wait()
            backward_image(
                i, images, attended, cotangent, sums, gate_sum, qkv, mixed, w_qkv, w_proj, router,
                gain_one, gain_two, partial, total, grad_dense, grad_small,
            )
            rs_copy(B_RS, i, partial, core_a).start()

        staged(step, 0, gates_core)
        staged(step, 1, gates_all)
        staged(step, 2, back)
        staged(step, 3, lambda i: join_core(bee, i, partial, core_a, far_a))
        staged(step, 4, lambda i: join_far(bee, i, partial, far_a, sums))
        staged(step, 5, finish)

    def grads_out(i):
        at = image_rows(i)
        return pltpu.make_async_copy(
            total.at[at, pl.ds(width, width)], grad_images.at[at, :], out_sems.at[0, i]
        )

    def rows_out(i):
        at = image_rows(i)
        return pltpu.make_async_copy(moe.at[at, :], output.at[at, :], out_sems.at[1, i])

    def finish(i):
        give_copy(B_AG, i, sums).wait_recv()
        last_image(i, images, sums, total, gain_one, total, width, grad_last)
        grads_out(i).start()

    def emit(i):
        give_copy(O_AG, i, moe).wait()
        output_image(i, images, attended, moe, moe)
        rows_out(i).start()

    base = turn

    def backward_turn(step):
        turns = base + step + jnp.maximum(step - 2, 0)
        tick(turns)
        backward_step(step)

        @pl.when(step >= 2)
        def _():
            tick(turns + 1)

    loop(count + 2, backward_turn)
    turn += 2 * count + 2

    def pack(i):
        start = i // 2 * DENSE_HALF + lax.rem(i, 2) * local
        dense[pl.ds(pl.multiple_of(start, 16), local), :] = grad_dense[i].astype(BF)

    def dense_view(i, side=0):
        start, size = DENSE_CUTS[i]
        return pl.ds(pl.multiple_of(side * DENSE_HALF + start, 16), size)

    def dense_copy(i):
        at = dense_view(i)
        return channel(DENSE, i, dense.at[dense_view(i, 1 - x), :], dense_x.at[at, :], pair)

    def dense_join(i):
        at = dense_view(i)
        dense_copy(i).wait()
        own = dense_view(i, x)
        dense[own, :] = (dense[own, :].astype(F32) + dense_x[at, :].astype(F32)).astype(BF)
        lift(pieces + i)

    small = len(DENSE_CUTS) - 1
    loop(4, pack)
    for i in range(small):
        dense_copy(i).start()
    join_core(bee, count - 1, partial, core_a, far_a)
    loop(count, lambda i: join_core(oh, i, moe_part, core_o, far_o))
    while turn < main_turns:
        tick(turn)
        turn += 1
    for i in range(count - 2, count):
        join_far(bee, i, partial, far_a, sums)
        finish(i - 1)
    finish(count - 1)
    for side, rows in enumerate((grad_small, grad_last)):
        dense[dense_view(small, side), :] = rows[...].astype(BF)
    dense_copy(small).start()
    for i in range(len(DENSE_CUTS)):
        dense_join(i)
        tick(turn)
        turn += 1
        join_far(oh, i, moe_part, far_o, moe)
        if i:
            emit(i - 1)
    emit(count - 1)
    while turn + pieces - main_turns < last + max(LAG, FORWARD):
        tick(turn)
        turn += 1

    def rest(i):
        rs_copy(D_RS, i, sum_part, core_d).wait_send()
        far_copy(D_Y, i, sum_part, far_d).wait_send()
        gate_near(i).wait_send()
        rs_copy(O_RS, i, moe_part, core_o).wait_send()
        far_copy(O_Y, i, moe_part, far_o).wait_send()
        grads_out(i).wait()
        rows_out(i).wait()

    loop(count, rest)
    sent_all(bee, partial, core_a, far_a, sums)

    def settle(n):
        @pl.when(outside)
        def _():
            low_copy(n).wait_send()

        @pl.when(inside)
        def _():
            mid_copy(n).wait_send()
            down_copy(n).wait_send()

        def act(swap, own):
            swap.wait()
            own.wait()

        each_out(n, act)

    loop(pieces, settle)
    for n in range(pieces, last):
        settle(n)


def eight_step(rows, back, held_row, held_col, w_qkv, w_proj, router, w_in, w_out, gain_one, gain_two):
    count, seq_len, width = rows.shape
    padded = count * SEQ_PAD
    local = w_proj.shape[0]
    half = width // 2
    wide = 2 * width + LANES
    pieces = 4 * width // PIECE
    last = pieces + len(DENSE_CUTS)
    vmem = pl.BlockSpec(memory_space=pltpu.VMEM)
    hbm = pl.BlockSpec(memory_space=pl.ANY)
    flat = ((padded, width), BF)
    part = ((padded, half), BF)
    thin = ((padded, LANES), BF)
    square = (width, width)
    start = [flat, flat, ((2, 2, seq_len, width), BF)]
    early = [((8, width), F32), ((1, width), F32), ((1, width), F32)]
    scratch = [((8, padded), jnp.int32), ((8, width), BF)] + [flat] * 5 + [((3, padded, local), BF), ((padded, local), BF)]
    scratch += [part] * 6 + [thin] * 4
    scratch += [((8, padded), F32)] * 2 + [((2 * CAP_PAD, width), BF)] * 4
    scratch += [((CAP_PAD, wide), BF), ((padded, wide), F32), ((2, *square), BF), ((2, *square), BF)]
    scratch += [((4, local, width), F32)] + [((16, width), F32)] * 2
    scratch += [((4 * width, width), BF)] * 2 + [((RING, PIECE, width), BF)]
    scratch += [((DENSE_HALF, width), BF)]
    dma = pltpu.SemaphoreType.DMA
    sems = [dma((21, count))] * 2 + [dma((2, 2))] + [dma((last,))] * 9 + [dma((2, count))]
    outs = [(flat[0], BF), (flat[0], F32)] + [((SPECIALIST_TOTAL, *square), BF)] * 2
    outs += [((4, local, width), BF), ((2, 16, width), BF)]
    return pl.pallas_call(
        step_kernel,
        out_shape=tuple(jax.ShapeDtypeStruct(shape, kind) for shape, kind in outs),
        in_specs=[vmem] * 7 + [hbm] * 4,
        out_specs=tuple(hbm for _ in outs),
        scratch_shapes=[pltpu.VMEM(*each) for each in start]
        + [dma((2, 2))]
        + [pltpu.VMEM(*each) for each in early + scratch]
        + sems,
        compiler_params=pltpu.CompilerParams(
            collective_id=0, has_side_effects=True, vmem_limit_bytes=VMEM_LIMIT
        ),
        cost_estimate=pl.CostEstimate(flops=6 * 10**10, bytes_accessed=10**8, transcendentals=0),
    )(
        held_row, held_col, w_qkv, w_proj, gain_one, gain_two, router, rows, back, w_in, w_out
    )


def trim_kernel(
    images_count, output, grad_images, grad_in, grad_out, grads, small,
    output_to, images_to, in_to, out_to, qkv_to, proj_to, router_to, first_to, second_to,
):
    turn = pl.program_id(0)
    in_to[...] = grad_in[...].astype(F32)
    out_to[...] = grad_out[...].astype(F32)

    @pl.when(turn < images_count)
    def _():
        output_to[0] = output[0][:SEQ]
        images_to[0] = grad_images[0][:SEQ]

    @pl.when(turn < 4)
    def _():
        rows = grads[0].astype(F32)

        @pl.when(turn < 3)
        def _():
            qkv_to[0] = rows

        @pl.when(turn == 3)
        def _():
            proj_to[...] = rows

    @pl.when(turn == 0)
    def _():
        rows = small[...].astype(F32)
        router_to[...] = rows[0, :SPECIALIST_TOTAL]
        second_to[...] = rows[0, 8]
        first_to[...] = rows[1, 0]


def trim(output, grad_images, grad_in, grad_out, grads, small):
    experts, width, _ = grad_in.shape
    local = grads.shape[1]
    images = output.shape[0]
    turns = 8
    rows = experts * width // turns
    cube = lambda size, count: pl.BlockSpec(
        (1, size, width), lambda i: (jnp.minimum(i, count - 1), 0, 0)
    )
    tall = pl.BlockSpec((rows, width), lambda i: (i, 0))
    whole = lambda *shape: pl.BlockSpec(shape, lambda i: (0,) * len(shape))
    flat = (experts * width, width)
    shapes = [(output.shape[0], SEQ, width), (output.shape[0], SEQ, width), flat, flat]
    shapes += [(3, local, width), (local, width), (experts, width), (width,), (width,)]
    kinds = [BF] + [F32] * 8
    got = pl.pallas_call(
        functools.partial(trim_kernel, images),
        grid=(turns,),
        out_shape=tuple(jax.ShapeDtypeStruct(a, b) for a, b in zip(shapes, kinds)),
        in_specs=[
            cube(SEQ_PAD, images), cube(SEQ_PAD, images), tall, tall, cube(local, 4),
            whole(*small.shape),
        ],
        out_specs=(
            cube(SEQ, images), cube(SEQ, images), tall, tall, cube(local, 3),
            whole(local, width), whole(experts, width), whole(width), whole(width),
        ),
        compiler_params=pltpu.CompilerParams(vmem_limit_bytes=VMEM_LIMIT),
        cost_estimate=pl.CostEstimate(flops=0, bytes_accessed=4 * 10**7, transcendentals=0),
    )(output, grad_images, grad_in.reshape(flat), grad_out.reshape(flat), grads, small)
    shape = (experts, width, width)
    return (*got[:2], got[2].reshape(shape), got[3].reshape(shape), *got[4:])


def per_device(
    images,
    w_qkv,
    w_proj,
    w_router,
    w_in,
    w_out,
    gain_one,
    gain_two,
    routes,
    order,
    counts,
    cotangent,
):
    img_count, seq_len, width = images.shape
    tokens = img_count * seq_len
    routes_g = routes.reshape(tokens, TOPK)
    held, kept_pairs = route_slots(routes_g, order[0], counts[0])
    held = jnp.pad(
        held.reshape(img_count, seq_len, SPECIALIST_TOTAL),
        ((0, 0), (0, SEQ_PAD - seq_len), (0, LANES - SPECIALIST_TOTAL)),
        constant_values=-1,
    )
    padded = img_count * SEQ_PAD
    held_col = held.reshape(padded, LANES)
    held_row = held_col[:, :8].T
    step = eight_step if lax.axis_size("dp") == 8 else plain_step
    output, grad_images, grad_in, grad_out, grads, small = step(
        images, cotangent, held_row, held_col, w_qkv.swapaxes(1, 2), w_proj, w_router.T, w_in, w_out,
        gain_one, gain_two,
    )
    cube = (img_count, SEQ_PAD, width)
    output, grad_images, grad_in, grad_out, grad_qkv, grad_proj, grad_router, first, second = trim(
        output.reshape(cube), grad_images.reshape(cube), grad_in, grad_out, grads, small
    )
    return (
        output,
        grad_images,
        grad_qkv.transpose(0, 2, 1),
        grad_proj,
        grad_router.T,
        grad_in,
        grad_out,
        first,
        second,
        kept_pairs.reshape(img_count, seq_len, TOPK),
    )


def solution(mesh):
    return jax.shard_map(
        per_device,
        mesh=mesh,
        in_specs=(
            P("dp", None, None),
            P(None, None, "tensor"),
            P("tensor", None),
            P(),
            P(None, None, "tensor"),
            P(None, "tensor", None),
            P(),
            P(),
            P("dp", None, None),
            P("dp", None),
            P("dp"),
            P("dp", None, None),
        ),
        out_specs=(
            P("dp", None, None),
            P("dp", None, None),
            P(None, None, "tensor"),
            P("tensor", None),
            P(),
            P(None, None, "tensor"),
            P(None, "tensor", None),
            P(),
            P(),
            P("dp", None, None),
        ),
        check_vma=False,
    )
```
